32 devices in a mesh: dp: 8 (over y, x, core), tensor: 4 (over z).
Axes of the slice: x: 2, y: 2, z: 4, core: 2. Of those that a mesh axis runs over, the one named last changes fastest.
Arguments:
- tokens: bfloat16 [24, 577, 1024], P('dp', None, 'tensor'), may hold values from -6 to 6
- image_mask: int32 [24], P('dp'), may hold values 0 or 1
- ln1_gain: bfloat16 [1024], P('tensor'), may hold values from 0.5 to 1.5
- first_norm_bias: bfloat16 [1024], P('tensor'), may hold values from -3 to 3
- w_attn: bfloat16 [1024, 3, 1024], P(None, None, 'tensor'), may hold values from -0.1875 to 0.1875
- qv_bias: bfloat16 [2, 1024], P(None, 'tensor'), may hold values from -3 to 3
- w_out: bfloat16 [1024, 1024], P('tensor'), may hold values from -0.75 to 0.75
- b_out: bfloat16 [1024], P('tensor'), may hold values from -3 to 3
- ln2_gain: bfloat16 [1024], P('tensor'), may hold values from 0.5 to 1.5
- second_norm_bias: bfloat16 [1024], P('tensor'), may hold values from -3 to 3
- w_fc1: bfloat16 [1024, 4096], P(None, 'tensor'), may hold values from -0.1875 to 0.1875
- b_fc1: bfloat16 [4096], P('tensor'), may hold values from -3 to 3
- w_fc2: bfloat16 [4096, 1024], P('tensor'), may hold values from -0.09375 to 0.09375
- b_fc2: bfloat16 [1024], P('tensor'), may hold values from -3 to 3
- cotangent: bfloat16 [24, 577, 1024], P('dp', None, 'tensor'), may hold values from -6 to 6
Outputs:
- block_out: bfloat16 [24, 577, 1024], P('dp', None, 'tensor')
- input_grad: bfloat16 [24, 577, 1024], P('dp', None, 'tensor')
- first_norm_gain_gradient: float32 [1024], P('tensor')
- grad_ln1_bias: float32 [1024], P('tensor')
- grad_w_attn: float32 [1024, 3, 1024], P(None, None, 'tensor')
- grad_qv_bias: float32 [2, 1024], P(None, 'tensor')
- grad_w_out: float32 [1024, 1024], P('tensor')
- grad_b_out: float32 [1024], P('tensor')
- second_norm_gain_gradient: float32 [1024], P('tensor')
- grad_ln2_bias: float32 [1024], P('tensor')
- grad_w_fc1: float32 [1024, 4096], P(None, 'tensor')
- grad_b_fc1: float32 [4096], P('tensor')
- grad_w_fc2: float32 [4096, 1024], P('tensor')
- grad_b_fc2: float32 [1024], P('tensor')
The draws below stay inside these ranges and needn't reach their ends.
All inputs are finite; a program needn't handle non-finite values. No bound on the sum of `image_mask` on one device may be relied on, other than what follows from the above.
Results may differ from the reference program's by a relative error of at most 0.014.
Values may be sent and summed in bfloat16 or wider, within the bound.
A program may use at most 128 MiB of HBM per device.

```python
import jax
import jax.numpy as jnp
from jax import lax

MODEL_WIDTH = 1024
HEADS = 16
HD = 64
FF = 4096
SEQ = 577
IMAGES = 24


def set_ends(array, rng, smallest, largest):
    longest = array.shape.index(max(array.shape))
    spots = []
    for shift in (0, 1):
        where = [jax.random.randint(jax.random.fold_in(rng, axis), (), 0, length) for axis, length in enumerate(array.shape)]
        where[longest] = (where[longest] + shift) % array.shape[longest]
        spots.append(tuple(where))
    return array.at[spots[0]].set(smallest).at[spots[1]].set(largest)


def level_of(rng, shape, cuts, smallest, high):
    gain = 1.0
    for position, shards_of in cuts:
        draws = jax.random.uniform(jax.random.fold_in(jax.random.fold_in(rng, 6), position), (shards_of,), jnp.float32, smallest / len(cuts), high / len(cuts))
        gain = gain * jnp.repeat(jnp.exp(draws), shape[position] // shards_of).reshape((-1,) + (1,) * (len(shape) - 1 - position))
    return gain


def noise(stream_key, extent, scale, most, pieces=(), dtype=jnp.bfloat16):
    array = scale * jax.random.normal(stream_key, extent, jnp.float32)
    if pieces:
        array = array * level_of(stream_key, extent, pieces, -0.22, 0.18)
    return jnp.clip(array, -most, most).astype(dtype)


def setup_inputs(seed: int = 0) -> dict:
    key_of = jax.random.split(jax.random.key(seed), 16)
    tokens = noise(key_of[0], (IMAGES, SEQ, MODEL_WIDTH), 1.0, 6.0, ((0, 8), (2, 4)))
    image_mask = set_ends((jax.random.randint(key_of[1], (IMAGES,), 0, 8) < 7).astype(jnp.int32), jax.random.fold_in(key_of[1], 1), 0, 1)
    ln1_gain = jnp.clip(1.0 + 0.1 * jax.random.normal(key_of[2], (MODEL_WIDTH,), jnp.float32), 0.5, 1.5).astype(jnp.bfloat16)
    first_norm_bias = noise(key_of[3], (MODEL_WIDTH,), 0.5, 3.0, ((0, 4),))
    w_attn = noise(key_of[4], (MODEL_WIDTH, 3, MODEL_WIDTH), MODEL_WIDTH ** -0.5, 0.1875, ((2, 4),))
    qv_bias = noise(key_of[5], (2, MODEL_WIDTH), 0.5, 3.0, ((1, 4),))
    w_out = noise(key_of[6], (MODEL_WIDTH, MODEL_WIDTH), (MODEL_WIDTH // 16) ** -0.5, 0.75, ((0, 4),))
    b_out = noise(key_of[7], (MODEL_WIDTH,), 0.5, 3.0, ((0, 4),))
    ln2_gain = jnp.clip(1.0 + 0.1 * jax.random.normal(key_of[8], (MODEL_WIDTH,), jnp.float32), 0.5, 1.5).astype(jnp.bfloat16)
    second_norm_bias = noise(key_of[9], (MODEL_WIDTH,), 0.5, 3.0, ((0, 4),))
    w_fc1 = noise(key_of[10], (MODEL_WIDTH, FF), MODEL_WIDTH ** -0.5, 0.1875, ((1, 4),))
    b_fc1 = noise(key_of[11], (FF,), 0.5, 3.0, ((0, 4),))
    w_fc2 = noise(key_of[12], (FF, MODEL_WIDTH), FF ** -0.5, 0.09375, ((0, 4),))
    b_fc2 = noise(key_of[13], (MODEL_WIDTH,), 0.5, 3.0, ((0, 4),))
    cotangent = noise(key_of[14], (IMAGES, SEQ, MODEL_WIDTH), 1.0, 6.0, ((0, 8), (2, 4)))
    return {"tokens": tokens, "image_mask": image_mask, "ln1_gain": ln1_gain, "first_norm_bias": first_norm_bias, "w_attn": w_attn, "qv_bias": qv_bias, "w_out": w_out, "b_out": b_out, "ln2_gain": ln2_gain, "second_norm_bias": second_norm_bias, "w_fc1": w_fc1, "b_fc1": b_fc1, "w_fc2": w_fc2, "b_fc2": b_fc2, "cotangent": cotangent}


@jax.custom_vjp
def low(v):
    return lax.optimization_barrier(v.astype(jnp.bfloat16)).astype(jnp.float32)

@jax.custom_vjp
def low_back(v):
    return v

def low_keep(v):
    return (low(v), None)

def low_pass(kept, incoming_gradient):
    return (incoming_gradient,)

def back_keep(v):
    return (v, None)

def back_low(kept, incoming_gradient):
    return (low(incoming_gradient),)
low.defvjp(low_keep, low_pass)
low_back.defvjp(back_keep, back_low)

def layer_norm(value, norm_gain, shift):
    middle = lax.optimization_barrier(jnp.mean(value, -1, keepdims=True))
    spread = lax.optimization_barrier(jnp.mean(value * value, -1, keepdims=True)) - middle * middle
    return (value - middle) * lax.rsqrt(spread + 1e-05) * norm_gain + shift

def high_dot(form, left, right):
    return jnp.einsum(form, left, right, precision=lax.Precision.HIGHEST)

def attend(query, keys, values):
    scores = low_back(high_dot('qhd,khd->hqk', query, keys) * HD ** (-0.5))
    top = lax.optimization_barrier(jnp.max(scores, -1, keepdims=True))
    expo = jnp.exp(scores - top)
    probs = low(expo / lax.optimization_barrier(jnp.sum(expo, -1, keepdims=True)))
    return high_dot('hqk,khd->qhd', probs, values)

def one_image(image, weight_mask, params):
    g1, b1, w_attn, qv_bias, w_out, b_out, g2, b2, w_fc1, b_fc1, w_fc2, b_fc2 = params
    h1 = low(layer_norm(image, g1, b1))
    qkv = high_dot('sd,dce->sce', h1, w_attn)
    query = low(low_back(qkv[:, 0] + qv_bias[0])).reshape(SEQ, HEADS, HD)
    keys = low(low_back(qkv[:, 1])).reshape(SEQ, HEADS, HD)
    values = low(low_back(qkv[:, 2] + qv_bias[1])).reshape(SEQ, HEADS, HD)
    context = jax.checkpoint(attend)(query, keys, values).reshape(SEQ, MODEL_WIDTH)
    context = low(low_back(context))
    attn = low_back(high_dot('sd,de->se', context, w_out) + b_out)
    residual_stream_state = image + attn
    h2 = low(layer_norm(residual_stream_state, g2, b2))
    hidden = low_back(high_dot('sd,df->sf', h2, w_fc1) + b_fc1)
    act = low(hidden * jax.nn.sigmoid(1.702 * hidden))
    mlp = low_back(high_dot('sf,fd->sd', act, w_fc2) + b_fc2)
    return (residual_stream_state + mlp) * weight_mask

def reference(tokens, image_mask, ln1_gain, first_norm_bias, w_attn, qv_bias, w_out, b_out, ln2_gain, second_norm_bias, w_fc1, b_fc1, w_fc2, b_fc2, cotangent):
    params = tuple((p.astype(jnp.float32) for p in (ln1_gain, first_norm_bias, w_attn, qv_bias, w_out, b_out, ln2_gain, second_norm_bias, w_fc1, b_fc1, w_fc2, b_fc2)))
    weights_mask = image_mask.astype(jnp.float32)

    def forward(block_inputs, weights):
        return lax.map(lambda pair: one_image(pair[0], pair[1], weights), (block_inputs, weights_mask))
    result, pull = jax.vjp(forward, tokens.astype(jnp.float32), params)
    input_grad, grads = pull(cotangent.astype(jnp.float32))
    return (result.astype(jnp.bfloat16), input_grad.astype(jnp.bfloat16), grads[0], grads[1], grads[2], grads[3], grads[4], grads[5], grads[6], grads[7], grads[8], grads[9], grads[10], grads[11])
```

```python
import functools

import jax
import jax.numpy as jnp
from jax import lax
from jax.experimental import pallas as pl
from jax.experimental.pallas import tpu as pltpu
from jax.sharding import PartitionSpec as P

MODEL_WIDTH = 1024
HD = 64


EPS = 1e-05


def norm_stats(value):
    total, squares = lax.psum((jnp.sum(value, 1), jnp.sum(value * value, 1)), "tensor")
    middle = total / MODEL_WIDTH
    spread = squares / MODEL_WIDTH - middle * middle
    return (middle[:, None], lax.rsqrt(spread + EPS)[:, None])


def layer_norm_reverse(incoming_gradient, normalized_input, norm_gain, inverse_deviation):
    gain_scaled_gradient = incoming_gradient * norm_gain
    first_norm_result, second_norm_result = lax.psum(
        (jnp.sum(gain_scaled_gradient, 1), jnp.sum(gain_scaled_gradient * normalized_input, 1)),
        "tensor",
    )
    return inverse_deviation * (
        gain_scaled_gradient
        - first_norm_result[:, None] / MODEL_WIDTH
        - normalized_input * second_norm_result[:, None] / MODEL_WIDTH
    )


def spread_features(value):
    return lax.all_gather(value, "tensor", axis=1, tiled=True)


def settle_sums(value):
    return lax.psum_scatter(value, "tensor", scatter_dimension=1, tiled=True)


def pair_dot(left, right):
    return lax.dot_general(
        left, right, (((0,), (0,)), ((), ())), preferred_element_type=jnp.float32
    )


def back_dot(left, right):
    return lax.dot_general(
        left, right, (((1,), (1,)), ((), ())), preferred_element_type=jnp.float32
    )


def attend_image(blocks):
    query, keys, values = blocks
    scale = HD ** (-0.5)
    scores = jnp.einsum("qhd,khd->hqk", query, keys, preferred_element_type=jnp.float32) * scale
    top = jnp.max(scores, -1, keepdims=True)
    expo = jnp.exp(scores - top)
    total = jnp.sum(expo, -1, keepdims=True)
    probs = expo / total
    log_total = top[..., 0] + jnp.log(total[..., 0])
    context = jnp.einsum(
        "hqk,khd->qhd", probs.astype(jnp.bfloat16), values, preferred_element_type=jnp.float32
    )
    return (context.astype(jnp.bfloat16), log_total)


def attend_back(blocks):
    query, keys, values, log_total, dcontext = blocks
    scale = HD ** (-0.5)
    scores = jnp.einsum("qhd,khd->hqk", query, keys, preferred_element_type=jnp.float32) * scale
    probs = jnp.exp(scores - log_total[..., None])
    dvalues = jnp.einsum(
        "hqk,qhd->khd", probs.astype(jnp.bfloat16), dcontext, preferred_element_type=jnp.float32
    )
    dprobs = jnp.einsum("qhd,khd->hqk", dcontext, values, preferred_element_type=jnp.float32)
    delta = jnp.sum(probs * dprobs, -1, keepdims=True)
    dscores = (probs * (dprobs - delta)).astype(jnp.bfloat16)
    dquery = jnp.einsum("hqk,khd->qhd", dscores, keys, preferred_element_type=jnp.float32) * scale
    dkeys = jnp.einsum("hqk,qhd->khd", dscores, query, preferred_element_type=jnp.float32) * scale
    return jnp.stack([dquery, dkeys, dvalues], 1).astype(jnp.bfloat16)


def local(
    tokens,
    image_mask,
    ln1_gain,
    first_norm_bias,
    w_attn,
    qv_bias,
    w_out,
    b_out,
    ln2_gain,
    second_norm_bias,
    w_fc1,
    b_fc1,
    w_fc2,
    b_fc2,
    cotangent,
):
    images, seq, width_dev = tokens.shape
    rows = images * seq
    heads_dev = width_dev // HD
    mask_rows = jnp.repeat(image_mask.astype(jnp.float32), seq)[:, None]
    first_norm_gain = ln1_gain.astype(jnp.float32)
    second_norm_gain = ln2_gain.astype(jnp.float32)
    block_inputs = tokens.astype(jnp.float32).reshape(rows, width_dev)
    first_midpoint_state, first_inverse_deviation = norm_stats(block_inputs)
    first_normalized_input = (block_inputs - first_midpoint_state) * first_inverse_deviation
    h1_full = spread_features(
        (first_normalized_input * first_norm_gain + first_norm_bias.astype(jnp.float32)).astype(
            jnp.bfloat16
        )
    )
    qkv = jnp.einsum("nd,dce->nce", h1_full, w_attn, preferred_element_type=jnp.float32)
    bias_rows = qv_bias.astype(jnp.float32)
    bias_full = jnp.stack([bias_rows[0], jnp.zeros_like(bias_rows[0]), bias_rows[1]], 0)
    qkv = (qkv + bias_full).astype(jnp.bfloat16)
    query = qkv[:, 0].reshape(images, seq, heads_dev, HD)
    keys = qkv[:, 1].reshape(images, seq, heads_dev, HD)
    values = qkv[:, 2].reshape(images, seq, heads_dev, HD)
    context, log_total = lax.map(attend_image, (query, keys, values))
    context_flat = context.reshape(rows, width_dev)
    attn = settle_sums(
        jnp.dot(context_flat, w_out, preferred_element_type=jnp.float32)
    ) + b_out.astype(jnp.float32)
    residual_stream_state = block_inputs + attn
    second_midpoint_state, second_inverse_deviation = norm_stats(residual_stream_state)
    second_normalized_input = (
        residual_stream_state - second_midpoint_state
    ) * second_inverse_deviation
    h2_full = spread_features(
        (second_normalized_input * second_norm_gain + second_norm_bias.astype(jnp.float32)).astype(
            jnp.bfloat16
        )
    )
    hidden = jnp.dot(h2_full, w_fc1, preferred_element_type=jnp.float32) + b_fc1.astype(jnp.float32)
    sigma = jax.nn.sigmoid(1.702 * hidden)
    act = (hidden * sigma).astype(jnp.bfloat16)
    mlp = settle_sums(jnp.dot(act, w_fc2, preferred_element_type=jnp.float32)) + b_fc2.astype(
        jnp.float32
    )
    block_out = (
        ((residual_stream_state + mlp) * mask_rows)
        .astype(jnp.bfloat16)
        .reshape(images, seq, width_dev)
    )
    output_gradient = cotangent.astype(jnp.float32).reshape(rows, width_dev) * mask_rows
    dy_full = spread_features(output_gradient.astype(jnp.bfloat16))
    grad_b_fc2 = jnp.sum(output_gradient, 0)
    grad_w_fc2 = pair_dot(act, dy_full)
    dact = back_dot(dy_full, w_fc2)
    dhidden = (dact * (sigma + 1.702 * hidden * sigma * (1.0 - sigma))).astype(jnp.bfloat16)
    grad_b_fc1 = jnp.sum(dhidden, 0, dtype=jnp.float32)
    grad_w_fc1 = pair_dot(h2_full, dhidden)
    second_hidden_gradient = settle_sums(back_dot(dhidden, w_fc1))
    second_norm_gain_gradient = jnp.sum(second_hidden_gradient * second_normalized_input, 0)
    grad_ln2_bias = jnp.sum(second_hidden_gradient, 0)
    residual_gradient = output_gradient + layer_norm_reverse(
        second_hidden_gradient, second_normalized_input, second_norm_gain, second_inverse_deviation
    )
    dattn = residual_gradient.astype(jnp.bfloat16)
    grad_b_out = jnp.sum(dattn, 0, dtype=jnp.float32)
    dattn_full = spread_features(dattn)
    grad_w_out = pair_dot(context_flat, dattn_full)
    dcontext = back_dot(dattn_full, w_out).astype(jnp.bfloat16).reshape(images, seq, heads_dev, HD)
    dqkv = lax.map(attend_back, (query, keys, values, log_total, dcontext))
    dqkv = dqkv.reshape(rows, 3, width_dev)
    grad_w_attn = jnp.einsum("nd,nce->dce", h1_full, dqkv, preferred_element_type=jnp.float32)
    bias_sums = jnp.sum(dqkv, 0, dtype=jnp.float32)
    grad_qv_bias = jnp.stack([bias_sums[0], bias_sums[2]], 0)
    first_hidden_gradient = settle_sums(
        jnp.einsum("nce,dce->nd", dqkv, w_attn, preferred_element_type=jnp.float32)
    )
    first_norm_gain_gradient = jnp.sum(first_hidden_gradient * first_normalized_input, 0)
    grad_ln1_bias = jnp.sum(first_hidden_gradient, 0)
    input_grad = (
        (
            residual_gradient
            + layer_norm_reverse(
                first_hidden_gradient,
                first_normalized_input,
                first_norm_gain,
                first_inverse_deviation,
            )
        )
        .astype(jnp.bfloat16)
        .reshape(images, seq, width_dev)
    )
    (
        first_norm_gain_gradient,
        grad_ln1_bias,
        grad_w_attn,
        grad_qv_bias,
        grad_w_out,
        grad_b_out,
        second_norm_gain_gradient,
        grad_ln2_bias,
        grad_w_fc1,
        grad_b_fc1,
        grad_w_fc2,
        grad_b_fc2,
    ) = lax.psum(
        (
            first_norm_gain_gradient,
            grad_ln1_bias,
            grad_w_attn,
            grad_qv_bias,
            grad_w_out,
            grad_b_out,
            second_norm_gain_gradient,
            grad_ln2_bias,
            grad_w_fc1,
            grad_b_fc1,
            grad_w_fc2,
            grad_b_fc2,
        ),
        "dp",
    )
    return (
        block_out,
        input_grad,
        first_norm_gain_gradient,
        grad_ln1_bias,
        grad_w_attn,
        grad_qv_bias,
        grad_w_out,
        grad_b_out,
        second_norm_gain_gradient,
        grad_ln2_bias,
        grad_w_fc1,
        grad_b_fc1,
        grad_w_fc2,
        grad_b_fc2,
    )


RING = 4


MESH_ID = pl.DeviceIdType.MESH
PAD = 592


def turned(p, q):
    for bit in (1, 2, 4):
        if q & bit:
            p = p + bit - 2 * bit * lax.rem(p // bit, 2)
    return p


def greet(p, z):
    barrier = pltpu.get_barrier_semaphore()
    for d in range(1, RING):
        pl.semaphore_signal(
            barrier, inc=1, device_id=(p, lax.rem(z + d, RING)), device_id_type=MESH_ID
        )
    for q in (1, 2, 4, 6):
        pl.semaphore_signal(barrier, inc=1, device_id=(turned(p, q), z), device_id_type=MESH_ID)
    pl.semaphore_wait(barrier, 7)


def gather_kernel(
    images,
    tokens,
    cotangent,
    small,
    attn_in,
    out_in,
    fc1_in,
    fc2_in,
    x_full,
    dy_full,
    small_full,
    attn_full,
    out_full,
    fc1_full,
    fc2_full,
    row_send,
    row_recv,
    small_send,
    small_recv,
    unit_send,
    unit_recv,
    local_sem,
):
    p = lax.axis_index("dp")
    z = lax.axis_index("tensor")
    core = lax.rem(p, 2)
    width = tokens.shape[2]
    greet(p, z)

    def remote(src, dst, send, recv, target):
        return pltpu.make_async_remote_copy(
            src_ref=src,
            dst_ref=dst,
            send_sem=send,
            recv_sem=recv,
            device_id=target,
            device_id_type=MESH_ID,
        )

    shifts = [lax.rem(z + d, RING) for d in range(RING)]

    def holds(plane):
        slot = plane - core
        return (slot >= 0) & (slot < images)

    def row_copy(which, source, target, d):
        dest = shifts[d]
        return remote(
            source.at[jnp.clip(dest - core, 0, images - 1)],
            target.at[:, pl.ds(pl.multiple_of(z * width, width), width)],
            row_send.at[which, d],
            row_recv.at[which, d],
            (p, dest),
        )

    def row_start(which, source, target):
        for d in range(1, RING):
            pl.when(holds(shifts[d]))(row_copy(which, source, target, d).start)

    def row_wait(which, source, target):
        for d in range(1, RING):
            pl.when(holds(shifts[d]))(row_copy(which, source, target, d).wait_send)
            pl.when(holds(z))(row_copy(which, source, target, d).wait_recv)

    def row_own(which, source, target):
        return pltpu.make_async_copy(
            source.at[jnp.clip(z - core, 0, images - 1)],
            target.at[:, pl.ds(pl.multiple_of(z * width, width), width)],
            local_sem.at[4, which],
        )

    def place(chunk, q, k):
        if chunk == 0:
            return attn_full.at[:, q // 2, k, q % 2]
        if chunk == 1:
            return out_full.at[q // 2, k, q % 2]
        return (fc1_full if chunk == 2 else fc2_full).at[q, k]

    pieces = (attn_in, out_in, fc1_in, fc2_in)

    def own_copy(chunk, q):
        return pltpu.make_async_copy(
            pieces[chunk].at[turned(p, q)], place(chunk, q, 0), local_sem.at[chunk, q]
        )

    def z_copy(chunk, d):
        return remote(
            pieces[chunk].at[p],
            place(chunk, 0, d),
            unit_send.at[chunk, d, 0],
            unit_recv.at[chunk, d, 0],
            (p, shifts[d]),
        )

    def plane_copy(chunk, k, source, target):
        flip = source ^ target
        return remote(
            place(chunk, source, k),
            place(chunk, target, k),
            unit_send.at[chunk, k, target],
            unit_recv.at[chunk, k, target],
            (turned(p, flip), z),
        )

    def small_copy(d):
        return remote(small, small_full.at[d], small_send.at[d], small_recv.at[d], (p, shifts[d]))

    small_own = pltpu.make_async_copy(small, small_full.at[0], local_sem.at[4, 2])

    for d in range(1, RING):
        small_copy(d).start()
        z_copy(0, d).start()
    row_start(0, tokens, x_full)
    row_own(0, tokens, x_full).start()
    small_own.start()
    for chunk in range(4):
        for q in range(8):
            own_copy(chunk, q).start()
    for d in range(1, RING):
        z_copy(1, d).start()
    for d in range(1, RING):
        z_copy(2, d).start()
    row_start(1, cotangent, dy_full)
    row_own(1, cotangent, dy_full).start()
    for d in range(1, RING):
        z_copy(3, d).start()

    def spread(chunk, k):
        z_copy(chunk, k).wait_recv()
        for target in (2, 4, 6, 1):
            plane_copy(chunk, k, 0, target).start()

    def share(chunk, k):
        for q in (2, 4, 6):
            plane_copy(chunk, k, 0, q).wait_recv()
            plane_copy(chunk, k, q, q + 1).start()

    for chunk in range(4):
        for k in range(1, RING):
            spread(chunk, k)
        if chunk:
            for k in range(1, RING):
                share(chunk - 1, k)
    for k in range(1, RING):
        share(3, k)
    for chunk in range(4):
        for k in range(1, RING):
            for target in (1, 3, 5, 7):
                plane_copy(chunk, k, target - 1, target).wait_recv()
    for chunk in range(4):
        for q in range(8):
            own_copy(chunk, q).wait()
        for k in range(1, RING):
            z_copy(chunk, k).wait_send()
            for target in range(1, 8):
                source = target - 1 if target % 2 else 0
                plane_copy(chunk, k, source, target).wait_send()
    for d in range(1, RING):
        small_copy(d).wait()
    small_own.wait()
    row_wait(0, tokens, x_full)
    row_wait(1, cotangent, dy_full)
    row_own(0, tokens, x_full).wait()
    row_own(1, cotangent, dy_full).wait()


def gather_all(tokens, cotangent, small, attn_in, out_in, fc1_in, fc2_in):
    images, rows, width = tokens.shape
    full = RING * width
    hid = fc1_in.shape[1]
    bf16 = jnp.bfloat16
    shapes = (
        (rows, full),
        (rows, full),
        (RING,) + small.shape,
        (3, 4, RING, 2, 32, full),
        (4, RING, 2, 32, full),
        (8, RING, hid, full),
        (8, RING, hid, full),
    )
    dma = pltpu.SemaphoreType.DMA
    return pl.pallas_call(
        functools.partial(gather_kernel, images),
        out_shape=[jax.ShapeDtypeStruct(s, bf16) for s in shapes],
        in_specs=[pl.BlockSpec(memory_space=pl.ANY)] * 7,
        out_specs=[pl.BlockSpec(memory_space=pl.ANY)] * 7,
        scratch_shapes=[
            dma((2, RING)),
            dma((2, RING)),
            dma((RING,)),
            dma((RING,)),
            dma((4, RING, 8)),
            dma((4, RING, 8)),
            dma((5, 8)),
        ],
        compiler_params=pltpu.CompilerParams(collective_id=0, has_side_effects=True),
    )(tokens, cotangent, small, attn_in, out_in, fc1_in, fc2_in)


def reduce_kernel(images, sizes, *refs):
    (
        block_in,
        grad_in,
        vector_in,
        g2,
        g1,
        go,
        ga,
        block_out,
        grad_out,
        vector_out,
        s2,
        s1,
        so,
        sa,
        held,
        kept,
        first,
        second,
        far,
        total,
        vec,
        vec_far,
        send,
        recv,
        row_send,
        row_recv,
        vec_send,
        vec_recv,
        local_sem,
    ) = refs
    p = lax.axis_index("dp")
    z = lax.axis_index("tensor")
    core = lax.rem(p, 2)
    width = block_out.shape[2]
    greet(p, z)
    grads = (g2, g1, go, ga)
    outs = (s2, s1, so, sa)
    starts = [sum(sizes[:i]) for i in range(4)]

    def remote(src, dst, ssem, rsem, target):
        return pltpu.make_async_remote_copy(
            src_ref=src,
            dst_ref=dst,
            send_sem=ssem,
            recv_sem=rsem,
            device_id=target,
            device_id_type=MESH_ID,
        )

    def near(q):
        return (turned(p, q), z)

    shifts = [lax.rem(z + d, RING) for d in range(RING)]

    slot = z - core
    live = (slot >= 0) & (slot < images)

    def columns(plane):
        return pl.ds(pl.multiple_of(plane * width, width), width)

    def row_copy(which, source, target, d):
        return remote(
            source.at[:, columns(shifts[d])],
            target.at[jnp.clip(slot, 0, images - 1)],
            row_send.at[which, d],
            row_recv.at[which, d],
            (p, shifts[d]),
        )

    def row_own(which, source, target):
        return pltpu.make_async_copy(
            source.at[:, columns(z)],
            target.at[jnp.clip(slot, 0, images - 1)],
            row_send.at[which, 0],
        )

    def row_start(which, source, target):
        @pl.when(live)
        def _():
            row_own(which, source, target).start()
            for d in range(1, RING):
                row_copy(which, source, target, d).start()

    def row_wait(which, source, target):
        @pl.when(live)
        def _():
            row_own(which, source, target).wait()
            for d in range(1, RING):
                row_copy(which, source, target, d).wait_send()

        for d in range(1, RING):
            other = lax.rem(z + RING - d, RING) - core
            pl.when((other >= 0) & (other < images))(
                row_copy(which, source, target, d).wait_recv
            )

    def rows(chunk):
        return pl.ds(starts[chunk], sizes[chunk])

    def core_copy(c):
        return remote(
            grads[c].at[:, :, 1], held.at[:, :, :, rows(c)], send.at[c, 0], recv.at[c, 0], near(1)
        )

    def keep_copy(c):
        return pltpu.make_async_copy(
            grads[c].at[:, :, 0], kept.at[:, :, :, rows(c)], local_sem.at[c, 0]
        )

    def x_copy(c):
        return remote(
            held.at[:, 1, 0:2, rows(c)], first.at[0, :, :, rows(c)], send.at[c, 1], recv.at[c, 1], near(2)
        )

    def y_copy(c):
        return remote(
            held.at[1, :, 2:4, rows(c)], first.at[1, :, :, rows(c)], send.at[c, 2], recv.at[c, 2], near(4)
        )

    def xy_copy(c):
        return remote(
            first.at[0, 1, :, rows(c)], second.at[0, :, rows(c)], send.at[c, 3], recv.at[c, 3], near(4)
        )

    def yx_copy(c):
        return remote(
            first.at[1, 1, :, rows(c)], second.at[1, :, rows(c)], send.at[c, 4], recv.at[c, 4], near(2)
        )

    def z_copy(c, k):
        return remote(
            second.at[k // 2, k % 2, rows(c)],
            far.at[k - 1, rows(c)],
            send.at[c, 4 + k],
            recv.at[c, 4 + k],
            (p, shifts[RING - k]),
        )

    def out_copy(c, q):
        return remote(
            total.at[rows(c)], outs[c].at[p], send.at[c, 7 + q], recv.at[c, 7 + q], near(q)
        )

    def out_own(c):
        return pltpu.make_async_copy(total.at[rows(c)], outs[c].at[p], local_sem.at[c, 1])

    def share_copy(c, q):
        return remote(
            outs[c].at[turned(p, q)],
            outs[c].at[turned(p, q)],
            send.at[c, 8 + q],
            recv.at[c, 8 + q],
            near(1),
        )

    def share_wait(c, q):
        return remote(
            outs[c].at[turned(p, q)],
            outs[c].at[turned(p, q + 1)],
            send.at[c, 8 + q],
            recv.at[c, 8 + q],
            near(1),
        )

    step = 16

    def add(dest, *sources):
        def body(i, _):
            at = pl.ds(pl.multiple_of(i * step, step), step)
            value = sources[0][at].astype(jnp.float32)
            for s in sources[1:]:
                value = value + s[at].astype(jnp.float32)
            dest[at] = value.astype(dest.dtype)
            return 0

        lax.fori_loop(0, dest.shape[0] // step, body, 0)

    def merge(c, y, x, ks):
        for k in ks:
            block = held.at[y, x, k, rows(c)]
            add(block, block, kept.at[y, x, k, rows(c)])

    def stage(c, s):
        if s == 0:
            core_copy(c).start()
            keep_copy(c).start()
        elif s == 1:
            core_copy(c).wait_recv()
            keep_copy(c).wait()
            for y in range(2):
                merge(c, y, 1, (0, 1))
            x_copy(c).start()
            for x in range(2):
                merge(c, 1, x, (2, 3))
            y_copy(c).start()
            for y in range(2):
                merge(c, y, 0, (0, 1))
            for x in range(2):
                merge(c, 0, x, (2, 3))
        elif s == 2:
            x_copy(c).wait_recv()
            for k in range(2):
                block = first.at[0, 1, k, rows(c)]
                add(block, block, held.at[1, 0, k, rows(c)])
            xy_copy(c).start()
            y_copy(c).wait_recv()
            for k in range(2):
                block = first.at[1, 1, k, rows(c)]
                add(block, block, held.at[0, 1, 2 + k, rows(c)])
            yx_copy(c).start()
        elif s == 3:
            xy_copy(c).wait_recv()
            for k in range(2):
                block = second.at[0, k, rows(c)]
                add(block, block, first.at[0, 0, k, rows(c)], held.at[0, 0, k, rows(c)])
                if k:
                    z_copy(c, 1).start()
            yx_copy(c).wait_recv()
            for k in range(2):
                block = second.at[1, k, rows(c)]
                add(block, block, first.at[1, 0, k, rows(c)], held.at[0, 0, 2 + k, rows(c)])
                z_copy(c, 2 + k).start()
        elif s == 4:
            for k in range(1, RING):
                z_copy(c, k).wait_recv()
            add(
                total.at[rows(c)],
                second.at[0, 0, rows(c)],
                *(far.at[k, rows(c)] for k in range(3)),
            )
            out_own(c).start()
            for q in (2, 4, 6, 1):
                out_copy(c, q).start()
        elif s == 5:
            for q in (2, 4, 6):
                out_copy_wait(c, q)
                share_copy(c, q).start()

    def out_copy_wait(c, q):
        remote(
            total.at[rows(c)], outs[c].at[turned(p, q)], send.at[c, 7 + q], recv.at[c, 7 + q], near(q)
        ).wait_recv()

    vec_in = pltpu.make_async_copy(vector_in, vec, local_sem.at[4, 0])
    vec_out = pltpu.make_async_copy(vec.at[0], vector_out, local_sem.at[4, 1])

    def vec_copy(i):
        return remote(vec, vec_far.at[i], vec_send.at[i], vec_recv.at[i], near((1, 2, 4)[i]))

    def vec_z(d):
        return remote(
            vec.at[shifts[d]], vec_far.at[3, d], vec_send.at[2 + d], vec_recv.at[2 + d], (p, shifts[d])
        )

    vec_in.start()
    stage(0, 0)
    stage(1, 0)
    stage(2, 0)
    stage(3, 0)
    row_start(0, block_in, block_out)
    row_start(1, grad_in, grad_out)
    vec_in.wait()
    vec_copy(0).start()
    for t in range(1, 9):
        for c in range(4):
            if 1 <= t - c <= 5:
                stage(c, t - c)
        if 1 <= t <= 3:
            vec_copy(t - 1).wait()
            vec[...] = vec[...] + vec_far[t - 1]
            if t < 3:
                vec_copy(t).start()
            else:
                for d in range(1, RING):
                    vec_z(d).start()
        if t == 4:
            for d in range(1, RING):
                vec_z(d).wait()
            vec[0] = vec[z] + (vec_far[3, 1] + (vec_far[3, 2] + vec_far[3, 3]))
            vec_out.start()
    for c in range(4):
        out_copy_wait(c, 1)
        for q in (2, 4, 6):
            share_wait(c, q).wait_recv()
        core_copy(c).wait_send()
        x_copy(c).wait_send()
        y_copy(c).wait_send()
        xy_copy(c).wait_send()
        yx_copy(c).wait_send()
        for k in range(1, RING):
            z_copy(c, k).wait_send()
        for q in (2, 4, 6, 1):
            out_copy(c, q).wait_send()
        for q in (2, 4, 6):
            share_copy(c, q).wait_send()
        out_own(c).wait()
    vec_out.wait()
    row_wait(0, block_in, block_out)
    row_wait(1, grad_in, grad_out)


def reduce_all(images, block, grad, vectors, g2, g1, go, ga):
    rows, full = block.shape
    width = full // RING
    sizes = tuple(g.shape[4] for g in (g2, g1, go, ga))
    every = sum(sizes)
    bf16 = jnp.bfloat16
    f32 = jnp.float32
    dma = pltpu.SemaphoreType.DMA
    outs = [jax.ShapeDtypeStruct((images, rows, width), bf16)] * 2
    outs.append(jax.ShapeDtypeStruct(vectors.shape[1:], f32))
    outs += [jax.ShapeDtypeStruct((8, n, full), bf16) for n in sizes]
    return pl.pallas_call(
        functools.partial(reduce_kernel, images, sizes),
        out_shape=outs,
        in_specs=[pl.BlockSpec(memory_space=pl.ANY)] * 7,
        out_specs=[pl.BlockSpec(memory_space=pl.ANY)] * 7,
        scratch_shapes=[
            pltpu.VMEM((2, 2, RING, every, full), bf16),
            pltpu.VMEM((2, 2, RING, every, full), bf16),
            pltpu.VMEM((2, 2, 2, every, full), bf16),
            pltpu.VMEM((2, 2, every, full), bf16),
            pltpu.VMEM((3, every, full), bf16),
            pltpu.VMEM((every, full), bf16),
            pltpu.VMEM(vectors.shape, f32),
            pltpu.VMEM((4,) + vectors.shape, f32),
            dma((4, 16)),
            dma((4, 16)),
            dma((2, RING)),
            dma((2, RING)),
            dma((6,)),
            dma((6,)),
            dma((5, 2)),
        ],
        compiler_params=pltpu.CompilerParams(
            collective_id=1, has_side_effects=True, vmem_limit_bytes=56 * 2**20
        ),
    )(block, grad, vectors, g2, g1, go, ga)


def low(value):
    return value.astype(jnp.bfloat16)


def wide(value):
    return value.astype(jnp.float32)


def pick(stack, index):
    return lax.dynamic_index_in_dim(stack, index, 0, keepdims=False)


def norm_full(value):
    middle = jnp.mean(value, 1, keepdims=True)
    spread = jnp.mean(value * value, 1, keepdims=True) - middle * middle
    inverse = lax.rsqrt(spread + EPS)
    return (value - middle) * inverse, inverse


def norm_back(gradient, normalized, gain, inverse):
    scaled = gradient * gain
    first = jnp.mean(scaled, 1, keepdims=True)
    second = jnp.mean(scaled * normalized, 1, keepdims=True)
    return inverse * (scaled - first - normalized * second)


def image_local(
    tokens,
    image_mask,
    ln1_gain,
    first_norm_bias,
    w_attn,
    qv_bias,
    w_out,
    b_out,
    ln2_gain,
    second_norm_bias,
    w_fc1,
    b_fc1,
    w_fc2,
    b_fc2,
    cotangent,
):
    images, seq, width = tokens.shape
    full = width * RING
    heads = full // HD
    p = lax.axis_index("dp")
    z = lax.axis_index("tensor")
    core = p % 2
    slot = z - core
    live = (slot >= 0) & (slot < images)
    mask = jnp.where(
        live, lax.dynamic_index_in_dim(image_mask, jnp.clip(slot, 0, images - 1), 0, False), 0
    ).astype(jnp.float32)
    rows = PAD

    attn_pieces = (
        jnp.transpose(w_attn, (1, 2, 0))
        .reshape(3, 8, 32, full)
        .transpose(1, 0, 2, 3)
    )
    out_pieces = w_out.reshape(8, 32, full)
    fc1_pieces = jnp.transpose(w_fc1).reshape(8, -1, full)
    fc2_pieces = w_fc2.reshape(8, -1, full)
    hid = fc1_pieces.shape[1]
    small = jnp.concatenate(
        [
            ln1_gain,
            first_norm_bias,
            b_out,
            ln2_gain,
            second_norm_bias,
            b_fc2,
            qv_bias.reshape(-1),
            b_fc1,
        ]
    ).reshape(3, full)
    small = jnp.pad(small, ((0, 13), (0, 0)))
    tail = ((0, 0), (0, rows - seq), (0, 0))
    x_rows, dy_rows, small_k, w_qkv, w_o, w_1, w_2 = gather_all(
        jnp.pad(tokens, tail),
        jnp.pad(cotangent, tail),
        small,
        attn_pieces,
        out_pieces,
        fc1_pieces,
        fc2_pieces,
    )
    block_inputs = jnp.where(live, wide(x_rows), 0.0)
    output_gradient = jnp.where(mask > 0, wide(dy_rows), 0.0)
    w_qkv = w_qkv.reshape(3, full, full)
    w_o = w_o.reshape(full, full)
    w_1 = w_1.reshape(-1, full)
    w_2 = w_2.reshape(-1, full)

    small_k = small_k[:, :3].reshape(RING, -1)
    small_j = jnp.stack([pick(small_k, (z - j) % RING) for j in range(RING)])

    def feature_vector(i):
        return wide(small_j[:, i * width : (i + 1) * width].reshape(full))

    first_norm_gain, first_bias, out_bias, second_norm_gain, second_bias, fc2_bias = (
        feature_vector(i) for i in range(6)
    )

    def relative(value):
        value = jnp.swapaxes(value, 0, 1)
        return jnp.stack([pick(value, p ^ q) for q in range(8)])

    def natural(value):
        value = jnp.stack([pick(value, r ^ p) for r in range(8)])
        value = jnp.swapaxes(value, 0, 1)
        return jnp.stack([pick(value, (z - j) % RING) for j in range(RING)])

    def heads_of(value):
        return value.reshape(4, 2, RING, 32).transpose(0, 2, 1, 3).reshape(-1)

    def heads_back(value):
        return value.reshape(4, RING, 2, 32).transpose(0, 2, 1, 3).reshape(8, RING, 32)

    qv_k = small_k[:, 6 * width : 8 * width].reshape(RING, 2, 8, 32)
    query_bias = wide(heads_of(relative(qv_k[:, 0])))
    value_bias = wide(heads_of(relative(qv_k[:, 1])))
    fc1_bias = wide(relative(small_k[:, 8 * width :].reshape(RING, 8, hid)).reshape(-1))

    first_hat, first_inverse = norm_full(block_inputs)
    h1 = low(first_hat * first_norm_gain + first_bias)
    query = low(back_dot(h1, w_qkv[0]) + query_bias)[:seq].reshape(seq, heads, HD)
    keys = low(back_dot(h1, w_qkv[1]))[:seq].reshape(seq, heads, HD)
    values = low(back_dot(h1, w_qkv[2]) + value_bias)[:seq].reshape(seq, heads, HD)
    context, log_total = attend_image((query, keys, values))
    short = ((0, rows - seq), (0, 0))
    context_flat = jnp.pad(context.reshape(seq, full), short)
    attn = jnp.dot(context_flat, w_o, preferred_element_type=jnp.float32) + out_bias
    residual = block_inputs + attn
    second_hat, second_inverse = norm_full(residual)
    h2 = low(second_hat * second_norm_gain + second_bias)
    hidden = back_dot(h2, w_1) + fc1_bias
    sigma = jax.nn.sigmoid(1.702 * hidden)
    act = low(hidden * sigma)
    slope = sigma + 1.702 * hidden * sigma * (1.0 - sigma)
    mlp = jnp.dot(act, w_2, preferred_element_type=jnp.float32) + fc2_bias
    block = low((residual + mlp) * mask)

    dy = low(output_gradient)
    grad_2 = low(pair_dot(act, dy)).reshape(2, 2, 2, RING, hid, full)
    dhidden = low(back_dot(dy, w_2) * slope)
    grad_1 = low(pair_dot(dhidden, h2)).reshape(2, 2, 2, RING, hid, full)
    dh2 = jnp.dot(dhidden, w_1, preferred_element_type=jnp.float32)
    second_gain_sum = jnp.sum(dh2 * second_hat, 0)
    second_bias_sum = jnp.sum(dh2, 0)
    residual_gradient = output_gradient + norm_back(
        dh2, second_hat, second_norm_gain, second_inverse
    )
    dattn = low(residual_gradient)
    dcontext = low(back_dot(dattn, w_o))

    def head_pieces(grad, count):
        grad = grad.reshape(count, 4, RING, 2, 32, full).transpose(1, 3, 2, 0, 4, 5)
        return grad.reshape(2, 2, 2, RING, count * 32, full)

    grad_o = head_pieces(low(pair_dot(context_flat, dattn)), 1)
    dqkv = attend_back((query, keys, values, log_total, dcontext[:seq].reshape(seq, heads, HD)))
    dqkv = jnp.pad(dqkv.reshape(seq, 3 * full), short)
    grad_a = head_pieces(low(pair_dot(dqkv, h1)), 3)
    dh1 = jnp.dot(dqkv, w_qkv.reshape(3 * full, full), preferred_element_type=jnp.float32)
    first_gain_sum = jnp.sum(dh1 * first_hat, 0)
    first_bias_sum = jnp.sum(dh1, 0)
    grad = low(residual_gradient + norm_back(dh1, first_hat, first_norm_gain, first_inverse))

    qkv_sums = jnp.sum(dqkv, 0, dtype=jnp.float32).reshape(3, full)
    vectors = jnp.concatenate(
        [
            v.reshape(RING, -1)
            for v in (
                first_gain_sum,
                first_bias_sum,
                jnp.sum(dattn, 0, dtype=jnp.float32),
                second_gain_sum,
                second_bias_sum,
                jnp.sum(output_gradient, 0),
                natural(heads_back(qkv_sums[0])),
                natural(heads_back(qkv_sums[2])),
                natural(jnp.sum(dhidden, 0, dtype=jnp.float32).reshape(8, RING, hid)),
            )
        ],
        1,
    ).reshape(RING, 24, 128)
    block_out, input_grad, vectors, s2, s1, so, sa = reduce_all(
        images, block, grad, vectors, grad_2, grad_1, grad_o, grad_a
    )
    vectors = vectors.reshape(-1)
    sums = [vectors[i * width : (i + 1) * width] for i in range(6)]
    return (
        block_out[:, :seq],
        input_grad[:, :seq],
        sums[0],
        sums[1],
        jnp.transpose(wide(sa).reshape(8, 3, 32, full), (3, 1, 0, 2)).reshape(full, 3, width),
        vectors[6 * width : 8 * width].reshape(2, width),
        wide(so).reshape(width, full),
        sums[2],
        sums[3],
        sums[4],
        jnp.transpose(wide(s1).reshape(8 * hid, full)),
        vectors[8 * width :],
        wide(s2).reshape(8 * hid, full),
        sums[5],
    )


def solution(mesh):
    in_specs = (
        P("dp", None, "tensor"),
        P("dp"),
        P("tensor"),
        P("tensor"),
        P(None, None, "tensor"),
        P(None, "tensor"),
        P("tensor", None),
        P("tensor"),
        P("tensor"),
        P("tensor"),
        P(None, "tensor"),
        P("tensor"),
        P("tensor", None),
        P("tensor"),
        P("dp", None, "tensor"),
    )
    out_specs = (
        P("dp", None, "tensor"),
        P("dp", None, "tensor"),
        P("tensor"),
        P("tensor"),
        P(None, None, "tensor"),
        P(None, "tensor"),
        P("tensor", None),
        P("tensor"),
        P("tensor"),
        P("tensor"),
        P(None, "tensor"),
        P("tensor"),
        P("tensor", None),
        P("tensor"),
    )
    owners = mesh.shape["dp"] == 8 and mesh.shape["tensor"] == RING

    def block(*arrays):
        images = arrays[0].shape[0] // mesh.shape["dp"]
        body = image_local if owners and images < RING else local
        return jax.shard_map(
            body, mesh=mesh, in_specs=in_specs, out_specs=out_specs, check_vma=False
        )(*arrays)

    return block
```

```python
import functools

import jax
import jax.numpy as jnp
from jax import lax
from jax.experimental import pallas as pl
from jax.experimental.pallas import tpu as pltpu
from jax.sharding import PartitionSpec as P

MODEL_WIDTH = 1024
HD = 64


EPS = 1e-05


def norm_stats(value):
    total, squares = lax.psum((jnp.sum(value, 1), jnp.sum(value * value, 1)), "tensor")
    middle = total / MODEL_WIDTH
    spread = squares / MODEL_WIDTH - middle * middle
    return (middle[:, None], lax.rsqrt(spread + EPS)[:, None])


def layer_norm_reverse(incoming_gradient, normalized_input, norm_gain, inverse_deviation):
    gain_scaled_gradient = incoming_gradient * norm_gain
    first_norm_result, second_norm_result = lax.psum(
        (jnp.sum(gain_scaled_gradient, 1), jnp.sum(gain_scaled_gradient * normalized_input, 1)),
        "tensor",
    )
    return inverse_deviation * (
        gain_scaled_gradient
        - first_norm_result[:, None] / MODEL_WIDTH
        - normalized_input * second_norm_result[:, None] / MODEL_WIDTH
    )


def spread_features(value):
    return lax.all_gather(value, "tensor", axis=1, tiled=True)


def settle_sums(value):
    return lax.psum_scatter(value, "tensor", scatter_dimension=1, tiled=True)


def pair_dot(left, right):
    return lax.dot_general(
        left, right, (((0,), (0,)), ((), ())), preferred_element_type=jnp.float32
    )


def back_dot(left, right):
    return lax.dot_general(
        left, right, (((1,), (1,)), ((), ())), preferred_element_type=jnp.float32
    )


def attend_image(blocks):
    query, keys, values = blocks
    scale = HD ** (-0.5)
    scores = jnp.einsum("qhd,khd->hqk", query, keys, preferred_element_type=jnp.float32) * scale
    top = jnp.max(scores, -1, keepdims=True)
    expo = jnp.exp(scores - top)
    total = jnp.sum(expo, -1, keepdims=True)
    probs = expo / total
    log_total = top[..., 0] + jnp.log(total[..., 0])
    context = jnp.einsum(
        "hqk,khd->qhd", probs.astype(jnp.bfloat16), values, preferred_element_type=jnp.float32
    )
    return (context.astype(jnp.bfloat16), log_total)


def attend_back(blocks):
    query, keys, values, log_total, dcontext = blocks
    scale = HD ** (-0.5)
    scores = jnp.einsum("qhd,khd->hqk", query, keys, preferred_element_type=jnp.float32) * scale
    probs = jnp.exp(scores - log_total[..., None])
    dvalues = jnp.einsum(
        "hqk,qhd->khd", probs.astype(jnp.bfloat16), dcontext, preferred_element_type=jnp.float32
    )
    dprobs = jnp.einsum("qhd,khd->hqk", dcontext, values, preferred_element_type=jnp.float32)
    delta = jnp.sum(probs * dprobs, -1, keepdims=True)
    dscores = (probs * (dprobs - delta)).astype(jnp.bfloat16)
    dquery = jnp.einsum("hqk,khd->qhd", dscores, keys, preferred_element_type=jnp.float32) * scale
    dkeys = jnp.einsum("hqk,qhd->khd", dscores, query, preferred_element_type=jnp.float32) * scale
    return jnp.stack([dquery, dkeys, dvalues], 1).astype(jnp.bfloat16)


def local(
    tokens,
    image_mask,
    ln1_gain,
    first_norm_bias,
    w_attn,
    qv_bias,
    w_out,
    b_out,
    ln2_gain,
    second_norm_bias,
    w_fc1,
    b_fc1,
    w_fc2,
    b_fc2,
    cotangent,
):
    images, seq, width_dev = tokens.shape
    rows = images * seq
    heads_dev = width_dev // HD
    mask_rows = jnp.repeat(image_mask.astype(jnp.float32), seq)[:, None]
    first_norm_gain = ln1_gain.astype(jnp.float32)
    second_norm_gain = ln2_gain.astype(jnp.float32)
    block_inputs = tokens.astype(jnp.float32).reshape(rows, width_dev)
    first_midpoint_state, first_inverse_deviation = norm_stats(block_inputs)
    first_normalized_input = (block_inputs - first_midpoint_state) * first_inverse_deviation
    h1_full = spread_features(
        (first_normalized_input * first_norm_gain + first_norm_bias.astype(jnp.float32)).astype(
            jnp.bfloat16
        )
    )
    qkv = jnp.einsum("nd,dce->nce", h1_full, w_attn, preferred_element_type=jnp.float32)
    bias_rows = qv_bias.astype(jnp.float32)
    bias_full = jnp.stack([bias_rows[0], jnp.zeros_like(bias_rows[0]), bias_rows[1]], 0)
    qkv = (qkv + bias_full).astype(jnp.bfloat16)
    query = qkv[:, 0].reshape(images, seq, heads_dev, HD)
    keys = qkv[:, 1].reshape(images, seq, heads_dev, HD)
    values = qkv[:, 2].reshape(images, seq, heads_dev, HD)
    context, log_total = lax.map(attend_image, (query, keys, values))
    context_flat = context.reshape(rows, width_dev)
    attn = settle_sums(
        jnp.dot(context_flat, w_out, preferred_element_type=jnp.float32)
    ) + b_out.astype(jnp.float32)
    residual_stream_state = block_inputs + attn
    second_midpoint_state, second_inverse_deviation = norm_stats(residual_stream_state)
    second_normalized_input = (
        residual_stream_state - second_midpoint_state
    ) * second_inverse_deviation
    h2_full = spread_features(
        (second_normalized_input * second_norm_gain + second_norm_bias.astype(jnp.float32)).astype(
            jnp.bfloat16
        )
    )
    hidden = jnp.dot(h2_full, w_fc1, preferred_element_type=jnp.float32) + b_fc1.astype(jnp.float32)
    sigma = jax.nn.sigmoid(1.702 * hidden)
    act = (hidden * sigma).astype(jnp.bfloat16)
    mlp = settle_sums(jnp.dot(act, w_fc2, preferred_element_type=jnp.float32)) + b_fc2.astype(
        jnp.float32
    )
    block_out = (
        ((residual_stream_state + mlp) * mask_rows)
        .astype(jnp.bfloat16)
        .reshape(images, seq, width_dev)
    )
    output_gradient = cotangent.astype(jnp.float32).reshape(rows, width_dev) * mask_rows
    dy_full = spread_features(output_gradient.astype(jnp.bfloat16))
    grad_b_fc2 = jnp.sum(output_gradient, 0)
    grad_w_fc2 = pair_dot(act, dy_full)
    dact = back_dot(dy_full, w_fc2)
    dhidden = (dact * (sigma + 1.702 * hidden * sigma * (1.0 - sigma))).astype(jnp.bfloat16)
    grad_b_fc1 = jnp.sum(dhidden, 0, dtype=jnp.float32)
    grad_w_fc1 = pair_dot(h2_full, dhidden)
    second_hidden_gradient = settle_sums(back_dot(dhidden, w_fc1))
    second_norm_gain_gradient = jnp.sum(second_hidden_gradient * second_normalized_input, 0)
    grad_ln2_bias = jnp.sum(second_hidden_gradient, 0)
    residual_gradient = output_gradient + layer_norm_reverse(
        second_hidden_gradient, second_normalized_input, second_norm_gain, second_inverse_deviation
    )
    dattn = residual_gradient.astype(jnp.bfloat16)
    grad_b_out = jnp.sum(dattn, 0, dtype=jnp.float32)
    dattn_full = spread_features(dattn)
    grad_w_out = pair_dot(context_flat, dattn_full)
    dcontext = back_dot(dattn_full, w_out).astype(jnp.bfloat16).reshape(images, seq, heads_dev, HD)
    dqkv = lax.map(attend_back, (query, keys, values, log_total, dcontext))
    dqkv = dqkv.reshape(rows, 3, width_dev)
    grad_w_attn = jnp.einsum("nd,nce->dce", h1_full, dqkv, preferred_element_type=jnp.float32)
    bias_sums = jnp.sum(dqkv, 0, dtype=jnp.float32)
    grad_qv_bias = jnp.stack([bias_sums[0], bias_sums[2]], 0)
    first_hidden_gradient = settle_sums(
        jnp.einsum("nce,dce->nd", dqkv, w_attn, preferred_element_type=jnp.float32)
    )
    first_norm_gain_gradient = jnp.sum(first_hidden_gradient * first_normalized_input, 0)
    grad_ln1_bias = jnp.sum(first_hidden_gradient, 0)
    input_grad = (
        (
            residual_gradient
            + layer_norm_reverse(
                first_hidden_gradient,
                first_normalized_input,
                first_norm_gain,
                first_inverse_deviation,
            )
        )
        .astype(jnp.bfloat16)
        .reshape(images, seq, width_dev)
    )
    (
        first_norm_gain_gradient,
        grad_ln1_bias,
        grad_w_attn,
        grad_qv_bias,
        grad_w_out,
        grad_b_out,
        second_norm_gain_gradient,
        grad_ln2_bias,
        grad_w_fc1,
        grad_b_fc1,
        grad_w_fc2,
        grad_b_fc2,
    ) = lax.psum(
        (
            first_norm_gain_gradient,
            grad_ln1_bias,
            grad_w_attn,
            grad_qv_bias,
            grad_w_out,
            grad_b_out,
            second_norm_gain_gradient,
            grad_ln2_bias,
            grad_w_fc1,
            grad_b_fc1,
            grad_w_fc2,
            grad_b_fc2,
        ),
        "dp",
    )
    return (
        block_out,
        input_grad,
        first_norm_gain_gradient,
        grad_ln1_bias,
        grad_w_attn,
        grad_qv_bias,
        grad_w_out,
        grad_b_out,
        second_norm_gain_gradient,
        grad_ln2_bias,
        grad_w_fc1,
        grad_b_fc1,
        grad_w_fc2,
        grad_b_fc2,
    )


RING = 4


MESH_ID = pl.DeviceIdType.MESH
ROWS = 640
TILE = 512


def low(value):
    return value.astype(jnp.bfloat16)


def wide(value):
    return value.astype(jnp.float32)


def dot_on(left, right, a, b):
    return lax.dot_general(
        left, right, (((a,), (b,)), ((), ())), preferred_element_type=jnp.float32
    )


def turned(p, q):
    return sum(lax.rem(p // bit + q // bit, 2) * bit for bit in (1, 2, 4))


def remote(src, dst, send, recv, target):
    return pltpu.make_async_remote_copy(
        src_ref=src,
        dst_ref=dst,
        send_sem=send,
        recv_sem=recv,
        device_id=target,
        device_id_type=MESH_ID,
    )


def rows_at(start, size):
    return pl.ds(pl.multiple_of(start, 16), size)


class Place:
    def __init__(self, images):
        self.p = lax.axis_index("dp")
        self.z = lax.axis_index("tensor")
        self.core = lax.rem(self.p, 2)
        self.images = images
        self.shifts = [lax.rem(self.z + d, RING) for d in range(RING)]
        self.slot = self.z - self.core
        self.live = self.holds(self.z)

    def holds(self, plane):
        return (plane - self.core >= 0) & (plane - self.core < self.images)

    def near(self, q):
        return (turned(self.p, q), self.z)

    def greet(self):
        barrier = pltpu.get_barrier_semaphore()
        for d in range(1, RING):
            pl.semaphore_signal(
                barrier, inc=1, device_id=(self.p, self.shifts[d]), device_id_type=MESH_ID
            )
        for q in (1, 2, 4, 6):
            pl.semaphore_signal(barrier, inc=1, device_id=self.near(q), device_id_type=MESH_ID)
        pl.semaphore_wait(barrier, 7)


def weight_copies(place, pieces, full, chunk, target, sem, c=0, q=0):
    if chunk >= 2:
        yield pltpu.make_async_copy(
            pieces.at[turned(place.p, q)], target.at[pl.ds(0, 128)], sem
        )
        yield pltpu.make_async_copy(full.at[q], target.at[pl.ds(128, 384)], sem)
        return
    for half in range(2):
        source = full.at[c, half] if chunk == 0 else full.at[half]
        yield pltpu.make_async_copy(source, target.at[pl.ds(half * TILE + 128, 384)], sem)
        for head in range(4):
            own = pieces.at[turned(place.p, 2 * head + half)]
            if chunk == 0:
                own = own.at[c]
            yield pltpu.make_async_copy(own, target.at[pl.ds(half * TILE + head * 32, 32)], sem)


class Gather:
    def __init__(self, place, pieces, fulls, sems):
        self.at = place
        self.p, self.z = place.p, place.z
        self.pieces = pieces
        self.fulls = fulls
        self.z_send, self.send, self.recv = sems
        z = self.z
        self.order = (
            jnp.where(z == 0, 3, 1),
            jnp.where((z == 0) | (z == 3), 2, 3),
            jnp.where(z == 0, 1, jnp.where(z == 3, 3, 2)),
        )

    def place(self, chunk, q, k, start=0, size=None):
        full = self.fulls[chunk]
        size = self.pieces[chunk].shape[-2] if size is None else size
        start = (k - 1) * 128 + start
        if chunk >= 2:
            return full.at[q, rows_at(start, size)]
        at = rows_at(start + (q // 2) * 32, size)
        return full.at[:, q % 2, at] if chunk == 0 else full.at[q % 2, at]

    def part(self, chunk, q, k, side):
        half = self.pieces[chunk].shape[-2] // 2
        return self.place(chunk, q, k, side * half, half)

    def up(self, chunk, k, source):
        return remote(
            source,
            self.place(chunk, 0, k + 1),
            self.z_send.at[chunk, k, 0],
            self.recv.at[chunk, k + 1, 0],
            (self.p, jnp.minimum(self.z + 1, RING - 1)),
        )

    def down(self, chunk, k, source):
        return remote(
            source,
            self.place(chunk, 0, k - 1),
            self.z_send.at[chunk, lax.rem(k, RING), 1],
            self.recv.at[chunk, k - 1, 0],
            (self.p, jnp.maximum(self.z - 1, 0)),
        )

    def z_start(self, chunk):
        piece = self.pieces[chunk].at[self.p]
        pl.when(self.z < RING - 1)(self.up(chunk, 0, piece).start)
        pl.when(self.z > 0)(self.down(chunk, RING, piece).start)

    def z_sent(self, chunk):
        piece = self.pieces[chunk].at[self.p]
        pl.when(self.z < RING - 1)(self.up(chunk, 0, piece).wait_send)
        pl.when(self.z > 0)(self.down(chunk, RING, piece).wait_send)
        for k in (1, 2, 3):
            here = self.place(chunk, 0, k)
            if k < 3:
                pl.when((self.z >= k) & (self.z < RING - 1))(self.up(chunk, k, here).wait_send)
            if k > 1:
                pl.when((self.z < k) & (self.z > 0))(self.down(chunk, k, here).wait_send)

    def plane(self, chunk, k, source, target):
        return remote(
            self.place(chunk, source, k),
            self.place(chunk, target, k),
            self.send.at[chunk, k, target],
            self.recv.at[chunk, k, target],
            self.at.near(source ^ target),
        )

    def corner(self, chunk, k, side):
        source, flip = ((4, 2), (2, 4))[side]
        return remote(
            self.part(chunk, source, k, side),
            self.part(chunk, 6, k, side),
            self.send.at[chunk, k, (6, 8)[side]],
            self.recv.at[chunk, k, (6, 8)[side]],
            self.at.near(flip),
        )

    def spread(self, chunk, i):
        k = self.order[i]
        here = self.place(chunk, 0, k)
        remote(
            here, here, self.send.at[chunk, k, 0], self.recv.at[chunk, k, 0], self.at.near(1)
        ).wait_recv()
        pl.when((self.z >= k) & (self.z < RING - 1))(self.up(chunk, k, here).start)
        pl.when((self.z < k) & (self.z > 0))(self.down(chunk, k, here).start)
        for target in (2, 4, 1):
            self.plane(chunk, k, 0, target).start()

    def relay(self, chunk, i):
        k = self.order[i]
        self.plane(chunk, k, 0, 4).wait_recv()
        self.corner(chunk, k, 0).start()
        self.plane(chunk, k, 0, 2).wait_recv()
        self.corner(chunk, k, 1).start()
        self.plane(chunk, k, 4, 5).start()
        self.plane(chunk, k, 2, 3).start()

    def share(self, chunk, i):
        k = self.order[i]
        self.corner(chunk, k, 0).wait_recv()
        self.corner(chunk, k, 1).wait_recv()
        self.plane(chunk, k, 6, 7).start()

    def whole(self, chunk):
        for k in range(1, RING):
            for target in (1, 3, 5, 7):
                self.plane(chunk, k, target - 1, target).wait_recv()

    def sent(self, chunk):
        self.z_sent(chunk)
        for k in range(1, RING):
            for source, target in ((0, 2), (0, 4), (0, 1), (4, 5), (2, 3), (6, 7)):
                self.plane(chunk, k, source, target).wait_send()
            self.corner(chunk, k, 0).wait_send()
            self.corner(chunk, k, 1).wait_send()


class Rows:
    def __init__(self, place, source, target, send, recv, local):
        self.at = place
        self.source, self.target = source, target
        self.send, self.recv, self.local = send, recv, local
        self.width = source.shape[2]

    def columns(self):
        return pl.ds(pl.multiple_of(self.at.z * self.width, self.width), self.width)

    def copy(self, d):
        dest = self.at.shifts[d]
        return remote(
            self.source.at[jnp.clip(dest - self.at.core, 0, self.at.images - 1)],
            self.target.at[:, self.columns()],
            self.send.at[d],
            self.recv.at[d],
            (self.at.p, dest),
        )

    def own(self):
        return pltpu.make_async_copy(
            self.source.at[jnp.clip(self.at.slot, 0, self.at.images - 1)],
            self.target.at[:, self.columns()],
            self.local,
        )

    def start(self):
        self.own().start()
        for d in range(1, RING):
            pl.when(self.at.holds(self.at.shifts[d]))(self.copy(d).start)

    def here(self):
        self.own().wait()
        for d in range(1, RING):
            pl.when(self.at.live)(self.copy(d).wait_recv)

    def sent(self):
        for d in range(1, RING):
            pl.when(self.at.holds(self.at.shifts[d]))(self.copy(d).wait_send)


def norm_rows(value, gain, shift):
    middle = jnp.mean(value, 1, keepdims=True)
    spread = jnp.mean(value * value, 1, keepdims=True) - middle * middle
    return (value - middle) * lax.rsqrt(spread + EPS) * gain + shift


def head_mask(lanes, h):
    lane = lax.broadcasted_iota(jnp.int32, (1, lanes), 1)
    return lax.rem(lane, 128) // 32 == h


def forward_kernel(images, seq, *refs):
    (
        tokens,
        cotangent,
        small,
        attn_in,
        out_in,
        fc1_in,
        fc2_in,
        dy_full,
        small_full,
        attn_full,
        out_full,
        fc1_full,
        fc2_full,
        x_rows_out,
        h1_out,
        qkv_out,
        ctx_out,
        r_out,
        h2_out,
        act_out,
        slope_out,
        x_full,
        x_v,
        h1_v,
        h2_v,
        qkv_v,
        ctx_v,
        r_v,
        w_v,
        act_v,
        slope_v,
        small_v,
        bias_v,
        row_send,
        row_recv,
        small_send,
        small_recv,
        z_send,
        unit_send,
        unit_recv,
        local_sem,
        w_sem,
        tile_sem,
        out_sem,
    ) = refs
    at = Place(images)
    p, z = at.p, at.z
    g = Gather(
        at,
        (attn_in, out_in, fc1_in, fc2_in),
        (attn_full, out_full, fc1_full, fc2_full),
        (z_send, unit_send, unit_recv),
    )
    x_rows = Rows(at, tokens, x_full, row_send.at[0], row_recv.at[0], local_sem.at[0])
    dy_rows = Rows(at, cotangent, dy_full, row_send.at[1], row_recv.at[1], local_sem.at[1])
    travel = x_full.shape[0]
    full = x_full.shape[1]
    quarter = full // RING

    def small_copy(d):
        return remote(
            small, small_full.at[d], small_send.at[d], small_recv.at[d], (p, at.shifts[d])
        )

    small_own = pltpu.make_async_copy(small, small_full.at[0], local_sem.at[2])

    at.greet()
    g.z_start(0)
    for d in range(1, RING):
        small_copy(d).start()
    small_own.start()
    x_rows.start()
    x_v[travel:] = jnp.zeros((ROWS - travel, full), x_v.dtype)

    g.spread(0, 0)
    g.spread(0, 1)
    g.z_start(1)
    g.spread(0, 2)
    for d in range(1, RING):
        small_copy(d).wait()
    small_own.wait()
    small_load = pltpu.make_async_copy(small_full, small_v, local_sem.at[3])
    small_load.start()
    x_rows.here()
    x_load = pltpu.make_async_copy(x_full, x_v.at[pl.ds(0, travel)], local_sem.at[4])
    x_load.start()
    small_load.wait()

    def feature(row, start):
        parts = [
            small_v[lax.rem(z + RING - j, RING), row : row + 1, start : start + quarter]
            for j in range(RING)
        ]
        return wide(jnp.concatenate(parts, 1))

    def unit_blocks(row, start, size):
        return [
            wide(small_v[k, row : row + 1, start : start + size]) for k in range(RING)
        ]

    gain, shift = feature(0, 0), feature(0, quarter)
    for c, start in ((0, 2 * quarter), (2, 3 * quarter)):
        for half in range(2):
            blocks = unit_blocks(1, start + half * 128, 128)
            bias_v[c : c + 1, half * TILE : (half + 1) * TILE] = jnp.concatenate(blocks, 1)
    bias_v[1:2] = jnp.zeros((1, full), jnp.float32)
    x_load.wait()

    def first_norm(i, _):
        block = rows_at(i * 16, 16)
        value = jnp.where(at.live, wide(x_v[block]), 0.0)
        x_v[block] = low(value)
        h1_v[block] = low(norm_rows(value, gain, shift))
        return 0

    lax.fori_loop(0, ROWS // 16, first_norm, 0)
    saves = [
        pltpu.make_async_copy(x_v, x_rows_out, out_sem.at[0]),
        pltpu.make_async_copy(h1_v, h1_out, out_sem.at[1]),
    ]
    for s in saves:
        s.start()

    for i in range(3):
        g.relay(0, i)
        g.spread(1, i)
        if i == 1:
            g.z_start(2)
        if i:
            g.share(0, i - 1)
    g.share(0, 2)
    g.whole(0)

    def tile_load(chunk, c, slot):
        return list(
            weight_copies(
                at,
                (attn_in, out_in)[chunk],
                (attn_full, out_full)[chunk],
                chunk,
                w_v.at[slot],
                w_sem.at[slot],
                c,
            )
        )

    def go(copies):
        for copy in copies:
            copy.start()

    def arrive(copies):
        for copy in copies:
            copy.wait()

    def filled(slot):
        pltpu.make_async_copy(w_v.at[slot], w_v.at[slot], w_sem.at[slot]).wait()

    loads = [tile_load(0, c, c % 2) for c in range(3)] + [tile_load(1, 0, 1)]
    go(loads[0])
    go(loads[1])
    steps = [
        lambda: g.spread(2, 0),
        lambda: g.relay(1, 0),
        lambda: g.relay(1, 1),
    ]
    for c in range(3):
        filled(c % 2)

        def project(i, _, c=c):
            block = rows_at(i * TILE, TILE)
            out = dot_on(h1_v[...], w_v[c % 2, block], 1, 1)
            lanes = pl.ds(pl.multiple_of(i * TILE, TILE), TILE)
            qkv_v[c, :, lanes] = low(out + bias_v[c : c + 1, lanes])
            return 0

        lax.fori_loop(0, 2, project, 0)
        if c == 0:
            go(loads[2])
        steps[c]()
    save = pltpu.make_async_copy(qkv_v, qkv_out, out_sem.at[2])
    save.start()
    saves.append(save)

    key = lax.broadcasted_iota(jnp.int32, (ROWS, 1), 0)

    def attend(k, _):
        lanes = [pl.ds(pl.multiple_of(k * 128 + half * TILE, 128), 128) for half in range(2)]

        def group(c):
            return jnp.concatenate([qkv_v[c, :, lane] for lane in lanes], 1)

        keys, values = group(1), group(2)
        for r in range(ROWS // 128):
            block = slice(r * 128, (r + 1) * 128)
            query = jnp.concatenate([qkv_v[0, block, lane] for lane in lanes], 1)
            query = query * jnp.bfloat16(HD ** (-0.5))
            out = None
            for h in range(4):
                mask = head_mask(256, h)
                scores = dot_on(keys, jnp.where(mask, query, jnp.bfloat16(0)), 1, 1)
                scores = jnp.where(key < seq, scores, -1e30)
                expo = jnp.exp(scores - jnp.max(scores, 0, keepdims=True))
                probs = low(expo * (1.0 / jnp.sum(expo, 0, keepdims=True)))
                part = dot_on(probs, values, 0, 0)
                out = part if out is None else jnp.where(mask, part, out)
            out = low(out)
            ctx_v[block, lanes[0]] = out[:, :128]
            ctx_v[block, lanes[1]] = out[:, 128:]
        return 0

    attention_steps = [
        [lambda: g.spread(2, 1), lambda: g.z_start(3), lambda: g.relay(1, 2)],
        [lambda: g.spread(2, 2), lambda: g.share(1, 0), lambda: g.share(1, 1)],
        [lambda: g.share(1, 2), lambda: g.relay(2, 0), lambda: g.spread(3, 0)],
        [lambda: g.relay(2, 1), lambda: g.spread(3, 1), dy_rows.start],
    ]
    for k in range(4):
        attend(k, 0)
        for step in attention_steps[k]:
            step()
    g.whole(1)
    go(loads[3])
    save = pltpu.make_async_copy(ctx_v, ctx_out, out_sem.at[3])
    save.start()
    saves.append(save)
    out_bias = feature(0, 2 * quarter)
    gain2, shift2 = feature(0, 3 * quarter), feature(1, 0)
    filled(1)
    for i in range(2):
        lanes = slice(i * TILE, (i + 1) * TILE)
        attn = dot_on(ctx_v[...], w_v[1, :, lanes], 1, 0)
        r_v[:, lanes] = wide(x_v[:, lanes]) + (attn + out_bias[:, lanes])
    save = pltpu.make_async_copy(r_v, r_out, out_sem.at[4])
    save.start()
    saves.append(save)
    g.relay(2, 2)
    g.spread(3, 2)
    g.share(2, 0)

    def second_norm(i, _):
        block = rows_at(i * 16, 16)
        h2_v[block] = low(norm_rows(r_v[block], gain2, shift2))
        return 0

    lax.fori_loop(0, ROWS // 16, second_norm, 0)
    save = pltpu.make_async_copy(h2_v, h2_out, out_sem.at[5])
    save.start()
    saves.append(save)
    g.share(2, 1)
    g.relay(3, 0)
    g.share(2, 2)
    g.whole(2)

    def pair_load(i):
        slot = i % 2
        for side in range(2):
            yield from weight_copies(
                at,
                fc1_in,
                fc1_full,
                2,
                w_v.at[slot, pl.ds(side * TILE, TILE)],
                w_sem.at[slot],
                q=2 * i + side,
            )

    def tile_saves(q):
        slot = q % 2
        return [
            pltpu.make_async_copy(act_v.at[slot], act_out.at[q], tile_sem.at[0, slot]),
            pltpu.make_async_copy(slope_v.at[slot], slope_out.at[q], tile_sem.at[1, slot]),
        ]

    pairs = [list(pair_load(i)) for i in range(4)]
    go(pairs[0])
    go(pairs[1])
    steps = [
        [lambda: g.relay(3, 1)],
        [lambda: g.relay(3, 2)],
        [lambda: g.share(3, 0), lambda: g.share(3, 1)],
        [lambda: g.share(3, 2)],
    ]
    for i in range(4):
        filled(i % 2)
        for side in range(2):
            q = 2 * i + side
            if q >= 2:
                arrive(tile_saves(q - 2))
            bias = jnp.concatenate(unit_blocks(2, q * 128, 128), 1)
            for j in range(2):
                cols = slice(j * 256, (j + 1) * 256)
                start = side * TILE + j * 256
                u = dot_on(h2_v[...], w_v[i % 2, start : start + 256], 1, 1) + bias[:, cols]
                sg = 1.0 / (1.0 + jnp.exp(-1.702 * u))
                act_v[side, :, cols] = low(u * sg)
                slope_v[side, :, cols] = low(sg + 1.702 * u * sg * (1.0 - sg))
            go(tile_saves(q))
        if i < 2:
            go(pairs[i + 2])
        for step in steps[i]:
            step()
    for q in (6, 7):
        arrive(tile_saves(q))
    arrive(saves)
    g.whole(3)
    dy_rows.here()
    for chunk in range(4):
        g.sent(chunk)
    x_rows.sent()
    dy_rows.sent()


def forward(seq, tokens, cotangent, small, attn_in, out_in, fc1_in, fc2_in):
    images, rows, width = tokens.shape
    full = RING * width
    bf16 = jnp.bfloat16
    f32 = jnp.float32
    dma = pltpu.SemaphoreType.DMA
    shapes = (
        ((rows, full), bf16),
        ((RING,) + small.shape, bf16),
        ((3, 2, 384, full), bf16),
        ((2, 384, full), bf16),
        ((8, 384, full), bf16),
        ((8, 384, full), bf16),
        ((ROWS, full), bf16),
        ((ROWS, full), bf16),
        ((3, ROWS, full), bf16),
        ((ROWS, full), bf16),
        ((ROWS, full), f32),
        ((ROWS, full), bf16),
        ((8, ROWS, TILE), bf16),
        ((8, ROWS, TILE), bf16),
        ((rows, full), bf16),
    )
    return pl.pallas_call(
        functools.partial(forward_kernel, images, seq),
        out_shape=[jax.ShapeDtypeStruct(s, d) for s, d in shapes],
        in_specs=[pl.BlockSpec(memory_space=pl.ANY)] * 7,
        out_specs=[pl.BlockSpec(memory_space=pl.ANY)] * len(shapes),
        scratch_shapes=[
            pltpu.VMEM((ROWS, full), bf16),
            pltpu.VMEM((ROWS, full), bf16),
            pltpu.VMEM((ROWS, full), bf16),
            pltpu.VMEM((3, ROWS, full), bf16),
            pltpu.VMEM((ROWS, full), bf16),
            pltpu.VMEM((ROWS, full), f32),
            pltpu.VMEM((2, 1024, full), bf16),
            pltpu.VMEM((2, ROWS, TILE), bf16),
            pltpu.VMEM((2, ROWS, TILE), bf16),
            pltpu.VMEM((RING,) + small.shape, bf16),
            pltpu.VMEM((8, full), f32),
            dma((2, RING)),
            dma((2, RING)),
            dma((RING,)),
            dma((RING,)),
            dma((4, RING, 2)),
            dma((4, RING, 9)),
            dma((4, RING, 9)),
            dma((5,)),
            dma((2,)),
            dma((2, 2)),
            dma((6,)),
        ],
        compiler_params=pltpu.CompilerParams(
            collective_id=0, has_side_effects=True, vmem_limit_bytes=56 * 2**20
        ),
    )(tokens, cotangent, small, attn_in, out_in, fc1_in, fc2_in)


class Reduce:
    def __init__(self, place, sizes, outs, bufs, sems):
        self.at = place
        self.sizes = sizes
        self.starts = [sum(sizes[:i]) for i in range(4)]
        self.outs = outs
        self.held, self.first, self.second, self.far, self.total, self.stage = bufs
        self.core_send, self.core_recv, self.send, self.recv, self.local = sems

    def rows(self, c):
        return pl.ds(self.starts[c], self.sizes[c])

    def give(self, group, xy, slot):
        y, x = xy // 2, lax.rem(xy, 2)
        c = min(group, 3)
        if c < 2:
            source, at = self.stage.at[slot], self.rows(c)
        else:
            source = self.stage.at[slot, :, pl.ds(xy * 32, 32)]
            at = pl.ds(self.starts[c] + (group - c) * 32, 32)
        return remote(
            source,
            self.held.at[y, x, :, at],
            self.core_send.at[group, xy],
            self.core_recv.at[group, xy],
            self.at.near(1),
        )

    def hop(self, source, target, c, i, q):
        return remote(source, target, self.send.at[c, i], self.recv.at[c, i], self.at.near(q))

    def x_copy(self, c, y):
        at = self.rows(c)
        return self.hop(self.held.at[y, 1, 0:2, at], self.first.at[0, y, :, at], c, y, 2)

    def y_copy(self, c, x):
        at = self.rows(c)
        return self.hop(self.held.at[1, x, 2:4, at], self.first.at[1, x, :, at], c, 2 + x, 4)

    def xy_copy(self, c):
        at = self.rows(c)
        return self.hop(self.first.at[0, 1, :, at], self.second.at[0, :, at], c, 4, 4)

    def yx_copy(self, c):
        at = self.rows(c)
        return self.hop(self.first.at[1, 1, :, at], self.second.at[1, :, at], c, 5, 2)

    def z_copy(self, c, k):
        return remote(
            self.second.at[k // 2, k % 2, self.rows(c)],
            self.far.at[k - 1, self.rows(c)],
            self.send.at[c, 5 + k],
            self.recv.at[c, 5 + k],
            (self.at.p, self.at.shifts[RING - k]),
        )

    def out_copy(self, c, q):
        return self.hop(self.total.at[self.rows(c)], self.outs[c].at[self.at.p], c, 8 + q, q)

    def out_here(self, c, q):
        block = self.outs[c].at[turned(self.at.p, q)]
        self.hop(self.total.at[self.rows(c)], block, c, 8 + q, q).wait_recv()

    def out_own(self, c):
        return pltpu.make_async_copy(
            self.total.at[self.rows(c)], self.outs[c].at[self.at.p], self.local.at[c]
        )

    def share(self, c, q):
        block = self.outs[c].at[turned(self.at.p, q)]
        return self.hop(block, block, c, 9 + q, 1)

    def share_here(self, c, q):
        block = self.outs[c].at[turned(self.at.p, q)]
        theirs = self.outs[c].at[turned(self.at.p, q + 1)]
        self.hop(block, theirs, c, 9 + q, 1).wait_recv()

    def add(self, dest, *sources):
        def body(i, _):
            at = rows_at(i * 16, 16)
            value = wide(sources[0][at])
            for s in sources[1:]:
                value = value + wide(s[at])
            dest[at] = low(value)
            return 0

        lax.fori_loop(0, dest.shape[0] // 16, body, 0)

    def turn(self, c):
        at = self.rows(c)
        self.x_copy(c, 1).wait_recv()
        for k in range(2):
            block = self.first.at[0, 1, k, at]
            self.add(block, block, self.held.at[1, 0, k, at])
        self.xy_copy(c).start()
        self.y_copy(c, 1).wait_recv()
        for k in range(2):
            block = self.first.at[1, 1, k, at]
            self.add(block, block, self.held.at[0, 1, 2 + k, at])
        self.yx_copy(c).start()

    def rise(self, c):
        at = self.rows(c)
        self.x_copy(c, 0).wait_recv()
        self.xy_copy(c).wait_recv()
        for k in range(2):
            block = self.second.at[0, k, at]
            self.add(block, block, self.first.at[0, 0, k, at], self.held.at[0, 0, k, at])
        self.z_copy(c, 1).start()
        self.y_copy(c, 0).wait_recv()
        self.yx_copy(c).wait_recv()
        for k in range(2):
            block = self.second.at[1, k, at]
            self.add(block, block, self.first.at[1, 0, k, at], self.held.at[0, 0, 2 + k, at])
            self.z_copy(c, 2 + k).start()

    def settle(self, c):
        at = self.rows(c)
        for k in range(1, RING):
            self.z_copy(c, k).wait_recv()
        self.add(
            self.total.at[at], self.second.at[0, 0, at], *(self.far.at[k, at] for k in range(3))
        )
        self.out_own(c).start()
        for q in (2, 4, 6, 1):
            self.out_copy(c, q).start()

    def spread(self, c):
        for q in (2, 4, 6):
            self.out_here(c, q)
            self.share(c, q).start()

    def finish(self, c):
        self.out_here(c, 1)
        for q in (2, 4, 6):
            self.share_here(c, q)
            self.share(c, q).wait_send()
        for i in range(2):
            self.x_copy(c, i).wait_send()
            self.y_copy(c, i).wait_send()
        self.xy_copy(c).wait_send()
        self.yx_copy(c).wait_send()
        for k in range(1, RING):
            self.z_copy(c, k).wait_send()
        for q in (2, 4, 6, 1):
            self.out_copy(c, q).wait_send()
        self.out_own(c).wait()


class Return:
    def __init__(self, place, source, target, send, recv):
        self.at = place
        self.source, self.target = source, target
        self.send, self.recv = send, recv
        self.rows, self.width = target.shape[1], target.shape[2]

    def pair(self, plane):
        columns = pl.ds(pl.multiple_of(plane * self.width, self.width), self.width)
        slot = jnp.clip(self.at.slot, 0, self.at.images - 1)
        return self.source.at[pl.ds(0, self.rows), columns], self.target.at[slot]

    def copy(self, d):
        source, target = self.pair(self.at.shifts[d])
        return remote(
            source, target, self.send.at[d], self.recv.at[d], (self.at.p, self.at.shifts[d])
        )

    def own(self):
        return pltpu.make_async_copy(*self.pair(self.at.z), self.send.at[0])

    def start(self):
        pl.when(self.at.live)(self.own().start)
        for d in range(1, RING):
            pl.when(self.at.live)(self.copy(d).start)

    def sent(self):
        pl.when(self.at.live)(self.own().wait)
        for d in range(1, RING):
            pl.when(self.at.live)(self.copy(d).wait_send)

    def here(self):
        for d in range(1, RING):
            other = lax.rem(self.at.z + RING - d, RING)
            pl.when(self.at.holds(other))(self.copy(d).wait_recv)


def norm_parts(value):
    middle = jnp.mean(value, 1, keepdims=True)
    spread = jnp.mean(value * value, 1, keepdims=True) - middle * middle
    inverse = lax.rsqrt(spread + EPS)
    return (value - middle) * inverse, inverse


def norm_reverse(gradient, normalized, gain, inverse):
    scaled = gradient * gain
    first = jnp.mean(scaled, 1, keepdims=True)
    second = jnp.mean(scaled * normalized, 1, keepdims=True)
    return inverse * (scaled - first - normalized * second)


def backward_kernel(images, seq, sizes, *refs):
    (
        mask_in,
        small_full,
        x_in,
        h1_in,
        qkv_in,
        ctx_in,
        r_in,
        h2_in,
        act_in,
        slope_in,
        dy_in,
        attn_in,
        out_in,
        fc1_in,
        fc2_in,
        attn_full,
        out_full,
        fc1_full,
        fc2_full,
        block_out,
        grad_out,
        vector_out,
        s2,
        s1,
        so,
        sa,
        held,
        first,
        second,
        far,
        total,
        stage,
        w_v,
        dy_v,
        h_v,
        act_v,
        du_v,
        mlp_v,
        dh_v,
        r_v,
        da_v,
        ctx_v,
        dctx_v,
        qkv_v,
        p_v,
        ds_v,
        dg_v,
        blk_v,
        sums_v,
        dus_v,
        small_v,
        vec,
        vec_far,
        core_send,
        core_recv,
        send,
        recv,
        row_send,
        row_recv,
        vec_send,
        vec_recv,
        local_sem,
        load_sem,
        tile_sem,
        w_sem,
    ) = refs
    at = Place(images)
    p, z = at.p, at.z
    full = x_in.shape[1]
    quarter = full // RING
    travel = dy_in.shape[0]
    red = Reduce(
        at,
        sizes,
        (s2, s1, so, sa),
        (held, first, second, far, total, stage),
        (core_send, core_recv, send, recv, local_sem),
    )
    blocks_back = Return(at, blk_v, block_out, row_send.at[0], row_recv.at[0])
    grads_back = Return(at, blk_v, grad_out, row_send.at[1], row_recv.at[1])

    def load(source, target, i):
        return pltpu.make_async_copy(source, target, load_sem.at[i])

    dy_load = load(dy_in, dy_v.at[pl.ds(0, travel)], 0)
    h2_load = load(h2_in, h_v, 1)
    r_load = load(r_in, r_v, 2)
    ctx_load = load(ctx_in, ctx_v, 3)
    qkv_load = load(qkv_in, qkv_v, 4)
    small_load = load(small_full, small_v, 5)
    h1_load = load(h1_in, h_v, 6)
    x_load = load(x_in, dy_v, 7)

    def tile_loads(q, slot):
        yield pltpu.make_async_copy(act_in.at[q], act_v.at[slot], tile_sem.at[0, slot])
        yield pltpu.make_async_copy(slope_in.at[q], du_v.at[slot], tile_sem.at[1, slot])
        for side, (pieces, whole) in enumerate(((fc1_in, fc1_full), (fc2_in, fc2_full))):
            yield from weight_copies(
                at, pieces, whole, 2, w_v.at[slot, pl.ds(side * TILE, TILE)], w_sem.at[slot], q=q
            )

    def matrix_loads(chunk, c, slot):
        pieces, whole = ((attn_in, attn_full), (out_in, out_full))[chunk]
        return weight_copies(at, pieces, whole, chunk, w_v.at[slot], w_sem.at[slot], c)

    def go(copies):
        for copy in copies:
            copy.start()

    def filled(slot):
        pltpu.make_async_copy(w_v.at[slot], w_v.at[slot], w_sem.at[slot]).wait()

    def turn_of(i):
        return jnp.where(i == 0, 3, jnp.where(i == 1, 1, jnp.where(i == 2, 2, 0)))

    dy_load.start()
    go(tile_loads(7, 0))
    h2_load.start()
    at.greet()
    go(tile_loads(6, 1))
    small_load.start()
    r_load.start()
    ctx_load.start()
    qkv_load.start()

    dy_v[travel:] = jnp.zeros((ROWS - travel, full), dy_v.dtype)
    sums_v[...] = jnp.zeros_like(sums_v)
    mask = mask_in[0:1, 0:1]
    dy_load.wait()

    def masked(i, _):
        block = rows_at(i * 16, 16)
        dy_v[block] = low(jnp.where(at.live, wide(dy_v[block]), 0.0) * mask)
        return 0

    lax.fori_loop(0, travel // 16, masked, 0)
    h2_load.wait()

    def halves(body):
        lax.fori_loop(0, 2, lambda j, _: (body(pl.ds(pl.multiple_of(j * TILE, TILE), TILE)), 0)[1], 0)

    def keep(group, xy, left, right):
        y, x = xy // 2, lax.rem(xy, 2)
        red.give(group, xy, 0).wait_recv()
        at_rows = red.rows(group)

        def body(cols):
            grad = dot_on(left[...], right[:, cols], 0, 0)
            for k in range(RING):
                old = wide(held[y, x, k, at_rows, cols])
                held[y, x, k, at_rows, cols] = low(old + grad[k * 128 : (k + 1) * 128])

        halves(body)
        pl.when(x == 1)(red.x_copy(group, y).start)
        pl.when(y == 1)(red.y_copy(group, x).start)

    def stage_fill(slot, left, right):
        def body(cols):
            grad = low(dot_on(left[...], right[:, cols], 0, 0))
            for k in range(RING):
                stage[slot, k, :, cols] = grad[k * 128 : (k + 1) * 128]

        halves(body)

    mlp_v[...] = jnp.zeros_like(mlp_v)
    dh_v[...] = jnp.zeros_like(dh_v)

    def hidden_tile(i, core):
        slot = 1 - core
        xy = turn_of(i)
        q = 2 * xy + core
        pltpu.make_async_copy(act_in.at[q], act_v.at[slot], tile_sem.at[0, slot]).wait()
        if core:
            pl.when(i > 0)(red.give(0, turn_of(i - 1), 0).wait_send)
            stage_fill(0, act_v.at[slot], dy_v)
            red.give(0, xy, 0).start()
        else:
            keep(0, xy, act_v.at[slot], dy_v)
        pltpu.make_async_copy(slope_in.at[q], du_v.at[slot], tile_sem.at[1, slot]).wait()
        filled(slot)

        def slopes(j, _):
            cols = pl.ds(pl.multiple_of(j * 256, 256), 256)
            start = pl.ds(pl.multiple_of(TILE + j * 256, 256), 256)
            dact = dot_on(dy_v[...], w_v[slot, start], 1, 1)
            du = low(dact * wide(du_v[slot, :, cols]))
            du_v[slot, :, cols] = du
            dus_v[pl.ds(q, 1), cols] = jnp.sum(wide(du), 0, keepdims=True)
            return 0

        lax.fori_loop(0, 2, slopes, 0)
        if core:
            pl.when(i > 0)(red.give(1, turn_of(i - 1), 1).wait_send)
            stage_fill(1, du_v.at[slot], h_v)
            red.give(1, xy, 1).start()
        else:
            keep(1, xy, du_v.at[slot], h_v)

        def back(cols):
            mlp_v[:, cols] += dot_on(act_v[slot], w_v[slot, TILE:, cols], 1, 0)
            dh_v[:, cols] += dot_on(du_v[slot], w_v[slot, :TILE, cols], 1, 0)

        halves(back)

        @pl.when(i < 3)
        def _():
            go(tile_loads(2 * turn_of(i + 1) + core, slot))

    def hidden_tiles(i, _):
        hidden_tile(i, 1)
        hidden_tile(i, 0)
        return 0

    lax.fori_loop(0, 4, hidden_tiles, 0)
    go(matrix_loads(1, 0, 0))
    go(matrix_loads(0, 0, 1))
    h1_load.start()

    small_load.wait()

    def feature(row, start):
        parts = [
            small_v[lax.rem(z + RING - j, RING), row : row + 1, start : start + quarter]
            for j in range(RING)
        ]
        return wide(jnp.concatenate(parts, 1))

    gain1, gain2 = feature(0, 0), feature(0, 3 * quarter)
    fc2_bias = feature(1, quarter)
    r_load.wait()

    def collect(i, value):
        sums_v[i] = sums_v[i] + (value[:8] + value[8:])

    def second_norm(i, _):
        block = rows_at(i * 16, 16)
        r1 = r_v[block]
        dy = wide(dy_v[block])
        blk_v[block] = low((r1 + (mlp_v[block] + fc2_bias)) * mask)
        hat, inverse = norm_parts(r1)
        dh = dh_v[block]
        dr1 = dy + norm_reverse(dh, hat, gain2, inverse)
        da = low(dr1)
        r_v[block] = dr1
        da_v[block] = da
        collect(2, wide(da))
        collect(3, dh * hat)
        collect(4, dh)
        collect(5, dy)
        return 0

    lax.fori_loop(0, ROWS // 16, second_norm, 0)
    blocks_back.start()
    x_load.start()
    ctx_load.wait()

    pending = [[red.give(0, 0, 0)], [red.give(1, 0, 1)]]

    def stage_free(slot):
        for copy in pending[slot]:
            copy.wait_send()
        pending[slot] = []

    def stage_go(slot, copies):
        go(copies)
        pending[slot] = copies

    far_half = pl.ds(TILE, TILE)
    near_half = pl.ds(0, TILE)
    stage_free(0)
    stage_fill(0, ctx_v.at[:, far_half], da_v)
    stage_go(0, [red.give(2, xy, 0) for xy in range(4)])
    filled(0)

    def dctx_half(rows):
        dctx_v[:, rows] = low(dot_on(da_v[...], w_v[0, rows], 1, 1))

    halves(dctx_half)

    def keep_heads(group, left, right):
        c = min(group, 3)
        start = red.starts[c] + (group - c) * 32
        for xy in range(4):
            red.give(group, xy, 0).wait_recv()
        def body(cols):
            grad = dot_on(left[...], right[:, cols], 0, 0)
            for xy in range(4):
                for k in range(RING):
                    rows = slice(start, start + 32)
                    at_row = k * 128 + xy * 32
                    old = wide(held[xy // 2, xy % 2, k, rows, cols])
                    held[xy // 2, xy % 2, k, rows, cols] = low(old + grad[at_row : at_row + 32])

        halves(body)

    def first_sends(c):
        red.x_copy(c, 1).start()
        red.y_copy(c, 1).start()
        red.x_copy(c, 0).start()
        red.y_copy(c, 0).start()

    keep_heads(2, ctx_v.at[:, near_half], da_v)
    first_sends(2)
    go(matrix_loads(0, 1, 0))
    qkv_load.wait()
    red.turn(0)

    key = lax.broadcasted_iota(jnp.int32, (ROWS, 1), 0)
    scale = HD ** (-0.5)

    def attend_back(k):
        lanes = [pl.ds(pl.multiple_of(k * 128 + half * TILE, 128), 128) for half in range(2)]

        def group(ref):
            return jnp.concatenate([ref[:, lane] for lane in lanes], 1)

        query = group(qkv_v.at[0]) * jnp.bfloat16(scale)
        keys, values = group(qkv_v.at[1]), group(qkv_v.at[2])
        dctx = group(dctx_v)
        none = jnp.bfloat16(0)

        def one_head(h, _):
            mask = head_mask(256, h)
            for r in range(ROWS // 128):
                cols = slice(r * 128, (r + 1) * 128)
                scores = dot_on(keys, jnp.where(mask, query[cols], none), 1, 1)
                scores = jnp.where(key < seq, scores, -1e30)
                expo = jnp.exp(scores - jnp.max(scores, 0, keepdims=True))
                probs = expo * (1.0 / jnp.sum(expo, 0, keepdims=True))
                dprobs = dot_on(values, jnp.where(mask, dctx[cols], none), 1, 1)
                delta = jnp.sum(probs * dprobs, 0, keepdims=True)
                p_v[:, cols] = low(probs)
                ds_v[:, cols] = low(probs * (dprobs - delta))
            dq = dot_on(ds_v[...], keys, 0, 0) * scale
            dk = dot_on(ds_v[...], query, 1, 0)
            dv = dot_on(p_v[...], dctx, 1, 0)
            for c, value in enumerate((dq, dk, dv)):
                dg_v[c] = jnp.where(mask, low(value), dg_v[c])
            return 0

        lax.fori_loop(0, 4, one_head, 0)
        for c in range(3):
            for half in range(2):
                qkv_v[c, :, lanes[half]] = dg_v[c, :, half * 128 : (half + 1) * 128]

    steps = [
        [lambda: red.turn(1), lambda: red.turn(2)],
        [lambda: red.rise(0)],
        [lambda: red.rise(1)],
        [lambda: red.rise(2), lambda: red.settle(0)],
    ]
    def attend_group(k, _):
        attend_back(k)
        for i in range(4):

            @pl.when(k == i)
            def _():
                for step in steps[i]:
                    step()

        return 0

    lax.fori_loop(0, 4, attend_group, 0)
    h1_load.wait()
    for c in range(3):
        slot = (c + 1) % 2
        stage_free(slot)
        stage_fill(slot, qkv_v.at[c, :, far_half], h_v)
        stage_go(slot, [red.give(3 + c, xy, slot) for xy in range(4)])
    for c in range(3):
        keep_heads(3 + c, qkv_v.at[c, :, near_half], h_v)
    first_sends(3)
    for c in range(3):
        slot = (c + 1) % 2
        filled(slot)

        def spread_back(cols, c=c, slot=slot):
            value = dot_on(qkv_v[c], w_v[slot, :, cols], 1, 0)
            dh_v[:, cols] = value if c == 0 else value + dh_v[:, cols]

        halves(spread_back)
        if c == 0:
            go(matrix_loads(0, 2, 1))
    red.spread(0)
    red.settle(1)
    x_load.wait()
    blocks_back.sent()

    def first_norm(i, _):
        block = rows_at(i * 16, 16)
        hat, inverse = norm_parts(wide(dy_v[block]))
        dh = dh_v[block]
        blk_v[block] = low(r_v[block] + norm_reverse(dh, hat, gain1, inverse))
        collect(0, dh * hat)
        collect(1, dh)
        return 0

    lax.fori_loop(0, ROWS // 16, first_norm, 0)
    grads_back.start()

    for i in range(6):
        value = jnp.sum(sums_v[i], 0, keepdims=True)
        for j in range(RING):
            for side in range(2):
                start = j * quarter + side * 128
                vec[j, 2 * i + side : 2 * i + side + 1] = value[:, start : start + 128]
    lane = lax.broadcasted_iota(jnp.int32, (8, 128), 1)
    for row, c in ((12, 0), (14, 2)):
        value = jnp.sum(wide(qkv_v[c]), 0, keepdims=True)
        for k in range(RING):
            sides = [
                jnp.broadcast_to(value[:, half * TILE + k * 128 : half * TILE + k * 128 + 128], (8, 128))
                for half in range(2)
            ]
            odd = at.core == 1
            sides = [jnp.where(odd, sides[1], sides[0]), jnp.where(odd, sides[0], sides[1])]
            for half in range(2):
                v = sides[half]
                near = jnp.where(
                    lax.rem(lane // 32, 2) == 0, pltpu.roll(v, 96, 1), pltpu.roll(v, 32, 1)
                )
                v = jnp.where(lax.rem(p // 2, 2) == 1, near, v)
                v = jnp.where(p // 4 == 1, pltpu.roll(v, 64, 1), v)
                vec[lax.rem(z + RING - k, RING), row + half : row + half + 1] = v[0:1]
    for q in range(8):
        for k in range(RING):
            at_row = pl.ds(16 + turned(p, q), 1)
            vec[lax.rem(z + RING - k, RING), at_row] = dus_v[q : q + 1, k * 128 : (k + 1) * 128]

    def vec_copy(i):
        return remote(vec, vec_far.at[i], vec_send.at[i], vec_recv.at[i], at.near((1, 2, 4)[i]))

    def vec_z(d):
        return remote(
            vec.at[at.shifts[d]],
            vec_far.at[3, d],
            vec_send.at[2 + d],
            vec_recv.at[2 + d],
            (p, at.shifts[d]),
        )

    def vec_step(i):
        vec_copy(i).wait()
        vec[...] = vec[...] + vec_far[i]

    vec_copy(0).start()
    red.turn(3)
    red.settle(2)
    vec_step(0)
    vec_copy(1).start()
    red.spread(1)
    vec_step(1)
    vec_copy(2).start()
    red.rise(3)
    vec_step(2)
    for d in range(1, RING):
        vec_z(d).start()
    red.spread(2)
    red.settle(3)
    for d in range(1, RING):
        vec_z(d).wait()
    vec[0] = vec[z] + (vec_far[3, 1] + (vec_far[3, 2] + vec_far[3, 3]))
    vec_out = pltpu.make_async_copy(vec.at[0], vector_out, local_sem.at[4])
    vec_out.start()
    red.spread(3)
    stage_free(0)
    stage_free(1)
    for c in range(4):
        red.finish(c)
    vec_out.wait()
    blocks_back.here()
    grads_back.sent()
    grads_back.here()


def backward(seq, images, mask, *arrays):
    travel, full = arrays[9].shape
    width = full // RING
    bf16 = jnp.bfloat16
    f32 = jnp.float32
    dma = pltpu.SemaphoreType.DMA
    attn_in, out_in, fc1_in, fc2_in = arrays[10:14]
    sizes = (fc2_in.shape[1], fc1_in.shape[1], out_in.shape[1], 3 * attn_in.shape[2])
    every = sum(sizes)
    outs = [jax.ShapeDtypeStruct((images, travel, width), bf16)] * 2
    outs.append(jax.ShapeDtypeStruct((24, 128), f32))
    outs += [jax.ShapeDtypeStruct((8, n, full), bf16) for n in sizes]
    any_space = pl.BlockSpec(memory_space=pl.ANY)
    vm = pltpu.VMEM
    return pl.pallas_call(
        functools.partial(backward_kernel, images, seq, sizes),
        out_shape=outs,
        in_specs=[pl.BlockSpec(memory_space=vm)] + [any_space] * len(arrays),
        out_specs=[any_space] * 7,
        scratch_shapes=[
            vm((2, 2, RING, every, full), bf16),
            vm((2, 2, 2, every, full), bf16),
            vm((2, 2, every, full), bf16),
            vm((3, every, full), bf16),
            vm((every, full), bf16),
            vm((2, RING, 128, full), bf16),
            vm((2, 1024, full), bf16),
            vm((ROWS, full), bf16),
            vm((ROWS, full), bf16),
            vm((2, ROWS, TILE), bf16),
            vm((2, ROWS, TILE), bf16),
            vm((ROWS, full), f32),
            vm((ROWS, full), f32),
            vm((ROWS, full), f32),
            vm((ROWS, full), bf16),
            vm((ROWS, full), bf16),
            vm((ROWS, full), bf16),
            vm((3, ROWS, full), bf16),
            vm((ROWS, ROWS), bf16),
            vm((ROWS, ROWS), bf16),
            vm((3, ROWS, 256), bf16),
            vm((ROWS, full), bf16),
            vm((6, 8, full), f32),
            vm((8, TILE), f32),
            vm(arrays[0].shape, bf16),
            vm((RING, 24, 128), f32),
            vm((4, RING, 24, 128), f32),
            dma((6, RING)),
            dma((6, RING)),
            dma((4, 16)),
            dma((4, 16)),
            dma((2, RING)),
            dma((2, RING)),
            dma((6,)),
            dma((6,)),
            dma((5,)),
            dma((8,)),
            dma((2, 2)),
            dma((2,)),
        ],
        compiler_params=pltpu.CompilerParams(
            collective_id=1, has_side_effects=True, vmem_limit_bytes=60 * 2**20
        ),
    )(mask, *arrays)


def pick(stack, index):
    return lax.dynamic_index_in_dim(stack, index, 0, keepdims=False)


def by_place(value, p):
    return jnp.stack([pick(value, turned(p, q)) for q in range(8)])


def prepare(tokens, cotangent, vectors, w_attn, qv_bias, w_out, w_fc1, b_fc1, w_fc2):
    images, seq, width = tokens.shape
    full = width * RING
    p = lax.axis_index("dp")
    attn = jnp.transpose(w_attn, (1, 2, 0)).reshape(3, 8, 32, full).transpose(1, 0, 2, 3)
    out = w_out.reshape(8, 32, full)
    fc1 = jnp.transpose(w_fc1).reshape(8, -1, full)
    fc2 = w_fc2.reshape(8, -1, full)
    qv = by_place(qv_bias.reshape(2, 8, 32).transpose(1, 0, 2), p)
    qv = qv.reshape(4, 2, 2, 32).transpose(2, 1, 0, 3).reshape(-1)
    hidden = by_place(b_fc1.reshape(8, -1), p).reshape(-1)
    small = jnp.concatenate(list(vectors) + [qv, hidden]).reshape(3, full)
    small = jnp.pad(small, ((0, 13), (0, 0)))
    tail = ((0, 0), (0, -seq % 16), (0, 0))
    return jnp.pad(tokens, tail), jnp.pad(cotangent, tail), small, attn, out, fc1, fc2


def image_local(
    tokens,
    image_mask,
    ln1_gain,
    first_norm_bias,
    w_attn,
    qv_bias,
    w_out,
    b_out,
    ln2_gain,
    second_norm_bias,
    w_fc1,
    b_fc1,
    w_fc2,
    b_fc2,
    cotangent,
):
    images, seq, width = tokens.shape
    full = width * RING
    p = lax.axis_index("dp")
    slot = lax.axis_index("tensor") - p % 2
    live = (slot >= 0) & (slot < images)
    mask = jnp.where(live, pick(image_mask, jnp.clip(slot, 0, images - 1)), 0)
    mask = jnp.full((8, 128), mask.astype(jnp.float32))
    vectors = (ln1_gain, first_norm_bias, b_out, ln2_gain, second_norm_bias, b_fc2)
    ready = prepare(tokens, cotangent, vectors, w_attn, qv_bias, w_out, w_fc1, b_fc1, w_fc2)
    dy, small, *rest = forward(seq, *ready)
    fulls, kept = rest[:4], rest[4:12]
    block_out, input_grad, sums, s2, s1, so, sa = backward(
        seq, images, mask, small, *kept, dy, *ready[3:], *fulls
    )
    pairs = sums.reshape(12, width)
    grad_qv = pairs[6:8].reshape(2, 2, 4, 32).transpose(0, 2, 1, 3).reshape(2, width)
    return (
        block_out[:, :seq],
        input_grad[:, :seq],
        pairs[0],
        pairs[1],
        jnp.transpose(wide(sa).reshape(8, 3, 32, full), (3, 1, 0, 2)).reshape(full, 3, width),
        grad_qv,
        wide(so).reshape(width, full),
        pairs[2],
        pairs[3],
        pairs[4],
        jnp.transpose(wide(s1).reshape(-1, full)),
        pairs[8:].reshape(-1),
        wide(s2).reshape(-1, full),
        pairs[5],
    )


def solution(mesh):
    in_specs = (
        P("dp", None, "tensor"),
        P("dp"),
        P("tensor"),
        P("tensor"),
        P(None, None, "tensor"),
        P(None, "tensor"),
        P("tensor", None),
        P("tensor"),
        P("tensor"),
        P("tensor"),
        P(None, "tensor"),
        P("tensor"),
        P("tensor", None),
        P("tensor"),
        P("dp", None, "tensor"),
    )
    out_specs = (
        P("dp", None, "tensor"),
        P("dp", None, "tensor"),
        P("tensor"),
        P("tensor"),
        P(None, None, "tensor"),
        P(None, "tensor"),
        P("tensor", None),
        P("tensor"),
        P("tensor"),
        P("tensor"),
        P(None, "tensor"),
        P("tensor"),
        P("tensor", None),
        P("tensor"),
    )
    owners = mesh.shape["dp"] == 8 and mesh.shape["tensor"] == RING

    def block(*arrays):
        images = arrays[0].shape[0] // mesh.shape["dp"]
        body = image_local if owners and images < RING else local
        return jax.shard_map(
            body, mesh=mesh, in_specs=in_specs, out_specs=out_specs, check_vma=False
        )(*arrays)

    return block
```

```python
import functools

import jax
import jax.numpy as jnp
from jax import lax
from jax.experimental import pallas as pl
from jax.experimental.pallas import tpu as pltpu
from jax.sharding import PartitionSpec as P

MODEL_WIDTH = 1024
HD = 64


EPS = 1e-05


def norm_stats(value):
    total, squares = lax.psum((jnp.sum(value, 1), jnp.sum(value * value, 1)), "tensor")
    middle = total / MODEL_WIDTH
    spread = squares / MODEL_WIDTH - middle * middle
    return (middle[:, None], lax.rsqrt(spread + EPS)[:, None])


def layer_norm_reverse(incoming_gradient, normalized_input, norm_gain, inverse_deviation):
    gain_scaled_gradient = incoming_gradient * norm_gain
    first_norm_result, second_norm_result = lax.psum(
        (jnp.sum(gain_scaled_gradient, 1), jnp.sum(gain_scaled_gradient * normalized_input, 1)),
        "tensor",
    )
    return inverse_deviation * (
        gain_scaled_gradient
        - first_norm_result[:, None] / MODEL_WIDTH
        - normalized_input * second_norm_result[:, None] / MODEL_WIDTH
    )


def spread_features(value):
    return lax.all_gather(value, "tensor", axis=1, tiled=True)


def settle_sums(value):
    return lax.psum_scatter(value, "tensor", scatter_dimension=1, tiled=True)


def pair_dot(left, right):
    return lax.dot_general(
        left, right, (((0,), (0,)), ((), ())), preferred_element_type=jnp.float32
    )


def back_dot(left, right):
    return lax.dot_general(
        left, right, (((1,), (1,)), ((), ())), preferred_element_type=jnp.float32
    )


def attend_image(blocks):
    query, keys, values = blocks
    scale = HD ** (-0.5)
    scores = jnp.einsum("qhd,khd->hqk", query, keys, preferred_element_type=jnp.float32) * scale
    top = jnp.max(scores, -1, keepdims=True)
    expo = jnp.exp(scores - top)
    total = jnp.sum(expo, -1, keepdims=True)
    probs = expo / total
    log_total = top[..., 0] + jnp.log(total[..., 0])
    context = jnp.einsum(
        "hqk,khd->qhd", probs.astype(jnp.bfloat16), values, preferred_element_type=jnp.float32
    )
    return (context.astype(jnp.bfloat16), log_total)


def attend_back(blocks):
    query, keys, values, log_total, dcontext = blocks
    scale = HD ** (-0.5)
    scores = jnp.einsum("qhd,khd->hqk", query, keys, preferred_element_type=jnp.float32) * scale
    probs = jnp.exp(scores - log_total[..., None])
    dvalues = jnp.einsum(
        "hqk,qhd->khd", probs.astype(jnp.bfloat16), dcontext, preferred_element_type=jnp.float32
    )
    dprobs = jnp.einsum("qhd,khd->hqk", dcontext, values, preferred_element_type=jnp.float32)
    delta = jnp.sum(probs * dprobs, -1, keepdims=True)
    dscores = (probs * (dprobs - delta)).astype(jnp.bfloat16)
    dquery = jnp.einsum("hqk,khd->qhd", dscores, keys, preferred_element_type=jnp.float32) * scale
    dkeys = jnp.einsum("hqk,qhd->khd", dscores, query, preferred_element_type=jnp.float32) * scale
    return jnp.stack([dquery, dkeys, dvalues], 1).astype(jnp.bfloat16)


def local(
    tokens,
    image_mask,
    ln1_gain,
    first_norm_bias,
    w_attn,
    qv_bias,
    w_out,
    b_out,
    ln2_gain,
    second_norm_bias,
    w_fc1,
    b_fc1,
    w_fc2,
    b_fc2,
    cotangent,
):
    images, seq, width_dev = tokens.shape
    rows = images * seq
    heads_dev = width_dev // HD
    mask_rows = jnp.repeat(image_mask.astype(jnp.float32), seq)[:, None]
    first_norm_gain = ln1_gain.astype(jnp.float32)
    second_norm_gain = ln2_gain.astype(jnp.float32)
    block_inputs = tokens.astype(jnp.float32).reshape(rows, width_dev)
    first_midpoint_state, first_inverse_deviation = norm_stats(block_inputs)
    first_normalized_input = (block_inputs - first_midpoint_state) * first_inverse_deviation
    h1_full = spread_features(
        (first_normalized_input * first_norm_gain + first_norm_bias.astype(jnp.float32)).astype(
            jnp.bfloat16
        )
    )
    qkv = jnp.einsum("nd,dce->nce", h1_full, w_attn, preferred_element_type=jnp.float32)
    bias_rows = qv_bias.astype(jnp.float32)
    bias_full = jnp.stack([bias_rows[0], jnp.zeros_like(bias_rows[0]), bias_rows[1]], 0)
    qkv = (qkv + bias_full).astype(jnp.bfloat16)
    query = qkv[:, 0].reshape(images, seq, heads_dev, HD)
    keys = qkv[:, 1].reshape(images, seq, heads_dev, HD)
    values = qkv[:, 2].reshape(images, seq, heads_dev, HD)
    context, log_total = lax.map(attend_image, (query, keys, values))
    context_flat = context.reshape(rows, width_dev)
    attn = settle_sums(
        jnp.dot(context_flat, w_out, preferred_element_type=jnp.float32)
    ) + b_out.astype(jnp.float32)
    residual_stream_state = block_inputs + attn
    second_midpoint_state, second_inverse_deviation = norm_stats(residual_stream_state)
    second_normalized_input = (
        residual_stream_state - second_midpoint_state
    ) * second_inverse_deviation
    h2_full = spread_features(
        (second_normalized_input * second_norm_gain + second_norm_bias.astype(jnp.float32)).astype(
            jnp.bfloat16
        )
    )
    hidden = jnp.dot(h2_full, w_fc1, preferred_element_type=jnp.float32) + b_fc1.astype(jnp.float32)
    sigma = jax.nn.sigmoid(1.702 * hidden)
    act = (hidden * sigma).astype(jnp.bfloat16)
    mlp = settle_sums(jnp.dot(act, w_fc2, preferred_element_type=jnp.float32)) + b_fc2.astype(
        jnp.float32
    )
    block_out = (
        ((residual_stream_state + mlp) * mask_rows)
        .astype(jnp.bfloat16)
        .reshape(images, seq, width_dev)
    )
    output_gradient = cotangent.astype(jnp.float32).reshape(rows, width_dev) * mask_rows
    dy_full = spread_features(output_gradient.astype(jnp.bfloat16))
    grad_b_fc2 = jnp.sum(output_gradient, 0)
    grad_w_fc2 = pair_dot(act, dy_full)
    dact = back_dot(dy_full, w_fc2)
    dhidden = (dact * (sigma + 1.702 * hidden * sigma * (1.0 - sigma))).astype(jnp.bfloat16)
    grad_b_fc1 = jnp.sum(dhidden, 0, dtype=jnp.float32)
    grad_w_fc1 = pair_dot(h2_full, dhidden)
    second_hidden_gradient = settle_sums(back_dot(dhidden, w_fc1))
    second_norm_gain_gradient = jnp.sum(second_hidden_gradient * second_normalized_input, 0)
    grad_ln2_bias = jnp.sum(second_hidden_gradient, 0)
    residual_gradient = output_gradient + layer_norm_reverse(
        second_hidden_gradient, second_normalized_input, second_norm_gain, second_inverse_deviation
    )
    dattn = residual_gradient.astype(jnp.bfloat16)
    grad_b_out = jnp.sum(dattn, 0, dtype=jnp.float32)
    dattn_full = spread_features(dattn)
    grad_w_out = pair_dot(context_flat, dattn_full)
    dcontext = back_dot(dattn_full, w_out).astype(jnp.bfloat16).reshape(images, seq, heads_dev, HD)
    dqkv = lax.map(attend_back, (query, keys, values, log_total, dcontext))
    dqkv = dqkv.reshape(rows, 3, width_dev)
    grad_w_attn = jnp.einsum("nd,nce->dce", h1_full, dqkv, preferred_element_type=jnp.float32)
    bias_sums = jnp.sum(dqkv, 0, dtype=jnp.float32)
    grad_qv_bias = jnp.stack([bias_sums[0], bias_sums[2]], 0)
    first_hidden_gradient = settle_sums(
        jnp.einsum("nce,dce->nd", dqkv, w_attn, preferred_element_type=jnp.float32)
    )
    first_norm_gain_gradient = jnp.sum(first_hidden_gradient * first_normalized_input, 0)
    grad_ln1_bias = jnp.sum(first_hidden_gradient, 0)
    input_grad = (
        (
            residual_gradient
            + layer_norm_reverse(
                first_hidden_gradient,
                first_normalized_input,
                first_norm_gain,
                first_inverse_deviation,
            )
        )
        .astype(jnp.bfloat16)
        .reshape(images, seq, width_dev)
    )
    (
        first_norm_gain_gradient,
        grad_ln1_bias,
        grad_w_attn,
        grad_qv_bias,
        grad_w_out,
        grad_b_out,
        second_norm_gain_gradient,
        grad_ln2_bias,
        grad_w_fc1,
        grad_b_fc1,
        grad_w_fc2,
        grad_b_fc2,
    ) = lax.psum(
        (
            first_norm_gain_gradient,
            grad_ln1_bias,
            grad_w_attn,
            grad_qv_bias,
            grad_w_out,
            grad_b_out,
            second_norm_gain_gradient,
            grad_ln2_bias,
            grad_w_fc1,
            grad_b_fc1,
            grad_w_fc2,
            grad_b_fc2,
        ),
        "dp",
    )
    return (
        block_out,
        input_grad,
        first_norm_gain_gradient,
        grad_ln1_bias,
        grad_w_attn,
        grad_qv_bias,
        grad_w_out,
        grad_b_out,
        second_norm_gain_gradient,
        grad_ln2_bias,
        grad_w_fc1,
        grad_b_fc1,
        grad_w_fc2,
        grad_b_fc2,
    )


RING = 4


MESH_ID = pl.DeviceIdType.MESH
ROWS = 640
TILE = 512


def low(value):
    return value.astype(jnp.bfloat16)


def wide(value):
    return value.astype(jnp.float32)


def dot_on(left, right, a, b):
    return lax.dot_general(
        left, right, (((a,), (b,)), ((), ())), preferred_element_type=jnp.float32
    )


def turned(p, q):
    return sum(lax.rem(p // bit + q // bit, 2) * bit for bit in (1, 2, 4))


def remote(src, dst, send, recv, target):
    return pltpu.make_async_remote_copy(
        src_ref=src,
        dst_ref=dst,
        send_sem=send,
        recv_sem=recv,
        device_id=target,
        device_id_type=MESH_ID,
    )


def rows_at(start, size):
    return pl.ds(pl.multiple_of(start, 16), size)


class Place:
    def __init__(self, images):
        self.p = lax.axis_index("dp")
        self.z = lax.axis_index("tensor")
        self.core = lax.rem(self.p, 2)
        self.images = images
        self.shifts = [lax.rem(self.z + d, RING) for d in range(RING)]
        self.slot = self.z - self.core
        self.live = self.holds(self.z)

    def holds(self, plane):
        return (plane - self.core >= 0) & (plane - self.core < self.images)

    def near(self, q):
        return (turned(self.p, q), self.z)

    def greet(self):
        barrier = pltpu.get_barrier_semaphore()
        for d in range(1, RING):
            pl.semaphore_signal(
                barrier, inc=1, device_id=(self.p, self.shifts[d]), device_id_type=MESH_ID
            )
        for q in (1, 2, 4, 6):
            pl.semaphore_signal(barrier, inc=1, device_id=self.near(q), device_id_type=MESH_ID)
        pl.semaphore_wait(barrier, 7)


def weight_copies(place, pieces, full, chunk, target, sem, c=0, q=0):
    if chunk >= 2:
        yield pltpu.make_async_copy(
            pieces.at[turned(place.p, q)], target.at[pl.ds(0, 128)], sem
        )
        yield pltpu.make_async_copy(full.at[q], target.at[pl.ds(128, 384)], sem)
        return
    for half in range(2):
        source = full.at[c, half] if chunk == 0 else full.at[half]
        yield pltpu.make_async_copy(source, target.at[pl.ds(half * TILE + 128, 384)], sem)
        for head in range(4):
            own = pieces.at[turned(place.p, 2 * head + half)]
            if chunk == 0:
                own = own.at[c]
            yield pltpu.make_async_copy(own, target.at[pl.ds(half * TILE + head * 32, 32)], sem)


def pair_heads(one, two):
    lane = lax.broadcasted_iota(jnp.int32, (1, 128), 1)
    return (
        jnp.where(lane < 64, one, low(pltpu.roll(wide(two), 64, 1))),
        jnp.where(lane < 64, low(pltpu.roll(wide(one), 64, 1)), two),
    )


def head_mask(h):
    lane = lax.broadcasted_iota(jnp.int32, (1, 128), 1)
    return lax.rem(lane, 64) // 32 == h


def group_lanes(k):
    return [pl.ds(pl.multiple_of(k * 128 + half * TILE, 128), 128) for half in range(2)]


def split_heads(source, target, k):
    lanes = group_lanes(k)
    target[0], target[1] = pair_heads(source[:, lanes[0]], source[:, lanes[1]])


def join_heads(source, target, k):
    lanes = group_lanes(k)
    target[:, lanes[0]], target[:, lanes[1]] = pair_heads(source[0], source[1])


class Gather:
    def __init__(self, place, pieces, fulls, sems):
        self.at = place
        self.p, self.z = place.p, place.z
        self.pieces = pieces
        self.fulls = fulls
        self.z_send, self.send, self.recv = sems
        z = self.z
        self.order = (
            jnp.where(z == 0, 3, 1),
            jnp.where((z == 0) | (z == 3), 2, 3),
            jnp.where(z == 0, 1, jnp.where(z == 3, 3, 2)),
        )

    def place(self, chunk, q, k, start=0, size=None):
        full = self.fulls[chunk]
        size = self.pieces[chunk].shape[-2] if size is None else size
        start = (k - 1) * 128 + start
        if chunk >= 2:
            return full.at[q, rows_at(start, size)]
        at = rows_at(start + (q // 2) * 32, size)
        return full.at[:, q % 2, at] if chunk == 0 else full.at[q % 2, at]

    def part(self, chunk, q, k, side):
        half = self.pieces[chunk].shape[-2] // 2
        return self.place(chunk, q, k, side * half, half)

    def up(self, chunk, k, source):
        return remote(
            source,
            self.place(chunk, 0, k + 1),
            self.z_send.at[chunk, k, 0],
            self.recv.at[chunk, k + 1, 0],
            (self.p, jnp.minimum(self.z + 1, RING - 1)),
        )

    def down(self, chunk, k, source):
        return remote(
            source,
            self.place(chunk, 0, k - 1),
            self.z_send.at[chunk, lax.rem(k, RING), 1],
            self.recv.at[chunk, k - 1, 0],
            (self.p, jnp.maximum(self.z - 1, 0)),
        )

    def z_start(self, chunk):
        piece = self.pieces[chunk].at[self.p]
        pl.when(self.z < RING - 1)(self.up(chunk, 0, piece).start)
        pl.when(self.z > 0)(self.down(chunk, RING, piece).start)

    def z_sent(self, chunk):
        piece = self.pieces[chunk].at[self.p]
        pl.when(self.z < RING - 1)(self.up(chunk, 0, piece).wait_send)
        pl.when(self.z > 0)(self.down(chunk, RING, piece).wait_send)
        for k in (1, 2, 3):
            here = self.place(chunk, 0, k)
            if k < 3:
                pl.when((self.z >= k) & (self.z < RING - 1))(self.up(chunk, k, here).wait_send)
            if k > 1:
                pl.when((self.z < k) & (self.z > 0))(self.down(chunk, k, here).wait_send)

    def plane(self, chunk, k, source, target):
        return remote(
            self.place(chunk, source, k),
            self.place(chunk, target, k),
            self.send.at[chunk, k, target],
            self.recv.at[chunk, k, target],
            self.at.near(source ^ target),
        )

    def corner(self, chunk, k, side):
        source, flip = ((4, 2), (2, 4))[side]
        return remote(
            self.part(chunk, source, k, side),
            self.part(chunk, 6, k, side),
            self.send.at[chunk, k, (6, 8)[side]],
            self.recv.at[chunk, k, (6, 8)[side]],
            self.at.near(flip),
        )

    def spread(self, chunk, i):
        k = self.order[i]
        here = self.place(chunk, 0, k)
        remote(
            here, here, self.send.at[chunk, k, 0], self.recv.at[chunk, k, 0], self.at.near(1)
        ).wait_recv()
        pl.when((self.z >= k) & (self.z < RING - 1))(self.up(chunk, k, here).start)
        pl.when((self.z < k) & (self.z > 0))(self.down(chunk, k, here).start)
        for target in (2, 4, 1):
            self.plane(chunk, k, 0, target).start()

    def relay(self, chunk, i):
        k = self.order[i]
        self.plane(chunk, k, 0, 4).wait_recv()
        self.corner(chunk, k, 0).start()
        self.plane(chunk, k, 0, 2).wait_recv()
        self.corner(chunk, k, 1).start()
        self.plane(chunk, k, 4, 5).start()
        self.plane(chunk, k, 2, 3).start()

    def share(self, chunk, i):
        k = self.order[i]
        self.corner(chunk, k, 0).wait_recv()
        self.corner(chunk, k, 1).wait_recv()
        self.plane(chunk, k, 6, 7).start()

    def whole(self, chunk):
        for k in range(1, RING):
            for target in (1, 3, 5, 7):
                self.plane(chunk, k, target - 1, target).wait_recv()

    def sent(self, chunk):
        self.z_sent(chunk)
        for k in range(1, RING):
            for source, target in ((0, 2), (0, 4), (0, 1), (4, 5), (2, 3), (6, 7)):
                self.plane(chunk, k, source, target).wait_send()
            self.corner(chunk, k, 0).wait_send()
            self.corner(chunk, k, 1).wait_send()


class Rows:
    def __init__(self, place, source, target, send, recv, local):
        self.at = place
        self.source, self.target = source, target
        self.send, self.recv, self.local = send, recv, local
        self.width = source.shape[2]

    def columns(self):
        return pl.ds(pl.multiple_of(self.at.z * self.width, self.width), self.width)

    def copy(self, d):
        dest = self.at.shifts[d]
        return remote(
            self.source.at[jnp.clip(dest - self.at.core, 0, self.at.images - 1)],
            self.target.at[:, self.columns()],
            self.send.at[d],
            self.recv.at[d],
            (self.at.p, dest),
        )

    def own(self):
        return pltpu.make_async_copy(
            self.source.at[jnp.clip(self.at.slot, 0, self.at.images - 1)],
            self.target.at[:, self.columns()],
            self.local,
        )

    def start(self):
        self.own().start()
        for d in range(1, RING):
            pl.when(self.at.holds(self.at.shifts[d]))(self.copy(d).start)

    def here(self):
        self.own().wait()
        for d in range(1, RING):
            pl.when(self.at.live)(self.copy(d).wait_recv)

    def sent(self):
        for d in range(1, RING):
            pl.when(self.at.holds(self.at.shifts[d]))(self.copy(d).wait_send)


def norm_rows(value, gain, shift):
    middle = jnp.mean(value, 1, keepdims=True)
    spread = jnp.mean(value * value, 1, keepdims=True) - middle * middle
    return (value - middle) * lax.rsqrt(spread + EPS) * gain + shift


def forward_kernel(images, seq, *refs):
    (
        tokens,
        cotangent,
        small,
        attn_in,
        out_in,
        fc1_in,
        fc2_in,
        dy_full,
        small_full,
        attn_full,
        out_full,
        fc1_full,
        fc2_full,
        x_rows_out,
        h1_out,
        qkv_out,
        ctx_out,
        r_out,
        h2_out,
        act_out,
        slope_out,
        x_full,
        x_v,
        h1_v,
        h2_v,
        qkv_v,
        ctx_v,
        r_v,
        w_v,
        act_v,
        slope_v,
        small_v,
        bias_v,
        pair_v,
        row_send,
        row_recv,
        small_send,
        small_recv,
        z_send,
        unit_send,
        unit_recv,
        local_sem,
        w_sem,
        tile_sem,
        out_sem,
    ) = refs
    at = Place(images)
    p, z = at.p, at.z
    g = Gather(
        at,
        (attn_in, out_in, fc1_in, fc2_in),
        (attn_full, out_full, fc1_full, fc2_full),
        (z_send, unit_send, unit_recv),
    )
    x_rows = Rows(at, tokens, x_full, row_send.at[0], row_recv.at[0], local_sem.at[0])
    dy_rows = Rows(at, cotangent, dy_full, row_send.at[1], row_recv.at[1], local_sem.at[1])
    travel = x_full.shape[0]
    full = x_full.shape[1]
    quarter = full // RING

    def small_copy(d):
        return remote(
            small, small_full.at[d], small_send.at[d], small_recv.at[d], (p, at.shifts[d])
        )

    small_own = pltpu.make_async_copy(small, small_full.at[0], local_sem.at[2])

    at.greet()
    g.z_start(0)
    for d in range(1, RING):
        small_copy(d).start()
    small_own.start()
    x_rows.start()
    x_v[travel:] = jnp.zeros((ROWS - travel, full), x_v.dtype)

    g.spread(0, 0)
    g.spread(0, 1)
    g.z_start(1)
    g.spread(0, 2)
    for d in range(1, RING):
        small_copy(d).wait()
    small_own.wait()
    small_load = pltpu.make_async_copy(small_full, small_v, local_sem.at[3])
    small_load.start()
    x_rows.here()
    x_load = pltpu.make_async_copy(x_full, x_v.at[pl.ds(0, travel)], local_sem.at[4])
    x_load.start()
    small_load.wait()

    def feature(row, start):
        parts = [
            small_v[lax.rem(z + RING - j, RING), row : row + 1, start : start + quarter]
            for j in range(RING)
        ]
        return wide(jnp.concatenate(parts, 1))

    def unit_blocks(row, start, size):
        return [
            wide(small_v[k, row : row + 1, start : start + size]) for k in range(RING)
        ]

    gain, shift = feature(0, 0), feature(0, quarter)
    for c, start in ((0, 2 * quarter), (2, 3 * quarter)):
        for half in range(2):
            blocks = unit_blocks(1, start + half * 128, 128)
            bias_v[c : c + 1, half * TILE : (half + 1) * TILE] = jnp.concatenate(blocks, 1)
    bias_v[1:2] = jnp.zeros((1, full), jnp.float32)
    x_load.wait()

    def first_norm(i, _):
        block = rows_at(i * 64, 64)
        value = jnp.where(at.live, wide(x_v[block]), 0.0)
        x_v[block] = low(value)
        h1_v[block] = low(norm_rows(value, gain, shift))
        return 0

    lax.fori_loop(0, ROWS // 64, first_norm, 0)
    saves = [
        pltpu.make_async_copy(x_v, x_rows_out, out_sem.at[0]),
        pltpu.make_async_copy(h1_v, h1_out, out_sem.at[1]),
    ]
    for s in saves:
        s.start()

    for i in range(3):
        g.relay(0, i)
        g.spread(1, i)
        if i == 1:
            g.z_start(2)
        if i:
            g.share(0, i - 1)
    g.share(0, 2)
    g.whole(0)

    def tile_load(chunk, c, slot):
        return list(
            weight_copies(
                at,
                (attn_in, out_in)[chunk],
                (attn_full, out_full)[chunk],
                chunk,
                w_v.at[slot],
                w_sem.at[slot],
                c,
            )
        )

    def go(copies):
        for copy in copies:
            copy.start()

    def arrive(copies):
        for copy in copies:
            copy.wait()

    def filled(slot):
        pltpu.make_async_copy(w_v.at[slot], w_v.at[slot], w_sem.at[slot]).wait()

    loads = [tile_load(0, c, c % 2) for c in range(3)] + [tile_load(1, 0, 1)]
    go(loads[0])
    go(loads[1])
    steps = [
        lambda: g.spread(2, 0),
        lambda: g.relay(1, 0),
        lambda: g.relay(1, 1),
    ]
    for c in range(3):
        filled(c % 2)

        def project(i, _, c=c):
            block = rows_at(i * TILE, TILE)
            out = dot_on(h1_v[...], w_v[c % 2, block], 1, 1)
            lanes = pl.ds(pl.multiple_of(i * TILE, TILE), TILE)
            qkv_v[c, :, lanes] = low(out + bias_v[c : c + 1, lanes])
            return 0

        lax.fori_loop(0, 2, project, 0)
        if c == 0:
            go(loads[2])
        steps[c]()
    save = pltpu.make_async_copy(qkv_v, qkv_out, out_sem.at[2])
    save.start()
    saves.append(save)

    key = lax.broadcasted_iota(jnp.int32, (ROWS, 1), 0)

    def attend(k, _):
        for c in range(3):
            split_heads(qkv_v.at[c], pair_v.at[c], k)
        for pair in range(2):
            keys, values = pair_v[1, pair], pair_v[2, pair]
            for r in range(ROWS // 128):
                block = slice(r * 128, (r + 1) * 128)
                query = pair_v[0, pair, block] * jnp.bfloat16(HD ** (-0.5))
                out = None
                for h in range(2):
                    mask = head_mask(h)
                    scores = dot_on(keys, jnp.where(mask, query, jnp.bfloat16(0)), 1, 1)
                    scores = jnp.where(key < seq, scores, -1e30)
                    expo = jnp.exp(scores - jnp.max(scores, 0, keepdims=True))
                    probs = low(expo * (1.0 / jnp.sum(expo, 0, keepdims=True)))
                    part = dot_on(probs, values, 0, 0)
                    out = part if out is None else jnp.where(mask, part, out)
                pair_v[0, pair, block] = low(out)
        join_heads(pair_v.at[0], ctx_v, k)
        for i in range(4):

            @pl.when(k == i)
            def _():
                for step in attention_steps[i]:
                    step()

        return 0

    attention_steps = [
        [lambda: g.spread(2, 1), lambda: g.z_start(3), lambda: g.relay(1, 2)],
        [lambda: g.spread(2, 2), lambda: g.share(1, 0), lambda: g.share(1, 1)],
        [lambda: g.share(1, 2), lambda: g.relay(2, 0), lambda: g.spread(3, 0)],
        [lambda: g.relay(2, 1), lambda: g.spread(3, 1), dy_rows.start],
    ]
    lax.fori_loop(0, 4, attend, 0)
    g.whole(1)
    go(loads[3])
    save = pltpu.make_async_copy(ctx_v, ctx_out, out_sem.at[3])
    save.start()
    saves.append(save)
    out_bias = feature(0, 2 * quarter)
    gain2, shift2 = feature(0, 3 * quarter), feature(1, 0)
    filled(1)
    for i in range(2):
        lanes = slice(i * TILE, (i + 1) * TILE)
        attn = dot_on(ctx_v[...], w_v[1, :, lanes], 1, 0)
        r_v[:, lanes] = wide(x_v[:, lanes]) + (attn + out_bias[:, lanes])
    save = pltpu.make_async_copy(r_v, r_out, out_sem.at[4])
    save.start()
    saves.append(save)
    g.relay(2, 2)
    g.spread(3, 2)
    g.share(2, 0)

    def second_norm(i, _):
        block = rows_at(i * 64, 64)
        h2_v[block] = low(norm_rows(r_v[block], gain2, shift2))
        return 0

    lax.fori_loop(0, ROWS // 64, second_norm, 0)
    save = pltpu.make_async_copy(h2_v, h2_out, out_sem.at[5])
    save.start()
    saves.append(save)
    g.share(2, 1)
    g.relay(3, 0)
    g.share(2, 2)
    g.whole(2)

    def pair_load(i):
        slot = i % 2
        for side in range(2):
            yield from weight_copies(
                at,
                fc1_in,
                fc1_full,
                2,
                w_v.at[slot, pl.ds(side * TILE, TILE)],
                w_sem.at[slot],
                q=2 * i + side,
            )

    def tile_saves(q):
        slot = q % 2
        return [
            pltpu.make_async_copy(act_v.at[slot], act_out.at[q], tile_sem.at[0, slot]),
            pltpu.make_async_copy(slope_v.at[slot], slope_out.at[q], tile_sem.at[1, slot]),
        ]

    pairs = [list(pair_load(i)) for i in range(4)]
    go(pairs[0])
    go(pairs[1])
    steps = [
        [lambda: g.relay(3, 1)],
        [lambda: g.relay(3, 2)],
        [lambda: g.share(3, 0), lambda: g.share(3, 1)],
        [lambda: g.share(3, 2)],
    ]
    for i in range(4):
        filled(i % 2)
        for side in range(2):
            q = 2 * i + side
            if q >= 2:
                arrive(tile_saves(q - 2))
            bias = jnp.concatenate(unit_blocks(2, q * 128, 128), 1)
            for j in range(2):
                cols = slice(j * 256, (j + 1) * 256)
                start = side * TILE + j * 256
                u = dot_on(h2_v[...], w_v[i % 2, start : start + 256], 1, 1) + bias[:, cols]
                sg = 1.0 / (1.0 + jnp.exp(-1.702 * u))
                act_v[side, :, cols] = low(u * sg)
                slope_v[side, :, cols] = low(sg + 1.702 * u * sg * (1.0 - sg))
            go(tile_saves(q))
        if i < 2:
            go(pairs[i + 2])
        for step in steps[i]:
            step()
    for q in (6, 7):
        arrive(tile_saves(q))
    arrive(saves)
    g.whole(3)
    dy_rows.here()
    for chunk in range(4):
        g.sent(chunk)
    x_rows.sent()
    dy_rows.sent()


def forward(seq, tokens, cotangent, small, attn_in, out_in, fc1_in, fc2_in):
    images, rows, width = tokens.shape
    full = RING * width
    bf16 = jnp.bfloat16
    f32 = jnp.float32
    dma = pltpu.SemaphoreType.DMA
    shapes = (
        ((rows, full), bf16),
        ((RING,) + small.shape, bf16),
        ((3, 2, 384, full), bf16),
        ((2, 384, full), bf16),
        ((8, 384, full), bf16),
        ((8, 384, full), bf16),
        ((ROWS, full), bf16),
        ((ROWS, full), bf16),
        ((3, ROWS, full), bf16),
        ((ROWS, full), bf16),
        ((ROWS, full), f32),
        ((ROWS, full), bf16),
        ((8, ROWS, TILE), bf16),
        ((8, ROWS, TILE), bf16),
        ((rows, full), bf16),
    )
    return pl.pallas_call(
        functools.partial(forward_kernel, images, seq),
        out_shape=[jax.ShapeDtypeStruct(s, d) for s, d in shapes],
        in_specs=[pl.BlockSpec(memory_space=pl.ANY)] * 7,
        out_specs=[pl.BlockSpec(memory_space=pl.ANY)] * len(shapes),
        scratch_shapes=[
            pltpu.VMEM((ROWS, full), bf16),
            pltpu.VMEM((ROWS, full), bf16),
            pltpu.VMEM((ROWS, full), bf16),
            pltpu.VMEM((3, ROWS, full), bf16),
            pltpu.VMEM((ROWS, full), bf16),
            pltpu.VMEM((ROWS, full), f32),
            pltpu.VMEM((2, 1024, full), bf16),
            pltpu.VMEM((2, ROWS, TILE), bf16),
            pltpu.VMEM((2, ROWS, TILE), bf16),
            pltpu.VMEM((RING,) + small.shape, bf16),
            pltpu.VMEM((8, full), f32),
            pltpu.VMEM((3, 2, ROWS, 128), bf16),
            dma((2, RING)),
            dma((2, RING)),
            dma((RING,)),
            dma((RING,)),
            dma((4, RING, 2)),
            dma((4, RING, 9)),
            dma((4, RING, 9)),
            dma((5,)),
            dma((2,)),
            dma((2, 2)),
            dma((6,)),
        ],
        compiler_params=pltpu.CompilerParams(
            collective_id=0, has_side_effects=True, vmem_limit_bytes=56 * 2**20
        ),
    )(tokens, cotangent, small, attn_in, out_in, fc1_in, fc2_in)


class Reduce:
    def __init__(self, place, sizes, outs, bufs, sems):
        self.at = place
        self.sizes = sizes
        self.starts = [sum(sizes[:i]) for i in range(4)]
        self.outs = outs
        self.held, self.first, self.second, self.far, self.total, self.stage = bufs
        self.core_send, self.core_recv, self.send, self.recv, self.local = sems

    def rows(self, c):
        return pl.ds(self.starts[c], self.sizes[c])

    def give(self, group, xy, slot):
        y, x = xy // 2, lax.rem(xy, 2)
        c = min(group, 3)
        if c < 2:
            source, at = self.stage.at[slot], self.rows(c)
        else:
            source = self.stage.at[slot, :, pl.ds(xy * 32, 32)]
            at = pl.ds(self.starts[c] + (group - c) * 32, 32)
        return remote(
            source,
            self.held.at[y, x, :, at],
            self.core_send.at[group, xy],
            self.core_recv.at[group, xy],
            self.at.near(1),
        )

    def hop(self, source, target, c, i, q):
        return remote(source, target, self.send.at[c, i], self.recv.at[c, i], self.at.near(q))

    def x_copy(self, c, y):
        at = self.rows(c)
        return self.hop(self.held.at[y, 1, 0:2, at], self.first.at[0, y, :, at], c, y, 2)

    def y_copy(self, c, x):
        at = self.rows(c)
        return self.hop(self.held.at[1, x, 2:4, at], self.first.at[1, x, :, at], c, 2 + x, 4)

    def xy_copy(self, c):
        at = self.rows(c)
        return self.hop(self.first.at[0, 1, :, at], self.second.at[0, :, at], c, 4, 4)

    def yx_copy(self, c):
        at = self.rows(c)
        return self.hop(self.first.at[1, 1, :, at], self.second.at[1, :, at], c, 5, 2)

    def z_copy(self, c, k):
        return remote(
            self.second.at[k // 2, k % 2, self.rows(c)],
            self.far.at[k - 1, self.rows(c)],
            self.send.at[c, 5 + k],
            self.recv.at[c, 5 + k],
            (self.at.p, self.at.shifts[RING - k]),
        )

    def out_copy(self, c, q):
        return self.hop(self.total.at[self.rows(c)], self.outs[c].at[self.at.p], c, 8 + q, q)

    def out_here(self, c, q):
        block = self.outs[c].at[turned(self.at.p, q)]
        self.hop(self.total.at[self.rows(c)], block, c, 8 + q, q).wait_recv()

    def out_own(self, c):
        return pltpu.make_async_copy(
            self.total.at[self.rows(c)], self.outs[c].at[self.at.p], self.local.at[c]
        )

    def share(self, c, q):
        block = self.outs[c].at[turned(self.at.p, q)]
        return self.hop(block, block, c, 9 + q, 1)

    def share_here(self, c, q):
        block = self.outs[c].at[turned(self.at.p, q)]
        theirs = self.outs[c].at[turned(self.at.p, q + 1)]
        self.hop(block, theirs, c, 9 + q, 1).wait_recv()

    def add(self, dest, *sources):
        def body(i, _):
            at = rows_at(i * 16, 16)
            value = wide(sources[0][at])
            for s in sources[1:]:
                value = value + wide(s[at])
            dest[at] = low(value)
            return 0

        lax.fori_loop(0, dest.shape[0] // 16, body, 0)

    def turn(self, c):
        at = self.rows(c)
        self.x_copy(c, 1).wait_recv()
        for k in range(2):
            block = self.first.at[0, 1, k, at]
            self.add(block, block, self.held.at[1, 0, k, at])
        self.xy_copy(c).start()
        self.y_copy(c, 1).wait_recv()
        for k in range(2):
            block = self.first.at[1, 1, k, at]
            self.add(block, block, self.held.at[0, 1, 2 + k, at])
        self.yx_copy(c).start()

    def rise(self, c):
        at = self.rows(c)
        self.x_copy(c, 0).wait_recv()
        self.xy_copy(c).wait_recv()
        for k in range(2):
            block = self.second.at[0, k, at]
            self.add(block, block, self.first.at[0, 0, k, at], self.held.at[0, 0, k, at])
        self.z_copy(c, 1).start()
        self.y_copy(c, 0).wait_recv()
        self.yx_copy(c).wait_recv()
        for k in range(2):
            block = self.second.at[1, k, at]
            self.add(block, block, self.first.at[1, 0, k, at], self.held.at[0, 0, 2 + k, at])
            self.z_copy(c, 2 + k).start()

    def settle(self, c):
        at = self.rows(c)
        for k in range(1, RING):
            self.z_copy(c, k).wait_recv()
        self.add(
            self.total.at[at], self.second.at[0, 0, at], *(self.far.at[k, at] for k in range(3))
        )
        self.out_own(c).start()
        for q in (2, 4, 6, 1):
            self.out_copy(c, q).start()

    def spread(self, c):
        for q in (2, 4, 6):
            self.out_here(c, q)
            self.share(c, q).start()

    def finish(self, c):
        self.out_here(c, 1)
        for q in (2, 4, 6):
            self.share_here(c, q)
            self.share(c, q).wait_send()
        for i in range(2):
            self.x_copy(c, i).wait_send()
            self.y_copy(c, i).wait_send()
        self.xy_copy(c).wait_send()
        self.yx_copy(c).wait_send()
        for k in range(1, RING):
            self.z_copy(c, k).wait_send()
        for q in (2, 4, 6, 1):
            self.out_copy(c, q).wait_send()
        self.out_own(c).wait()


class Return:
    def __init__(self, place, source, target, send, recv):
        self.at = place
        self.source, self.target = source, target
        self.send, self.recv = send, recv
        self.rows, self.width = target.shape[1], target.shape[2]

    def pair(self, plane):
        columns = pl.ds(pl.multiple_of(plane * self.width, self.width), self.width)
        slot = jnp.clip(self.at.slot, 0, self.at.images - 1)
        return self.source.at[pl.ds(0, self.rows), columns], self.target.at[slot]

    def copy(self, d):
        source, target = self.pair(self.at.shifts[d])
        return remote(
            source, target, self.send.at[d], self.recv.at[d], (self.at.p, self.at.shifts[d])
        )

    def own(self):
        return pltpu.make_async_copy(*self.pair(self.at.z), self.send.at[0])

    def start(self):
        pl.when(self.at.live)(self.own().start)
        for d in range(1, RING):
            pl.when(self.at.live)(self.copy(d).start)

    def sent(self):
        pl.when(self.at.live)(self.own().wait)
        for d in range(1, RING):
            pl.when(self.at.live)(self.copy(d).wait_send)

    def here(self):
        for d in range(1, RING):
            other = lax.rem(self.at.z + RING - d, RING)
            pl.when(self.at.holds(other))(self.copy(d).wait_recv)


def norm_parts(value):
    middle = jnp.mean(value, 1, keepdims=True)
    spread = jnp.mean(value * value, 1, keepdims=True) - middle * middle
    inverse = lax.rsqrt(spread + EPS)
    return (value - middle) * inverse, inverse


def norm_reverse(gradient, normalized, gain, inverse):
    scaled = gradient * gain
    first = jnp.mean(scaled, 1, keepdims=True)
    second = jnp.mean(scaled * normalized, 1, keepdims=True)
    return inverse * (scaled - first - normalized * second)


def backward_kernel(images, seq, sizes, *refs):
    (
        mask_in,
        small_full,
        x_in,
        h1_in,
        qkv_in,
        ctx_in,
        r_in,
        h2_in,
        act_in,
        slope_in,
        dy_in,
        attn_in,
        out_in,
        fc1_in,
        fc2_in,
        attn_full,
        out_full,
        fc1_full,
        fc2_full,
        block_out,
        grad_out,
        vector_out,
        s2,
        s1,
        so,
        sa,
        held,
        first,
        second,
        far,
        total,
        stage,
        w_v,
        dy_v,
        h_v,
        act_v,
        du_v,
        mlp_v,
        dh_v,
        r_v,
        da_v,
        ctx_v,
        dctx_v,
        qkv_v,
        p_v,
        ds_v,
        dg_v,
        pair_v,
        blk_v,
        sums_v,
        dus_v,
        small_v,
        vec,
        vec_far,
        core_send,
        core_recv,
        send,
        recv,
        row_send,
        row_recv,
        vec_send,
        vec_recv,
        local_sem,
        load_sem,
        tile_sem,
        w_sem,
    ) = refs
    at = Place(images)
    p, z = at.p, at.z
    full = x_in.shape[1]
    quarter = full // RING
    travel = dy_in.shape[0]
    red = Reduce(
        at,
        sizes,
        (s2, s1, so, sa),
        (held, first, second, far, total, stage),
        (core_send, core_recv, send, recv, local_sem),
    )
    blocks_back = Return(at, blk_v, block_out, row_send.at[0], row_recv.at[0])
    grads_back = Return(at, blk_v, grad_out, row_send.at[1], row_recv.at[1])

    def load(source, target, i):
        return pltpu.make_async_copy(source, target, load_sem.at[i])

    dy_load = load(dy_in, dy_v.at[pl.ds(0, travel)], 0)
    h2_load = load(h2_in, h_v, 1)
    r_load = load(r_in, r_v, 2)
    ctx_load = load(ctx_in, ctx_v, 3)
    qkv_load = load(qkv_in, qkv_v, 4)
    small_load = load(small_full, small_v, 5)
    h1_load = load(h1_in, h_v, 6)
    x_load = load(x_in, dy_v, 7)

    def tile_loads(q, slot):
        yield pltpu.make_async_copy(act_in.at[q], act_v.at[slot], tile_sem.at[0, slot])
        yield pltpu.make_async_copy(slope_in.at[q], du_v.at[slot], tile_sem.at[1, slot])
        for side, (pieces, whole) in enumerate(((fc1_in, fc1_full), (fc2_in, fc2_full))):
            yield from weight_copies(
                at, pieces, whole, 2, w_v.at[slot, pl.ds(side * TILE, TILE)], w_sem.at[slot], q=q
            )

    def matrix_loads(chunk, c, slot):
        pieces, whole = ((attn_in, attn_full), (out_in, out_full))[chunk]
        return weight_copies(at, pieces, whole, chunk, w_v.at[slot], w_sem.at[slot], c)

    def go(copies):
        for copy in copies:
            copy.start()

    def filled(slot):
        pltpu.make_async_copy(w_v.at[slot], w_v.at[slot], w_sem.at[slot]).wait()

    def turn_of(i):
        return jnp.where(i == 0, 3, jnp.where(i == 1, 1, jnp.where(i == 2, 2, 0)))

    dy_load.start()
    go(tile_loads(7, 0))
    h2_load.start()
    at.greet()
    go(tile_loads(6, 1))
    small_load.start()
    r_load.start()
    ctx_load.start()
    qkv_load.start()

    dy_v[travel:] = jnp.zeros((ROWS - travel, full), dy_v.dtype)
    sums_v[...] = jnp.zeros_like(sums_v)
    mask = mask_in[0:1, 0:1]
    dy_load.wait()

    def masked(i, _):
        block = rows_at(i * 16, 16)
        dy_v[block] = low(jnp.where(at.live, wide(dy_v[block]), 0.0) * mask)
        return 0

    lax.fori_loop(0, travel // 16, masked, 0)
    h2_load.wait()

    def halves(body):
        lax.fori_loop(0, 2, lambda j, _: (body(pl.ds(pl.multiple_of(j * TILE, TILE), TILE)), 0)[1], 0)

    def keep(group, xy, left, right):
        y, x = xy // 2, lax.rem(xy, 2)
        red.give(group, xy, 0).wait_recv()
        at_rows = red.rows(group)

        def body(cols):
            grad = dot_on(left[...], right[:, cols], 0, 0)
            for k in range(RING):
                old = wide(held[y, x, k, at_rows, cols])
                held[y, x, k, at_rows, cols] = low(old + grad[k * 128 : (k + 1) * 128])

        halves(body)
        pl.when(x == 1)(red.x_copy(group, y).start)
        pl.when(y == 1)(red.y_copy(group, x).start)

    def stage_fill(slot, left, right):
        def body(cols):
            grad = low(dot_on(left[...], right[:, cols], 0, 0))
            for k in range(RING):
                stage[slot, k, :, cols] = grad[k * 128 : (k + 1) * 128]

        halves(body)

    mlp_v[...] = jnp.zeros_like(mlp_v)
    dh_v[...] = jnp.zeros_like(dh_v)

    def hidden_tile(i, core):
        slot = 1 - core
        xy = turn_of(i)
        q = 2 * xy + core
        pltpu.make_async_copy(act_in.at[q], act_v.at[slot], tile_sem.at[0, slot]).wait()
        if core:
            pl.when(i > 0)(red.give(0, turn_of(i - 1), 0).wait_send)
            stage_fill(0, act_v.at[slot], dy_v)
            red.give(0, xy, 0).start()
        else:
            keep(0, xy, act_v.at[slot], dy_v)
        pltpu.make_async_copy(slope_in.at[q], du_v.at[slot], tile_sem.at[1, slot]).wait()
        filled(slot)

        def slopes(j, _):
            cols = pl.ds(pl.multiple_of(j * 256, 256), 256)
            start = pl.ds(pl.multiple_of(TILE + j * 256, 256), 256)
            dact = dot_on(dy_v[...], w_v[slot, start], 1, 1)
            du = low(dact * wide(du_v[slot, :, cols]))
            du_v[slot, :, cols] = du
            dus_v[pl.ds(q, 1), cols] = jnp.sum(wide(du), 0, keepdims=True)
            return 0

        lax.fori_loop(0, 2, slopes, 0)
        if core:
            pl.when(i > 0)(red.give(1, turn_of(i - 1), 1).wait_send)
            stage_fill(1, du_v.at[slot], h_v)
            red.give(1, xy, 1).start()
        else:
            keep(1, xy, du_v.at[slot], h_v)

        def back(cols):
            mlp_v[:, cols] += dot_on(act_v[slot], w_v[slot, TILE:, cols], 1, 0)
            dh_v[:, cols] += dot_on(du_v[slot], w_v[slot, :TILE, cols], 1, 0)

        halves(back)

        @pl.when(i < 3)
        def _():
            go(tile_loads(2 * turn_of(i + 1) + core, slot))

    def hidden_tiles(i, _):
        hidden_tile(i, 1)
        hidden_tile(i, 0)
        return 0

    lax.fori_loop(0, 4, hidden_tiles, 0)
    go(matrix_loads(1, 0, 0))
    go(matrix_loads(0, 0, 1))
    h1_load.start()

    small_load.wait()

    def feature(row, start):
        parts = [
            small_v[lax.rem(z + RING - j, RING), row : row + 1, start : start + quarter]
            for j in range(RING)
        ]
        return wide(jnp.concatenate(parts, 1))

    gain1, gain2 = feature(0, 0), feature(0, 3 * quarter)
    fc2_bias = feature(1, quarter)
    r_load.wait()

    def collect(i, value):
        sums_v[i] = sums_v[i] + sum(value[r : r + 8] for r in range(0, value.shape[0], 8))

    def second_norm(i, _):
        block = rows_at(i * 32, 32)
        r1 = r_v[block]
        dy = wide(dy_v[block])
        blk_v[block] = low((r1 + (mlp_v[block] + fc2_bias)) * mask)
        hat, inverse = norm_parts(r1)
        dh = dh_v[block]
        dr1 = dy + norm_reverse(dh, hat, gain2, inverse)
        da = low(dr1)
        r_v[block] = dr1
        da_v[block] = da
        collect(2, wide(da))
        collect(3, dh * hat)
        collect(4, dh)
        collect(5, dy)
        return 0

    lax.fori_loop(0, ROWS // 32, second_norm, 0)
    blocks_back.start()
    x_load.start()
    ctx_load.wait()

    pending = [[red.give(0, 0, 0)], [red.give(1, 0, 1)]]

    def stage_free(slot):
        for copy in pending[slot]:
            copy.wait_send()
        pending[slot] = []

    def stage_go(slot, copies):
        go(copies)
        pending[slot] = copies

    far_half = pl.ds(TILE, TILE)
    near_half = pl.ds(0, TILE)
    stage_free(0)
    stage_fill(0, ctx_v.at[:, far_half], da_v)
    stage_go(0, [red.give(2, xy, 0) for xy in range(4)])
    filled(0)

    def dctx_half(rows):
        dctx_v[:, rows] = low(dot_on(da_v[...], w_v[0, rows], 1, 1))

    halves(dctx_half)

    def keep_heads(group, left, right):
        c = min(group, 3)
        start = red.starts[c] + (group - c) * 32
        for xy in range(4):
            red.give(group, xy, 0).wait_recv()
        def body(cols):
            grad = dot_on(left[...], right[:, cols], 0, 0)
            for xy in range(4):
                for k in range(RING):
                    rows = slice(start, start + 32)
                    at_row = k * 128 + xy * 32
                    old = wide(held[xy // 2, xy % 2, k, rows, cols])
                    held[xy // 2, xy % 2, k, rows, cols] = low(old + grad[at_row : at_row + 32])

        halves(body)

    def first_sends(c):
        red.x_copy(c, 1).start()
        red.y_copy(c, 1).start()
        red.x_copy(c, 0).start()
        red.y_copy(c, 0).start()

    keep_heads(2, ctx_v.at[:, near_half], da_v)
    first_sends(2)
    go(matrix_loads(0, 1, 0))
    qkv_load.wait()
    red.turn(0)

    key = lax.broadcasted_iota(jnp.int32, (ROWS, 1), 0)
    scale = HD ** (-0.5)

    none = jnp.bfloat16(0)

    def attend_back(k):
        for c in range(3):
            split_heads(qkv_v.at[c], pair_v.at[c], k)
        split_heads(dctx_v, pair_v.at[3], k)

        def one_pair(pair, _):
            query = pair_v[0, pair] * jnp.bfloat16(scale)
            keys, values = pair_v[1, pair], pair_v[2, pair]
            dctx = pair_v[3, pair]
            for h in range(2):
                mask = head_mask(h)
                for r in range(ROWS // 128):
                    cols = slice(r * 128, (r + 1) * 128)
                    scores = dot_on(keys, jnp.where(mask, query[cols], none), 1, 1)
                    scores = jnp.where(key < seq, scores, -1e30)
                    expo = jnp.exp(scores - jnp.max(scores, 0, keepdims=True))
                    probs = expo * (1.0 / jnp.sum(expo, 0, keepdims=True))
                    dprobs = dot_on(values, jnp.where(mask, dctx[cols], none), 1, 1)
                    delta = jnp.sum(probs * dprobs, 0, keepdims=True)
                    p_v[:, cols] = low(probs)
                    ds_v[:, cols] = low(probs * (dprobs - delta))
                dq = dot_on(ds_v[...], keys, 0, 0) * scale
                dk = dot_on(ds_v[...], query, 1, 0)
                dv = dot_on(p_v[...], dctx, 1, 0)
                for c, value in enumerate((dq, dk, dv)):
                    if h == 0:
                        dg_v[c, pair] = low(value)
                    else:
                        dg_v[c, pair] = jnp.where(mask, low(value), dg_v[c, pair])
            return 0

        lax.fori_loop(0, 2, one_pair, 0)
        for c in range(3):
            join_heads(dg_v.at[c], qkv_v.at[c], k)

    steps = [
        [lambda: red.turn(1), lambda: red.turn(2)],
        [lambda: red.rise(0)],
        [lambda: red.rise(1)],
        [lambda: red.rise(2), lambda: red.settle(0)],
    ]
    def attend_group(k, _):
        attend_back(k)
        for i in range(4):

            @pl.when(k == i)
            def _():
                for step in steps[i]:
                    step()

        return 0

    lax.fori_loop(0, 4, attend_group, 0)
    h1_load.wait()
    for c in range(3):
        slot = (c + 1) % 2
        stage_free(slot)
        stage_fill(slot, qkv_v.at[c, :, far_half], h_v)
        stage_go(slot, [red.give(3 + c, xy, slot) for xy in range(4)])
    for c in range(3):
        keep_heads(3 + c, qkv_v.at[c, :, near_half], h_v)
    first_sends(3)
    for c in range(3):
        slot = (c + 1) % 2
        filled(slot)

        def spread_back(cols, c=c, slot=slot):
            value = dot_on(qkv_v[c], w_v[slot, :, cols], 1, 0)
            dh_v[:, cols] = value if c == 0 else value + dh_v[:, cols]

        halves(spread_back)
        if c == 0:
            go(matrix_loads(0, 2, 1))
    red.spread(0)
    red.settle(1)
    x_load.wait()
    blocks_back.sent()

    def first_norm(i, _):
        block = rows_at(i * 32, 32)
        hat, inverse = norm_parts(wide(dy_v[block]))
        dh = dh_v[block]
        blk_v[block] = low(r_v[block] + norm_reverse(dh, hat, gain1, inverse))
        collect(0, dh * hat)
        collect(1, dh)
        return 0

    lax.fori_loop(0, ROWS // 32, first_norm, 0)
    grads_back.start()

    for i in range(6):
        value = jnp.sum(sums_v[i], 0, keepdims=True)
        for j in range(RING):
            for side in range(2):
                start = j * quarter + side * 128
                vec[j, 2 * i + side : 2 * i + side + 1] = value[:, start : start + 128]
    lane = lax.broadcasted_iota(jnp.int32, (8, 128), 1)
    for row, c in ((12, 0), (14, 2)):
        value = jnp.sum(wide(qkv_v[c]), 0, keepdims=True)
        for k in range(RING):
            sides = [
                jnp.broadcast_to(value[:, half * TILE + k * 128 : half * TILE + k * 128 + 128], (8, 128))
                for half in range(2)
            ]
            odd = at.core == 1
            sides = [jnp.where(odd, sides[1], sides[0]), jnp.where(odd, sides[0], sides[1])]
            for half in range(2):
                v = sides[half]
                near = jnp.where(
                    lax.rem(lane // 32, 2) == 0, pltpu.roll(v, 96, 1), pltpu.roll(v, 32, 1)
                )
                v = jnp.where(lax.rem(p // 2, 2) == 1, near, v)
                v = jnp.where(p // 4 == 1, pltpu.roll(v, 64, 1), v)
                vec[lax.rem(z + RING - k, RING), row + half : row + half + 1] = v[0:1]
    for q in range(8):
        for k in range(RING):
            at_row = pl.ds(16 + turned(p, q), 1)
            vec[lax.rem(z + RING - k, RING), at_row] = dus_v[q : q + 1, k * 128 : (k + 1) * 128]

    def vec_copy(i):
        return remote(vec, vec_far.at[i], vec_send.at[i], vec_recv.at[i], at.near((1, 2, 4)[i]))

    def vec_z(d):
        return remote(
            vec.at[at.shifts[d]],
            vec_far.at[3, d],
            vec_send.at[2 + d],
            vec_recv.at[2 + d],
            (p, at.shifts[d]),
        )

    def vec_step(i):
        vec_copy(i).wait()
        vec[...] = vec[...] + vec_far[i]

    vec_copy(0).start()
    red.turn(3)
    red.settle(2)
    vec_step(0)
    vec_copy(1).start()
    red.spread(1)
    vec_step(1)
    vec_copy(2).start()
    red.rise(3)
    vec_step(2)
    for d in range(1, RING):
        vec_z(d).start()
    red.spread(2)
    red.settle(3)
    for d in range(1, RING):
        vec_z(d).wait()
    vec[0] = vec[z] + (vec_far[3, 1] + (vec_far[3, 2] + vec_far[3, 3]))
    vec_out = pltpu.make_async_copy(vec.at[0], vector_out, local_sem.at[4])
    vec_out.start()
    red.spread(3)
    stage_free(0)
    stage_free(1)
    for c in range(4):
        red.finish(c)
    vec_out.wait()
    blocks_back.here()
    grads_back.sent()
    grads_back.here()


def backward(seq, images, mask, *arrays):
    travel, full = arrays[9].shape
    width = full // RING
    bf16 = jnp.bfloat16
    f32 = jnp.float32
    dma = pltpu.SemaphoreType.DMA
    attn_in, out_in, fc1_in, fc2_in = arrays[10:14]
    sizes = (fc2_in.shape[1], fc1_in.shape[1], out_in.shape[1], 3 * attn_in.shape[2])
    every = sum(sizes)
    outs = [jax.ShapeDtypeStruct((images, travel, width), bf16)] * 2
    outs.append(jax.ShapeDtypeStruct((24, 128), f32))
    outs += [jax.ShapeDtypeStruct((8, n, full), bf16) for n in sizes]
    any_space = pl.BlockSpec(memory_space=pl.ANY)
    vm = pltpu.VMEM
    return pl.pallas_call(
        functools.partial(backward_kernel, images, seq, sizes),
        out_shape=outs,
        in_specs=[pl.BlockSpec(memory_space=vm)] + [any_space] * len(arrays),
        out_specs=[any_space] * 7,
        scratch_shapes=[
            vm((2, 2, RING, every, full), bf16),
            vm((2, 2, 2, every, full), bf16),
            vm((2, 2, every, full), bf16),
            vm((3, every, full), bf16),
            vm((every, full), bf16),
            vm((2, RING, 128, full), bf16),
            vm((2, 1024, full), bf16),
            vm((ROWS, full), bf16),
            vm((ROWS, full), bf16),
            vm((2, ROWS, TILE), bf16),
            vm((2, ROWS, TILE), bf16),
            vm((ROWS, full), f32),
            vm((ROWS, full), f32),
            vm((ROWS, full), f32),
            vm((ROWS, full), bf16),
            vm((ROWS, full), bf16),
            vm((ROWS, full), bf16),
            vm((3, ROWS, full), bf16),
            vm((ROWS, ROWS), bf16),
            vm((ROWS, ROWS), bf16),
            vm((3, 2, ROWS, 128), bf16),
            vm((4, 2, ROWS, 128), bf16),
            vm((ROWS, full), bf16),
            vm((6, 8, full), f32),
            vm((8, TILE), f32),
            vm(arrays[0].shape, bf16),
            vm((RING, 24, 128), f32),
            vm((4, RING, 24, 128), f32),
            dma((6, RING)),
            dma((6, RING)),
            dma((4, 16)),
            dma((4, 16)),
            dma((2, RING)),
            dma((2, RING)),
            dma((6,)),
            dma((6,)),
            dma((5,)),
            dma((8,)),
            dma((2, 2)),
            dma((2,)),
        ],
        compiler_params=pltpu.CompilerParams(
            collective_id=1, has_side_effects=True, vmem_limit_bytes=60 * 2**20
        ),
    )(mask, *arrays)


def pick(stack, index):
    return lax.dynamic_index_in_dim(stack, index, 0, keepdims=False)


def by_place(value, p):
    return jnp.stack([pick(value, turned(p, q)) for q in range(8)])


def prepare(tokens, cotangent, vectors, w_attn, qv_bias, w_out, w_fc1, b_fc1, w_fc2):
    images, seq, width = tokens.shape
    full = width * RING
    p = lax.axis_index("dp")
    attn = jnp.transpose(w_attn, (1, 2, 0)).reshape(3, 8, 32, full).transpose(1, 0, 2, 3)
    out = w_out.reshape(8, 32, full)
    fc1 = jnp.transpose(w_fc1).reshape(8, -1, full)
    fc2 = w_fc2.reshape(8, -1, full)
    qv = by_place(qv_bias.reshape(2, 8, 32).transpose(1, 0, 2), p)
    qv = qv.reshape(4, 2, 2, 32).transpose(2, 1, 0, 3).reshape(-1)
    hidden = by_place(b_fc1.reshape(8, -1), p).reshape(-1)
    small = jnp.concatenate(list(vectors) + [qv, hidden]).reshape(3, full)
    small = jnp.pad(small, ((0, 13), (0, 0)))
    tail = ((0, 0), (0, -seq % 16), (0, 0))
    return jnp.pad(tokens, tail), jnp.pad(cotangent, tail), small, attn, out, fc1, fc2


def image_local(
    tokens,
    image_mask,
    ln1_gain,
    first_norm_bias,
    w_attn,
    qv_bias,
    w_out,
    b_out,
    ln2_gain,
    second_norm_bias,
    w_fc1,
    b_fc1,
    w_fc2,
    b_fc2,
    cotangent,
):
    images, seq, width = tokens.shape
    full = width * RING
    p = lax.axis_index("dp")
    slot = lax.axis_index("tensor") - p % 2
    live = (slot >= 0) & (slot < images)
    mask = jnp.where(live, pick(image_mask, jnp.clip(slot, 0, images - 1)), 0)
    mask = jnp.full((8, 128), mask.astype(jnp.float32))
    vectors = (ln1_gain, first_norm_bias, b_out, ln2_gain, second_norm_bias, b_fc2)
    ready = prepare(tokens, cotangent, vectors, w_attn, qv_bias, w_out, w_fc1, b_fc1, w_fc2)
    dy, small, *rest = forward(seq, *ready)
    fulls, kept = rest[:4], rest[4:12]
    block_out, input_grad, sums, s2, s1, so, sa = backward(
        seq, images, mask, small, *kept, dy, *ready[3:], *fulls
    )
    pairs = sums.reshape(12, width)
    grad_qv = pairs[6:8].reshape(2, 2, 4, 32).transpose(0, 2, 1, 3).reshape(2, width)
    return (
        block_out[:, :seq],
        input_grad[:, :seq],
        pairs[0],
        pairs[1],
        jnp.transpose(wide(sa).reshape(8, 3, 32, full), (3, 1, 0, 2)).reshape(full, 3, width),
        grad_qv,
        wide(so).reshape(width, full),
        pairs[2],
        pairs[3],
        pairs[4],
        jnp.transpose(wide(s1).reshape(-1, full)),
        pairs[8:].reshape(-1),
        wide(s2).reshape(-1, full),
        pairs[5],
    )


def solution(mesh):
    in_specs = (
        P("dp", None, "tensor"),
        P("dp"),
        P("tensor"),
        P("tensor"),
        P(None, None, "tensor"),
        P(None, "tensor"),
        P("tensor", None),
        P("tensor"),
        P("tensor"),
        P("tensor"),
        P(None, "tensor"),
        P("tensor"),
        P("tensor", None),
        P("tensor"),
        P("dp", None, "tensor"),
    )
    out_specs = (
        P("dp", None, "tensor"),
        P("dp", None, "tensor"),
        P("tensor"),
        P("tensor"),
        P(None, None, "tensor"),
        P(None, "tensor"),
        P("tensor", None),
        P("tensor"),
        P("tensor"),
        P("tensor"),
        P(None, "tensor"),
        P("tensor"),
        P("tensor", None),
        P("tensor"),
    )
    owners = mesh.shape["dp"] == 8 and mesh.shape["tensor"] == RING

    def block(*arrays):
        images = arrays[0].shape[0] // mesh.shape["dp"]
        body = image_local if owners and images < RING else local
        return jax.shard_map(
            body, mesh=mesh, in_specs=in_specs, out_specs=out_specs, check_vma=False
        )(*arrays)

    return block
```

```python
import functools

import jax
import jax.numpy as jnp
from jax import lax
from jax.experimental import pallas as pl
from jax.experimental.pallas import tpu as pltpu
from jax.sharding import PartitionSpec as P

MODEL_WIDTH = 1024
HD = 64


EPS = 1e-05


def norm_stats(value):
    total, squares = lax.psum((jnp.sum(value, 1), jnp.sum(value * value, 1)), "tensor")
    middle = total / MODEL_WIDTH
    spread = squares / MODEL_WIDTH - middle * middle
    return (middle[:, None], lax.rsqrt(spread + EPS)[:, None])


def layer_norm_reverse(incoming_gradient, normalized_input, norm_gain, inverse_deviation):
    gain_scaled_gradient = incoming_gradient * norm_gain
    first_norm_result, second_norm_result = lax.psum(
        (jnp.sum(gain_scaled_gradient, 1), jnp.sum(gain_scaled_gradient * normalized_input, 1)),
        "tensor",
    )
    return inverse_deviation * (
        gain_scaled_gradient
        - first_norm_result[:, None] / MODEL_WIDTH
        - normalized_input * second_norm_result[:, None] / MODEL_WIDTH
    )


def spread_features(value):
    return lax.all_gather(value, "tensor", axis=1, tiled=True)


def settle_sums(value):
    return lax.psum_scatter(value, "tensor", scatter_dimension=1, tiled=True)


def pair_dot(left, right):
    return lax.dot_general(
        left, right, (((0,), (0,)), ((), ())), preferred_element_type=jnp.float32
    )


def back_dot(left, right):
    return lax.dot_general(
        left, right, (((1,), (1,)), ((), ())), preferred_element_type=jnp.float32
    )


def attend_image(blocks):
    query, keys, values = blocks
    scale = HD ** (-0.5)
    scores = jnp.einsum("qhd,khd->hqk", query, keys, preferred_element_type=jnp.float32) * scale
    top = jnp.max(scores, -1, keepdims=True)
    expo = jnp.exp(scores - top)
    total = jnp.sum(expo, -1, keepdims=True)
    probs = expo / total
    log_total = top[..., 0] + jnp.log(total[..., 0])
    context = jnp.einsum(
        "hqk,khd->qhd", probs.astype(jnp.bfloat16), values, preferred_element_type=jnp.float32
    )
    return (context.astype(jnp.bfloat16), log_total)


def attend_back(blocks):
    query, keys, values, log_total, dcontext = blocks
    scale = HD ** (-0.5)
    scores = jnp.einsum("qhd,khd->hqk", query, keys, preferred_element_type=jnp.float32) * scale
    probs = jnp.exp(scores - log_total[..., None])
    dvalues = jnp.einsum(
        "hqk,qhd->khd", probs.astype(jnp.bfloat16), dcontext, preferred_element_type=jnp.float32
    )
    dprobs = jnp.einsum("qhd,khd->hqk", dcontext, values, preferred_element_type=jnp.float32)
    delta = jnp.sum(probs * dprobs, -1, keepdims=True)
    dscores = (probs * (dprobs - delta)).astype(jnp.bfloat16)
    dquery = jnp.einsum("hqk,khd->qhd", dscores, keys, preferred_element_type=jnp.float32) * scale
    dkeys = jnp.einsum("hqk,qhd->khd", dscores, query, preferred_element_type=jnp.float32) * scale
    return jnp.stack([dquery, dkeys, dvalues], 1).astype(jnp.bfloat16)


def local(
    tokens,
    image_mask,
    ln1_gain,
    first_norm_bias,
    w_attn,
    qv_bias,
    w_out,
    b_out,
    ln2_gain,
    second_norm_bias,
    w_fc1,
    b_fc1,
    w_fc2,
    b_fc2,
    cotangent,
):
    images, seq, width_dev = tokens.shape
    rows = images * seq
    heads_dev = width_dev // HD
    mask_rows = jnp.repeat(image_mask.astype(jnp.float32), seq)[:, None]
    first_norm_gain = ln1_gain.astype(jnp.float32)
    second_norm_gain = ln2_gain.astype(jnp.float32)
    block_inputs = tokens.astype(jnp.float32).reshape(rows, width_dev)
    first_midpoint_state, first_inverse_deviation = norm_stats(block_inputs)
    first_normalized_input = (block_inputs - first_midpoint_state) * first_inverse_deviation
    h1_full = spread_features(
        (first_normalized_input * first_norm_gain + first_norm_bias.astype(jnp.float32)).astype(
            jnp.bfloat16
        )
    )
    qkv = jnp.einsum("nd,dce->nce", h1_full, w_attn, preferred_element_type=jnp.float32)
    bias_rows = qv_bias.astype(jnp.float32)
    bias_full = jnp.stack([bias_rows[0], jnp.zeros_like(bias_rows[0]), bias_rows[1]], 0)
    qkv = (qkv + bias_full).astype(jnp.bfloat16)
    query = qkv[:, 0].reshape(images, seq, heads_dev, HD)
    keys = qkv[:, 1].reshape(images, seq, heads_dev, HD)
    values = qkv[:, 2].reshape(images, seq, heads_dev, HD)
    context, log_total = lax.map(attend_image, (query, keys, values))
    context_flat = context.reshape(rows, width_dev)
    attn = settle_sums(
        jnp.dot(context_flat, w_out, preferred_element_type=jnp.float32)
    ) + b_out.astype(jnp.float32)
    residual_stream_state = block_inputs + attn
    second_midpoint_state, second_inverse_deviation = norm_stats(residual_stream_state)
    second_normalized_input = (
        residual_stream_state - second_midpoint_state
    ) * second_inverse_deviation
    h2_full = spread_features(
        (second_normalized_input * second_norm_gain + second_norm_bias.astype(jnp.float32)).astype(
            jnp.bfloat16
        )
    )
    hidden = jnp.dot(h2_full, w_fc1, preferred_element_type=jnp.float32) + b_fc1.astype(jnp.float32)
    sigma = jax.nn.sigmoid(1.702 * hidden)
    act = (hidden * sigma).astype(jnp.bfloat16)
    mlp = settle_sums(jnp.dot(act, w_fc2, preferred_element_type=jnp.float32)) + b_fc2.astype(
        jnp.float32
    )
    block_out = (
        ((residual_stream_state + mlp) * mask_rows)
        .astype(jnp.bfloat16)
        .reshape(images, seq, width_dev)
    )
    output_gradient = cotangent.astype(jnp.float32).reshape(rows, width_dev) * mask_rows
    dy_full = spread_features(output_gradient.astype(jnp.bfloat16))
    grad_b_fc2 = jnp.sum(output_gradient, 0)
    grad_w_fc2 = pair_dot(act, dy_full)
    dact = back_dot(dy_full, w_fc2)
    dhidden = (dact * (sigma + 1.702 * hidden * sigma * (1.0 - sigma))).astype(jnp.bfloat16)
    grad_b_fc1 = jnp.sum(dhidden, 0, dtype=jnp.float32)
    grad_w_fc1 = pair_dot(h2_full, dhidden)
    second_hidden_gradient = settle_sums(back_dot(dhidden, w_fc1))
    second_norm_gain_gradient = jnp.sum(second_hidden_gradient * second_normalized_input, 0)
    grad_ln2_bias = jnp.sum(second_hidden_gradient, 0)
    residual_gradient = output_gradient + layer_norm_reverse(
        second_hidden_gradient, second_normalized_input, second_norm_gain, second_inverse_deviation
    )
    dattn = residual_gradient.astype(jnp.bfloat16)
    grad_b_out = jnp.sum(dattn, 0, dtype=jnp.float32)
    dattn_full = spread_features(dattn)
    grad_w_out = pair_dot(context_flat, dattn_full)
    dcontext = back_dot(dattn_full, w_out).astype(jnp.bfloat16).reshape(images, seq, heads_dev, HD)
    dqkv = lax.map(attend_back, (query, keys, values, log_total, dcontext))
    dqkv = dqkv.reshape(rows, 3, width_dev)
    grad_w_attn = jnp.einsum("nd,nce->dce", h1_full, dqkv, preferred_element_type=jnp.float32)
    bias_sums = jnp.sum(dqkv, 0, dtype=jnp.float32)
    grad_qv_bias = jnp.stack([bias_sums[0], bias_sums[2]], 0)
    first_hidden_gradient = settle_sums(
        jnp.einsum("nce,dce->nd", dqkv, w_attn, preferred_element_type=jnp.float32)
    )
    first_norm_gain_gradient = jnp.sum(first_hidden_gradient * first_normalized_input, 0)
    grad_ln1_bias = jnp.sum(first_hidden_gradient, 0)
    input_grad = (
        (
            residual_gradient
            + layer_norm_reverse(
                first_hidden_gradient,
                first_normalized_input,
                first_norm_gain,
                first_inverse_deviation,
            )
        )
        .astype(jnp.bfloat16)
        .reshape(images, seq, width_dev)
    )
    (
        first_norm_gain_gradient,
        grad_ln1_bias,
        grad_w_attn,
        grad_qv_bias,
        grad_w_out,
        grad_b_out,
        second_norm_gain_gradient,
        grad_ln2_bias,
        grad_w_fc1,
        grad_b_fc1,
        grad_w_fc2,
        grad_b_fc2,
    ) = lax.psum(
        (
            first_norm_gain_gradient,
            grad_ln1_bias,
            grad_w_attn,
            grad_qv_bias,
            grad_w_out,
            grad_b_out,
            second_norm_gain_gradient,
            grad_ln2_bias,
            grad_w_fc1,
            grad_b_fc1,
            grad_w_fc2,
            grad_b_fc2,
        ),
        "dp",
    )
    return (
        block_out,
        input_grad,
        first_norm_gain_gradient,
        grad_ln1_bias,
        grad_w_attn,
        grad_qv_bias,
        grad_w_out,
        grad_b_out,
        second_norm_gain_gradient,
        grad_ln2_bias,
        grad_w_fc1,
        grad_b_fc1,
        grad_w_fc2,
        grad_b_fc2,
    )


RING = 4


MESH_ID = pl.DeviceIdType.MESH
ROWS = 640
TILE = 512


def low(value):
    return value.astype(jnp.bfloat16)


def wide(value):
    return value.astype(jnp.float32)


def dot_on(left, right, a, b):
    return lax.dot_general(
        left, right, (((a,), (b,)), ((), ())), preferred_element_type=jnp.float32
    )


def turned(p, q):
    return sum(lax.rem(p // bit + q // bit, 2) * bit for bit in (1, 2, 4))


def remote(src, dst, send, recv, target):
    return pltpu.make_async_remote_copy(
        src_ref=src,
        dst_ref=dst,
        send_sem=send,
        recv_sem=recv,
        device_id=target,
        device_id_type=MESH_ID,
    )


def rows_at(start, size):
    return pl.ds(pl.multiple_of(start, 16), size)


class Place:
    def __init__(self, images):
        self.p = lax.axis_index("dp")
        self.z = lax.axis_index("tensor")
        self.core = lax.rem(self.p, 2)
        self.images = images
        self.shifts = [lax.rem(self.z + d, RING) for d in range(RING)]
        self.slot = self.z - self.core
        self.live = self.holds(self.z)

    def holds(self, plane):
        return (plane - self.core >= 0) & (plane - self.core < self.images)

    def near(self, q):
        return (turned(self.p, q), self.z)

    def greet(self):
        barrier = pltpu.get_barrier_semaphore()
        for d in range(1, RING):
            pl.semaphore_signal(
                barrier, inc=1, device_id=(self.p, self.shifts[d]), device_id_type=MESH_ID
            )
        for q in (1, 2, 4, 6):
            pl.semaphore_signal(barrier, inc=1, device_id=self.near(q), device_id_type=MESH_ID)
        pl.semaphore_wait(barrier, 7)


def weight_copies(place, pieces, full, chunk, target, sem, c=0, q=0):
    if chunk >= 2:
        yield pltpu.make_async_copy(
            pieces.at[turned(place.p, q)], target.at[pl.ds(0, 128)], sem
        )
        yield pltpu.make_async_copy(full.at[q], target.at[pl.ds(128, 384)], sem)
        return
    for half in range(2):
        source = full.at[c, half] if chunk == 0 else full.at[half]
        yield pltpu.make_async_copy(source, target.at[pl.ds(half * TILE + 128, 384)], sem)
        for head in range(4):
            own = pieces.at[turned(place.p, 2 * head + half)]
            if chunk == 0:
                own = own.at[c]
            yield pltpu.make_async_copy(own, target.at[pl.ds(half * TILE + head * 32, 32)], sem)


def pair_heads(one, two):
    lane = lax.broadcasted_iota(jnp.int32, (1, 128), 1)
    return (
        jnp.where(lane < 64, one, low(pltpu.roll(wide(two), 64, 1))),
        jnp.where(lane < 64, low(pltpu.roll(wide(one), 64, 1)), two),
    )


def head_mask(h):
    lane = lax.broadcasted_iota(jnp.int32, (1, 128), 1)
    return lax.rem(lane, 64) // 32 == h


def group_lanes(k):
    return [pl.ds(pl.multiple_of(k * 128 + half * TILE, 128), 128) for half in range(2)]


def split_heads(source, target, k):
    lanes = group_lanes(k)
    target[0], target[1] = pair_heads(source[:, lanes[0]], source[:, lanes[1]])


def join_heads(source, target, k):
    lanes = group_lanes(k)
    target[:, lanes[0]], target[:, lanes[1]] = pair_heads(source[0], source[1])


def turn_heads(sides, p):
    odd = lax.rem(p, 2) == 1
    sides = [jnp.where(odd, sides[1], sides[0]), jnp.where(odd, sides[0], sides[1])]
    lane = lax.broadcasted_iota(jnp.int32, (8, 128), 1)
    out = []
    for v in sides:
        near = jnp.where(lax.rem(lane // 32, 2) == 0, pltpu.roll(v, 96, 1), pltpu.roll(v, 32, 1))
        v = jnp.where(lax.rem(p // 2, 2) == 1, near, v)
        out.append(jnp.where(p // 4 == 1, pltpu.roll(v, 64, 1), v))
    return out


def feature(small_f, z, i):
    parts = [
        small_f[lax.rem(z + RING - j, RING), row : row + 1]
        for j in range(RING)
        for row in (2 * i, 2 * i + 1)
    ]
    return jnp.concatenate(parts, 1)


class Gather:
    def __init__(self, place, pieces, fulls, sems):
        self.at = place
        self.p, self.z = place.p, place.z
        self.pieces = pieces
        self.fulls = fulls
        self.z_send, self.send, self.recv = sems
        z = self.z
        self.order = (
            jnp.where(z == 0, 3, 1),
            jnp.where((z == 0) | (z == 3), 2, 3),
            jnp.where(z == 0, 1, jnp.where(z == 3, 3, 2)),
        )

    def place(self, chunk, q, k, start=0, size=None):
        full = self.fulls[chunk]
        size = self.pieces[chunk].shape[-2] if size is None else size
        start = (k - 1) * 128 + start
        if chunk >= 2:
            return full.at[q, rows_at(start, size)]
        at = rows_at(start + (q // 2) * 32, size)
        return full.at[:, q % 2, at] if chunk == 0 else full.at[q % 2, at]

    def part(self, chunk, q, k, side):
        half = self.pieces[chunk].shape[-2] // 2
        return self.place(chunk, q, k, side * half, half)

    def up(self, chunk, k, source):
        return remote(
            source,
            self.place(chunk, 0, k + 1),
            self.z_send.at[chunk, k, 0],
            self.recv.at[chunk, k + 1, 0],
            (self.p, jnp.minimum(self.z + 1, RING - 1)),
        )

    def down(self, chunk, k, source):
        return remote(
            source,
            self.place(chunk, 0, k - 1),
            self.z_send.at[chunk, lax.rem(k, RING), 1],
            self.recv.at[chunk, k - 1, 0],
            (self.p, jnp.maximum(self.z - 1, 0)),
        )

    def z_start(self, chunk):
        piece = self.pieces[chunk].at[self.p]
        pl.when(self.z < RING - 1)(self.up(chunk, 0, piece).start)
        pl.when(self.z > 0)(self.down(chunk, RING, piece).start)

    def z_sent(self, chunk):
        piece = self.pieces[chunk].at[self.p]
        pl.when(self.z < RING - 1)(self.up(chunk, 0, piece).wait_send)
        pl.when(self.z > 0)(self.down(chunk, RING, piece).wait_send)
        for k in (1, 2, 3):
            here = self.place(chunk, 0, k)
            if k < 3:
                pl.when((self.z >= k) & (self.z < RING - 1))(self.up(chunk, k, here).wait_send)
            if k > 1:
                pl.when((self.z < k) & (self.z > 0))(self.down(chunk, k, here).wait_send)

    def plane(self, chunk, k, source, target):
        return remote(
            self.place(chunk, source, k),
            self.place(chunk, target, k),
            self.send.at[chunk, k, target],
            self.recv.at[chunk, k, target],
            self.at.near(source ^ target),
        )

    def corner(self, chunk, k, side):
        source, flip = ((4, 2), (2, 4))[side]
        return remote(
            self.part(chunk, source, k, side),
            self.part(chunk, 6, k, side),
            self.send.at[chunk, k, (6, 8)[side]],
            self.recv.at[chunk, k, (6, 8)[side]],
            self.at.near(flip),
        )

    def spread(self, chunk, i):
        k = self.order[i]
        here = self.place(chunk, 0, k)
        remote(
            here, here, self.send.at[chunk, k, 0], self.recv.at[chunk, k, 0], self.at.near(1)
        ).wait_recv()
        pl.when((self.z >= k) & (self.z < RING - 1))(self.up(chunk, k, here).start)
        pl.when((self.z < k) & (self.z > 0))(self.down(chunk, k, here).start)
        for target in (2, 4, 1):
            self.plane(chunk, k, 0, target).start()

    def relay(self, chunk, i):
        k = self.order[i]
        self.plane(chunk, k, 0, 4).wait_recv()
        self.corner(chunk, k, 0).start()
        self.plane(chunk, k, 0, 2).wait_recv()
        self.corner(chunk, k, 1).start()
        self.plane(chunk, k, 4, 5).start()
        self.plane(chunk, k, 2, 3).start()

    def share(self, chunk, i):
        k = self.order[i]
        self.corner(chunk, k, 0).wait_recv()
        self.corner(chunk, k, 1).wait_recv()
        self.plane(chunk, k, 6, 7).start()

    def whole(self, chunk):
        for k in range(1, RING):
            for target in (1, 3, 5, 7):
                self.plane(chunk, k, target - 1, target).wait_recv()

    def sent(self, chunk):
        self.z_sent(chunk)
        for k in range(1, RING):
            for source, target in ((0, 2), (0, 4), (0, 1), (4, 5), (2, 3), (6, 7)):
                self.plane(chunk, k, source, target).wait_send()
            self.corner(chunk, k, 0).wait_send()
            self.corner(chunk, k, 1).wait_send()


class Rows:
    def __init__(self, place, source, target, send, recv, local):
        self.at = place
        self.source, self.target = source, target
        self.send, self.recv, self.local = send, recv, local
        self.width = source.shape[2]

    def columns(self):
        return pl.ds(pl.multiple_of(self.at.z * self.width, self.width), self.width)

    def copy(self, d):
        dest = self.at.shifts[d]
        return remote(
            self.source.at[jnp.clip(dest - self.at.core, 0, self.at.images - 1)],
            self.target.at[:, self.columns()],
            self.send.at[d],
            self.recv.at[d],
            (self.at.p, dest),
        )

    def own(self):
        return pltpu.make_async_copy(
            self.source.at[jnp.clip(self.at.slot, 0, self.at.images - 1)],
            self.target.at[:, self.columns()],
            self.local,
        )

    def start(self):
        self.own().start()
        for d in range(1, RING):
            pl.when(self.at.holds(self.at.shifts[d]))(self.copy(d).start)

    def here(self):
        self.own().wait()
        for d in range(1, RING):
            pl.when(self.at.live)(self.copy(d).wait_recv)

    def sent(self):
        for d in range(1, RING):
            pl.when(self.at.holds(self.at.shifts[d]))(self.copy(d).wait_send)


def norm_rows(value, gain, shift):
    middle = jnp.mean(value, 1, keepdims=True)
    spread = jnp.mean(value * value, 1, keepdims=True) - middle * middle
    return (value - middle) * lax.rsqrt(spread + EPS) * gain + shift


def forward_kernel(images, seq, *refs):
    (
        tokens,
        cotangent,
        small,
        attn_in,
        out_in,
        fc1_raw,
        fc2_in,
        dy_full,
        small_full,
        attn_full,
        out_full,
        fc1_full,
        fc2_full,
        x_rows_out,
        h1_out,
        qkv_out,
        ctx_out,
        r_out,
        h2_out,
        act_out,
        slope_out,
        fc1_in,
        x_full,
        x_in,
        x_v,
        h1_v,
        h2_v,
        qkv_v,
        ctx_v,
        r_v,
        w_v,
        act_v,
        slope_v,
        small_v,
        small_f,
        bias_v,
        pair_v,
        row_send,
        row_recv,
        small_send,
        small_recv,
        z_send,
        unit_send,
        unit_recv,
        local_sem,
        w_sem,
        tile_sem,
        out_sem,
    ) = refs
    at = Place(images)
    p, z = at.p, at.z
    g = Gather(
        at,
        (attn_in, out_in, fc1_in, fc2_in),
        (attn_full, out_full, fc1_full, fc2_full),
        (z_send, unit_send, unit_recv),
    )
    x_rows = Rows(at, tokens, x_full, row_send.at[0], row_recv.at[0], local_sem.at[0])
    dy_rows = Rows(at, cotangent, dy_full, row_send.at[1], row_recv.at[1], local_sem.at[1])
    full = x_full.shape[1]

    def small_copy(d):
        return remote(
            small, small_full.at[d], small_send.at[d], small_recv.at[d], (p, at.shifts[d])
        )

    small_own = pltpu.make_async_copy(small, small_full.at[0], local_sem.at[2])

    fc1_load = pltpu.make_async_copy(fc1_raw, w_v.at[0], local_sem.at[6])
    fc1_load.start()
    at.greet()
    g.z_start(0)
    for d in range(1, RING):
        small_copy(d).start()
    small_own.start()
    x_rows.start()

    g.z_start(1)
    fc1_load.wait()
    for i in range(8):
        rows = slice(i * 128, (i + 1) * 128)
        w_v[1, rows] = w_v[0, :, rows].T
        pltpu.make_async_copy(w_v.at[1, pl.ds(i * 128, 128)], fc1_in.at[i], local_sem.at[5]).start()
    g.spread(0, 0)
    g.spread(0, 1)
    g.spread(0, 2)
    pltpu.make_async_copy(w_v.at[1], w_v.at[1], local_sem.at[5]).wait()
    for d in range(1, RING):
        small_copy(d).wait()
    small_own.wait()
    small_load = pltpu.make_async_copy(small_full, small_v, local_sem.at[3])
    small_load.start()
    x_rows.here()
    x_load = pltpu.make_async_copy(x_full, x_in, local_sem.at[4])
    x_load.start()
    small_load.wait()

    small_f[...] = wide(small_v[...])
    gain, shift = feature(small_f, z, 0), feature(small_f, z, 1)
    for c, row in ((0, 12), (2, 14)):
        for k in range(RING):
            sides = [
                jnp.broadcast_to(small_f[k, row + half : row + half + 1], (8, 128))
                for half in range(2)
            ]
            for half, side in enumerate(turn_heads(sides, p)):
                start = half * TILE + k * 128
                bias_v[c : c + 1, start : start + 128] = side[0:1]
    bias_v[1:2] = jnp.zeros((1, full), jnp.float32)
    x_load.wait()

    def first_norm_of(block, value):
        value = jnp.where(at.live, wide(value), 0.0)
        x_v[block] = low(value)
        h1_v[block] = low(norm_rows(value, gain, shift))

    def first_norm(i, _):
        block = rows_at(i * 64, 64)
        first_norm_of(block, x_in[block])
        return 0

    whole_blocks = seq // 64 * 64
    lax.fori_loop(0, seq // 64, first_norm, 0)
    rest = wide(x_in[whole_blocks:seq])
    rest = jnp.concatenate([rest, jnp.zeros((ROWS - seq, full), jnp.float32)], 0)
    first_norm_of(slice(whole_blocks, ROWS), rest)
    saves = [
        pltpu.make_async_copy(x_v, x_rows_out, out_sem.at[0]),
        pltpu.make_async_copy(h1_v, h1_out, out_sem.at[1]),
    ]
    for s in saves:
        s.start()

    for i in range(3):
        g.relay(0, i)
        g.spread(1, i)
        if i == 1:
            g.z_start(2)
        if i:
            g.share(0, i - 1)
    g.share(0, 2)
    g.whole(0)

    def tile_load(chunk, c, slot):
        return list(
            weight_copies(
                at,
                (attn_in, out_in)[chunk],
                (attn_full, out_full)[chunk],
                chunk,
                w_v.at[slot],
                w_sem.at[slot],
                c,
            )
        )

    def go(copies):
        for copy in copies:
            copy.start()

    def arrive(copies):
        for copy in copies:
            copy.wait()

    def filled(slot):
        pltpu.make_async_copy(w_v.at[slot], w_v.at[slot], w_sem.at[slot]).wait()

    loads = [tile_load(0, c, c % 2) for c in range(3)] + [tile_load(1, 0, 1)]
    go(loads[0])
    go(loads[1])
    steps = [
        lambda: g.spread(2, 0),
        lambda: g.relay(1, 0),
        lambda: g.relay(1, 1),
    ]
    for c in range(3):
        filled(c % 2)

        def project(i, _, c=c):
            block = rows_at(i * TILE, TILE)
            out = dot_on(h1_v[...], w_v[c % 2, block], 1, 1)
            lanes = pl.ds(pl.multiple_of(i * TILE, TILE), TILE)
            qkv_v[c, :, lanes] = low(out + bias_v[c : c + 1, lanes])
            return 0

        lax.fori_loop(0, 2, project, 0)
        if c == 0:
            go(loads[2])
        steps[c]()
    save = pltpu.make_async_copy(qkv_v, qkv_out, out_sem.at[2])
    save.start()
    saves.append(save)

    key = lax.broadcasted_iota(jnp.int32, (ROWS, 1), 0)

    def attend(k, _):
        for c in range(3):
            split_heads(qkv_v.at[c], pair_v.at[c], k)
        for pair in range(2):
            keys, values = pair_v[1, pair], pair_v[2, pair]
            for r in range(ROWS // 128):
                block = slice(r * 128, (r + 1) * 128)
                query = pair_v[0, pair, block] * jnp.bfloat16(HD ** (-0.5))
                out = None
                for h in range(2):
                    mask = head_mask(h)
                    scores = dot_on(keys, jnp.where(mask, query, jnp.bfloat16(0)), 1, 1)
                    scores = jnp.where(key < seq, scores, -1e30)
                    expo = jnp.exp(scores - jnp.max(scores, 0, keepdims=True))
                    probs = low(expo * (1.0 / jnp.sum(expo, 0, keepdims=True)))
                    part = dot_on(probs, values, 0, 0)
                    out = part if out is None else jnp.where(mask, part, out)
                pair_v[0, pair, block] = low(out)
        join_heads(pair_v.at[0], ctx_v, k)
        for i in range(4):

            @pl.when(k == i)
            def _():
                for step in attention_steps[i]:
                    step()

        return 0

    attention_steps = [
        [lambda: g.spread(2, 1), lambda: g.z_start(3), lambda: g.relay(1, 2)],
        [lambda: g.spread(2, 2), lambda: g.share(1, 0), lambda: g.share(1, 1)],
        [lambda: g.share(1, 2), lambda: g.relay(2, 0), lambda: g.spread(3, 0)],
        [lambda: g.relay(2, 1), lambda: g.spread(3, 1), dy_rows.start],
    ]
    lax.fori_loop(0, 4, attend, 0)
    g.whole(1)
    go(loads[3])
    save = pltpu.make_async_copy(ctx_v, ctx_out, out_sem.at[3])
    save.start()
    saves.append(save)
    out_bias = feature(small_f, z, 2)
    gain2, shift2 = feature(small_f, z, 3), feature(small_f, z, 4)
    filled(1)
    for i in range(2):
        lanes = slice(i * TILE, (i + 1) * TILE)
        attn = dot_on(ctx_v[...], w_v[1, :, lanes], 1, 0)
        r_v[:, lanes] = wide(x_v[:, lanes]) + (attn + out_bias[:, lanes])
    save = pltpu.make_async_copy(r_v, r_out, out_sem.at[4])
    save.start()
    saves.append(save)
    g.relay(2, 2)
    g.spread(3, 2)
    g.share(2, 0)

    def second_norm(i, _):
        block = rows_at(i * 64, 64)
        h2_v[block] = low(norm_rows(r_v[block], gain2, shift2))
        return 0

    lax.fori_loop(0, ROWS // 64, second_norm, 0)
    save = pltpu.make_async_copy(h2_v, h2_out, out_sem.at[5])
    save.start()
    saves.append(save)
    g.share(2, 1)
    g.relay(3, 0)
    g.share(2, 2)
    g.whole(2)

    def pair_load(i):
        slot = i % 2
        for side in range(2):
            yield from weight_copies(
                at,
                fc1_in,
                fc1_full,
                2,
                w_v.at[slot, pl.ds(side * TILE, TILE)],
                w_sem.at[slot],
                q=2 * i + side,
            )

    def tile_saves(q):
        slot = q % 2
        return [
            pltpu.make_async_copy(act_v.at[slot], act_out.at[q], tile_sem.at[0, slot]),
            pltpu.make_async_copy(slope_v.at[slot], slope_out.at[q], tile_sem.at[1, slot]),
        ]

    pairs = [list(pair_load(i)) for i in range(4)]
    go(pairs[0])
    go(pairs[1])
    steps = [
        [lambda: g.relay(3, 1)],
        [lambda: g.relay(3, 2)],
        [lambda: g.share(3, 0), lambda: g.share(3, 1)],
        [lambda: g.share(3, 2)],
    ]
    for i in range(4):
        filled(i % 2)
        for side in range(2):
            q = 2 * i + side
            if q >= 2:
                arrive(tile_saves(q - 2))
            row = pl.ds(16 + turned(p, q), 1)
            bias = jnp.concatenate([small_f[k, row] for k in range(RING)], 1)
            for j in range(2):
                cols = slice(j * 256, (j + 1) * 256)
                start = side * TILE + j * 256
                u = dot_on(h2_v[...], w_v[i % 2, start : start + 256], 1, 1) + bias[:, cols]
                sg = 1.0 / (1.0 + jnp.exp(-1.702 * u))
                act_v[side, :, cols] = low(u * sg)
                slope_v[side, :, cols] = low(sg + 1.702 * u * sg * (1.0 - sg))
            go(tile_saves(q))
        if i < 2:
            go(pairs[i + 2])
        for step in steps[i]:
            step()
    for q in (6, 7):
        arrive(tile_saves(q))
    arrive(saves)
    g.whole(3)
    dy_rows.here()
    for chunk in range(4):
        g.sent(chunk)
    x_rows.sent()
    dy_rows.sent()


def forward(tokens, cotangent, small, attn_in, out_in, fc1_raw, fc2_in):
    images, rows, width = tokens.shape
    full = RING * width
    bf16 = jnp.bfloat16
    f32 = jnp.float32
    dma = pltpu.SemaphoreType.DMA
    shapes = (
        ((rows, full), bf16),
        ((RING,) + small.shape, bf16),
        ((3, 2, 384, full), bf16),
        ((2, 384, full), bf16),
        ((8, 384, full), bf16),
        ((8, 384, full), bf16),
        ((ROWS, full), bf16),
        ((ROWS, full), bf16),
        ((3, ROWS, full), bf16),
        ((ROWS, full), bf16),
        ((ROWS, full), f32),
        ((ROWS, full), bf16),
        ((8, ROWS, TILE), bf16),
        ((8, ROWS, TILE), bf16),
        (fc2_in.shape, bf16),
        ((rows, full), bf16),
    )
    return pl.pallas_call(
        functools.partial(forward_kernel, images, rows),
        out_shape=[jax.ShapeDtypeStruct(s, d) for s, d in shapes],
        in_specs=[pl.BlockSpec(memory_space=pl.ANY)] * 7,
        out_specs=[pl.BlockSpec(memory_space=pl.ANY)] * len(shapes),
        scratch_shapes=[
            pltpu.VMEM((rows, full), bf16),
            pltpu.VMEM((ROWS, full), bf16),
            pltpu.VMEM((ROWS, full), bf16),
            pltpu.VMEM((ROWS, full), bf16),
            pltpu.VMEM((3, ROWS, full), bf16),
            pltpu.VMEM((ROWS, full), bf16),
            pltpu.VMEM((ROWS, full), f32),
            pltpu.VMEM((2, 1024, full), bf16),
            pltpu.VMEM((2, ROWS, TILE), bf16),
            pltpu.VMEM((2, ROWS, TILE), bf16),
            pltpu.VMEM((RING,) + small.shape, bf16),
            pltpu.VMEM((RING,) + small.shape, f32),
            pltpu.VMEM((8, full), f32),
            pltpu.VMEM((3, 2, ROWS, 128), bf16),
            dma((2, RING)),
            dma((2, RING)),
            dma((RING,)),
            dma((RING,)),
            dma((4, RING, 2)),
            dma((4, RING, 9)),
            dma((4, RING, 9)),
            dma((7,)),
            dma((2,)),
            dma((2, 2)),
            dma((6,)),
        ],
        compiler_params=pltpu.CompilerParams(
            collective_id=0, has_side_effects=True, vmem_limit_bytes=56 * 2**20
        ),
    )(tokens, cotangent, small, attn_in, out_in, fc1_raw, fc2_in)


class Reduce:
    def __init__(self, place, sizes, outs, bufs, sems):
        self.at = place
        self.sizes = sizes
        self.starts = [sum(sizes[:i]) for i in range(4)]
        self.outs = outs
        self.held, self.first, self.second, self.far, self.total, self.stage = bufs
        self.core_send, self.core_recv, self.send, self.recv, self.local = sems[:5]
        self.plane_send, self.plane_recv = sems[5:]

    def rows(self, c):
        return pl.ds(self.starts[c], self.sizes[c])

    def give(self, group, xy, slot):
        y, x = xy // 2, lax.rem(xy, 2)
        at = self.rows(group)
        source = self.stage.at[slot]
        if group == 2:
            source = source.at[:, pl.ds(xy * 32, 32)]
        return remote(
            source,
            self.held.at[y, x, :, at],
            self.core_send.at[group, xy],
            self.core_recv.at[group, xy],
            self.at.near(1),
        )

    def hop(self, source, target, c, i, q):
        return remote(source, target, self.send.at[c, i], self.recv.at[c, i], self.at.near(q))

    def x_copy(self, c, y):
        at = self.rows(c)
        return self.hop(self.held.at[y, 1, 0:2, at], self.first.at[0, y, :, at], c, y, 2)

    def y_copy(self, c, x):
        at = self.rows(c)
        return self.hop(self.held.at[1, x, 2:4, at], self.first.at[1, x, :, at], c, 2 + x, 4)

    def xy_copy(self, c):
        at = self.rows(c)
        return self.hop(self.first.at[0, 1, :, at], self.second.at[0, :, at], c, 4, 4)

    def yx_copy(self, c):
        at = self.rows(c)
        return self.hop(self.first.at[1, 1, :, at], self.second.at[1, :, at], c, 5, 2)

    def z_copy(self, c, k):
        return remote(
            self.second.at[k // 2, k % 2, self.rows(c)],
            self.far.at[k - 1, self.rows(c)],
            self.send.at[c, 5 + k],
            self.recv.at[c, 5 + k],
            (self.at.p, self.at.shifts[RING - k]),
        )

    def out_copy(self, c, q):
        return self.hop(self.total.at[self.rows(c)], self.outs[c].at[self.at.p], c, {1: 9, 2: 10, 4: 11}[q], q)

    def out_here(self, c, q):
        block = self.outs[c].at[turned(self.at.p, q)]
        self.hop(self.total.at[self.rows(c)], block, c, {1: 9, 2: 10, 4: 11}[q], q).wait_recv()

    def corner(self, c, side):
        source, flip = ((4, 2), (2, 4))[side]
        half = self.sizes[c] // 2
        at = pl.ds(side * half, half)
        block = self.outs[c].at[turned(self.at.p, source), at]
        return self.hop(block, block, c, 14 + side, flip)

    def corner_here(self, c):
        half = self.sizes[c] // 2
        for side in range(2):
            block = self.outs[c].at[turned(self.at.p, 6), pl.ds(side * half, half)]
            self.hop(block, block, c, 14 + side, 2).wait_recv()

    def out_own(self, c):
        return pltpu.make_async_copy(
            self.total.at[self.rows(c)], self.outs[c].at[self.at.p], self.local.at[c]
        )

    def share(self, c, q):
        block = self.outs[c].at[turned(self.at.p, q)]
        return self.hop(block, block, c, 16 + q // 2, 1)

    def share_here(self, c, q):
        block = self.outs[c].at[turned(self.at.p, q)]
        theirs = self.outs[c].at[turned(self.at.p, q + 1)]
        self.hop(block, theirs, c, 16 + q // 2, 1).wait_recv()

    def add(self, dest, *sources):
        def body(i, _):
            at = rows_at(i * 16, 16)
            value = wide(sources[0][at])
            for s in sources[1:]:
                value = value + wide(s[at])
            dest[at] = low(value)
            return 0

        lax.fori_loop(0, dest.shape[0] // 16, body, 0)

    def turn(self, c):
        at = self.rows(c)
        self.x_copy(c, 1).wait_recv()
        for k in range(2):
            block = self.first.at[0, 1, k, at]
            self.add(block, block, self.held.at[1, 0, k, at])
        self.xy_copy(c).start()
        self.y_copy(c, 1).wait_recv()
        for k in range(2):
            block = self.first.at[1, 1, k, at]
            self.add(block, block, self.held.at[0, 1, 2 + k, at])
        self.yx_copy(c).start()

    def rise(self, c):
        at = self.rows(c)
        self.x_copy(c, 0).wait_recv()
        self.xy_copy(c).wait_recv()
        for k in range(2):
            block = self.second.at[0, k, at]
            self.add(block, block, self.first.at[0, 0, k, at], self.held.at[0, 0, k, at])
        self.z_copy(c, 1).start()
        self.y_copy(c, 0).wait_recv()
        self.yx_copy(c).wait_recv()
        for k in range(2):
            block = self.second.at[1, k, at]
            self.add(block, block, self.first.at[1, 0, k, at], self.held.at[0, 0, 2 + k, at])
            self.z_copy(c, 2 + k).start()

    def settle(self, c):
        at = self.rows(c)
        for k in range(1, RING):
            self.z_copy(c, k).wait_recv()
        self.add(
            self.total.at[at], self.second.at[0, 0, at], *(self.far.at[k, at] for k in range(3))
        )
        self.out_own(c).start()
        for q in (2, 4, 1):
            self.out_copy(c, q).start()

    def relay(self, c):
        self.out_here(c, 4)
        self.corner(c, 0).start()
        self.out_here(c, 2)
        self.corner(c, 1).start()
        for q in (2, 4):
            self.share(c, q).start()

    def last(self, c):
        self.corner_here(c)
        self.share(c, 6).start()

    def whole(self, c):
        self.out_own(c).wait()
        self.out_here(c, 1)
        for q in (2, 4, 6):
            self.share_here(c, q)

    def give_plane(self, k, slot, y):
        return remote(
            self.stage.at[slot, pl.ds(2 * y, 2), pl.ds(0, self.sizes[3])],
            self.held.at[y, :, k, self.rows(3)],
            self.core_send.at[3 + y, k],
            self.core_recv.at[3 + y, k],
            self.at.near(1),
        )

    def plane_hop(self, source, target, k, i, q):
        return remote(
            source, target, self.plane_send.at[k, i], self.plane_recv.at[k, i], self.at.near(q)
        )

    def plane_first(self, k):
        at, side = self.rows(3), k // 2
        source = self.held.at[:, 1, k, at] if side == 0 else self.held.at[1, :, k, at]
        return self.plane_hop(source, self.first.at[side, :, k % 2, at], k, 0, (2, 4)[side])

    def plane_second(self, k):
        at, side = self.rows(3), k // 2
        return self.plane_hop(
            self.first.at[side, 1, k % 2, at],
            self.second.at[side, k % 2, at],
            k,
            1,
            (4, 2)[side],
        )

    def plane_turn(self, k):
        at, side = self.rows(3), k // 2
        self.plane_first(k).wait_recv()
        block = self.first.at[side, 1, k % 2, at]
        own = self.held.at[1, 0, k, at] if side == 0 else self.held.at[0, 1, k, at]
        self.add(block, block, own)
        self.plane_second(k).start()

    def plane_rise(self, k):
        at, side = self.rows(3), k // 2
        self.plane_second(k).wait_recv()
        block = self.second.at[side, k % 2, at]
        self.add(block, block, self.first.at[side, 0, k % 2, at], self.held.at[0, 0, k, at])
        if k:
            self.z_copy(3, k).start()

    def finish(self, c):
        for q in (2, 4, 6):
            self.share(c, q).wait_send()
        if c < 3:
            for i in range(2):
                self.x_copy(c, i).wait_send()
                self.y_copy(c, i).wait_send()
            self.xy_copy(c).wait_send()
            self.yx_copy(c).wait_send()
        else:
            for k in range(RING):
                self.plane_first(k).wait_send()
                self.plane_second(k).wait_send()
        for k in range(1, RING):
            self.z_copy(c, k).wait_send()
        for q in (2, 4, 1):
            self.out_copy(c, q).wait_send()
        for side in range(2):
            self.corner(c, side).wait_send()


class Return:
    def __init__(self, place, source, target, send, recv):
        self.at = place
        self.source, self.target = source, target
        self.send, self.recv = send, recv
        self.width = target.shape[2]

    def pair(self, plane):
        columns = pl.ds(pl.multiple_of(plane * self.width, self.width), self.width)
        slot = jnp.clip(self.at.slot, 0, self.at.images - 1)
        return self.source.at[:, columns], self.target.at[slot]

    def copy(self, d):
        source, target = self.pair(self.at.shifts[d])
        return remote(
            source, target, self.send.at[d], self.recv.at[d], (self.at.p, self.at.shifts[d])
        )

    def own(self):
        return pltpu.make_async_copy(*self.pair(self.at.z), self.send.at[0])

    def start(self):
        pl.when(self.at.live)(self.own().start)
        for d in range(1, RING):
            pl.when(self.at.live)(self.copy(d).start)

    def sent(self):
        pl.when(self.at.live)(self.own().wait)
        for d in range(1, RING):
            pl.when(self.at.live)(self.copy(d).wait_send)

    def here(self):
        for d in range(1, RING):
            other = lax.rem(self.at.z + RING - d, RING)
            pl.when(self.at.holds(other))(self.copy(d).wait_recv)


def norm_parts(value):
    middle = jnp.mean(value, 1, keepdims=True)
    spread = jnp.mean(value * value, 1, keepdims=True) - middle * middle
    inverse = lax.rsqrt(spread + EPS)
    return (value - middle) * inverse, inverse


def norm_reverse(gradient, normalized, gain, inverse):
    scaled = gradient * gain
    first = jnp.mean(scaled, 1, keepdims=True)
    second = jnp.mean(scaled * normalized, 1, keepdims=True)
    return inverse * (scaled - first - normalized * second)


def backward_kernel(images, seq, sizes, *refs):
    (
        mask_in,
        small_full,
        x_in,
        h1_in,
        qkv_in,
        ctx_in,
        r_in,
        h2_in,
        act_in,
        slope_in,
        dy_in,
        attn_in,
        out_in,
        fc1_in,
        fc2_in,
        attn_full,
        out_full,
        fc1_full,
        fc2_full,
        block_out,
        grad_out,
        vector_out,
        s2,
        s1,
        so,
        sa,
        t1,
        ta,
        held,
        first,
        second,
        far,
        total,
        stage,
        w_v,
        dy_v,
        h_v,
        act_v,
        du_v,
        mlp_v,
        dh_v,
        r_v,
        da_v,
        ctx_v,
        dctx_v,
        qkv_v,
        p_v,
        ds_v,
        blk_v,
        sums_v,
        dus_v,
        small_v,
        small_f,
        vec,
        vec_far,
        core_send,
        core_recv,
        send,
        recv,
        row_send,
        row_recv,
        vec_send,
        vec_recv,
        local_sem,
        plane_send,
        plane_recv,
        load_sem,
        tile_sem,
        w_sem,
    ) = refs
    at = Place(images)
    p, z = at.p, at.z
    full = x_in.shape[1]
    quarter = full // RING
    done = seq // 32 * 32
    red = Reduce(
        at,
        sizes,
        (s2, s1, so, sa),
        (held, first, second, far, total, stage),
        (core_send, core_recv, send, recv, local_sem, plane_send, plane_recv),
    )
    blocks_back = Return(at, blk_v, block_out, row_send.at[0], row_recv.at[0])
    grads_back = Return(at, blk_v, grad_out, row_send.at[1], row_recv.at[1])

    def load(source, target, i):
        return pltpu.make_async_copy(source, target, load_sem.at[i])

    dy_load = load(dy_in, blk_v, 0)
    h2_load = load(h2_in, h_v, 1)
    r_load = load(r_in, r_v, 2)
    ctx_load = load(ctx_in, ctx_v, 3)
    qkv_load = load(qkv_in, qkv_v, 4)
    small_load = load(small_full, small_v, 5)
    h1_load = load(h1_in, h_v, 6)
    x_load = load(x_in, dy_v, 7)

    def tile_loads(q, slot):
        yield pltpu.make_async_copy(act_in.at[q], act_v.at[slot], tile_sem.at[0, slot])
        yield pltpu.make_async_copy(slope_in.at[q], du_v.at[slot], tile_sem.at[1, slot])
        for side, (pieces, whole) in enumerate(((fc1_in, fc1_full), (fc2_in, fc2_full))):
            yield from weight_copies(
                at, pieces, whole, 2, w_v.at[slot, pl.ds(side * TILE, TILE)], w_sem.at[slot], q=q
            )

    def matrix_loads(chunk, c, slot):
        pieces, whole = ((attn_in, attn_full), (out_in, out_full))[chunk]
        return weight_copies(at, pieces, whole, chunk, w_v.at[slot], w_sem.at[slot], c)

    def go(copies):
        for copy in copies:
            copy.start()

    def filled(slot):
        pltpu.make_async_copy(w_v.at[slot], w_v.at[slot], w_sem.at[slot]).wait()

    def turn_of(i):
        return jnp.where(i == 0, 3, jnp.where(i == 1, 1, jnp.where(i == 2, 2, 0)))

    dy_load.start()
    go(tile_loads(7, 0))
    h2_load.start()
    at.greet()
    go(tile_loads(6, 1))
    small_load.start()
    r_load.start()
    ctx_load.start()
    qkv_load.start()

    sums_v[...] = jnp.zeros_like(sums_v)
    mask = mask_in[jnp.clip(at.slot, 0, images - 1)].astype(jnp.float32)
    dy_load.wait()

    def masked(value):
        return jnp.where(at.live, wide(value), 0.0) * mask

    def mask_rows(i, _):
        block = rows_at(i * 32, 32)
        dy_v[block] = low(masked(blk_v[block]))
        return 0

    lax.fori_loop(0, done // 32, mask_rows, 0)
    rest = jnp.zeros((ROWS - seq, full), jnp.float32)
    dy_v[done:] = low(jnp.concatenate([masked(blk_v[done:seq]), rest], 0))
    h2_load.wait()

    def halves(body):
        lax.fori_loop(0, 2, lambda j, _: (body(pl.ds(pl.multiple_of(j * TILE, TILE), TILE)), 0)[1], 0)

    def keep(group, xy, left, right):
        y, x = xy // 2, lax.rem(xy, 2)
        red.give(group, xy, 0).wait_recv()
        at_rows = red.rows(group)

        def body(cols):
            grad = dot_on(left[...], right[:, cols], 0, 0)
            for k in range(RING):
                old = wide(held[y, x, k, at_rows, cols])
                held[y, x, k, at_rows, cols] = low(old + grad[k * 128 : (k + 1) * 128])

        halves(body)
        pl.when(x == 1)(red.x_copy(group, y).start)
        pl.when(y == 1)(red.y_copy(group, x).start)

    def stage_fill(slot, left, right):
        def body(cols):
            grad = low(dot_on(left[...], right[:, cols], 0, 0))
            for k in range(RING):
                stage[slot, k, :, cols] = grad[k * 128 : (k + 1) * 128]

        halves(body)

    mlp_v[...] = jnp.zeros_like(mlp_v)
    dh_v[...] = jnp.zeros_like(dh_v)

    def hidden_tile(i, core):
        slot = 1 - core
        xy = turn_of(i)
        q = 2 * xy + core
        pltpu.make_async_copy(act_in.at[q], act_v.at[slot], tile_sem.at[0, slot]).wait()
        if core:
            pl.when(i > 0)(red.give(0, turn_of(i - 1), 0).wait_send)
            stage_fill(0, act_v.at[slot], dy_v)
            red.give(0, xy, 0).start()
        else:
            keep(0, xy, act_v.at[slot], dy_v)
        pltpu.make_async_copy(slope_in.at[q], du_v.at[slot], tile_sem.at[1, slot]).wait()
        filled(slot)

        def slopes(j, _):
            cols = pl.ds(pl.multiple_of(j * 256, 256), 256)
            start = pl.ds(pl.multiple_of(TILE + j * 256, 256), 256)
            dact = dot_on(dy_v[...], w_v[slot, start], 1, 1)
            du = low(dact * wide(du_v[slot, :, cols]))
            du_v[slot, :, cols] = du
            dus_v[pl.ds(q, 1), cols] = jnp.sum(wide(du), 0, keepdims=True)
            return 0

        lax.fori_loop(0, 2, slopes, 0)
        if core:
            pl.when(i > 0)(red.give(1, turn_of(i - 1), 1).wait_send)
            stage_fill(1, du_v.at[slot], h_v)
            red.give(1, xy, 1).start()
        else:
            keep(1, xy, du_v.at[slot], h_v)

        def back(cols):
            mlp_v[:, cols] += dot_on(act_v[slot], w_v[slot, TILE:, cols], 1, 0)
            dh_v[:, cols] += dot_on(du_v[slot], w_v[slot, :TILE, cols], 1, 0)

        halves(back)

        @pl.when(i < 3)
        def _():
            go(tile_loads(2 * turn_of(i + 1) + core, slot))

    def hidden_tiles(i, _):
        hidden_tile(i, 1)
        hidden_tile(i, 0)
        return 0

    lax.fori_loop(0, 4, hidden_tiles, 0)
    go(matrix_loads(1, 0, 0))
    go(matrix_loads(0, 0, 1))
    h1_load.start()

    small_load.wait()

    small_f[...] = wide(small_v[...])
    gain1, gain2 = feature(small_f, z, 0), feature(small_f, z, 3)
    fc2_bias = feature(small_f, z, 5)
    r_load.wait()

    def collect(i, value):
        sums_v[i] = sums_v[i] + sum(value[r : r + 8] for r in range(0, value.shape[0], 8))

    def second_norm(block):
        r1 = r_v[block]
        dy = wide(dy_v[block])
        out = low((r1 + (mlp_v[block] + fc2_bias)) * mask)
        hat, inverse = norm_parts(r1)
        dh = dh_v[block]
        dr1 = dy + norm_reverse(dh, hat, gain2, inverse)
        da = low(dr1)
        r_v[block] = dr1
        da_v[block] = da
        collect(2, wide(da))
        collect(3, dh * hat)
        collect(4, dh)
        collect(5, dy)
        return out

    def by_blocks(norm):
        def body(i, _):
            block = rows_at(i * 32, 32)
            blk_v[block] = norm(block)
            return 0

        lax.fori_loop(0, done // 32, body, 0)
        out = norm(slice(done, done + 32))
        blk_v[done:seq] = out[: seq - done]

    by_blocks(second_norm)
    for ref in (r_v, da_v):
        ref[done + 32 :] = jnp.zeros((ROWS - done - 32, full), ref.dtype)
    blocks_back.start()
    x_load.start()
    ctx_load.wait()

    pending = [[red.give(0, 0, 0)], [red.give(1, 0, 1)]]

    def stage_free(slot):
        for copy in pending[slot]:
            copy.wait_send()
        pending[slot] = []

    def stage_go(slot, copies):
        go(copies)
        pending[slot] = copies

    far_half = pl.ds(TILE, TILE)
    near_half = pl.ds(0, TILE)
    stage_free(0)
    stage_fill(0, ctx_v.at[:, far_half], da_v)
    stage_go(0, [red.give(2, xy, 0) for xy in range(4)])
    filled(0)

    def dctx_half(rows):
        dctx_v[:, rows] = low(dot_on(da_v[...], w_v[0, rows], 1, 1))

    halves(dctx_half)

    def keep_heads(group, left, right):
        start = red.starts[group]
        for xy in range(4):
            red.give(group, xy, 0).wait_recv()
        def body(cols):
            grad = dot_on(left[...], right[:, cols], 0, 0)
            for xy in range(4):
                for k in range(RING):
                    rows = slice(start, start + 32)
                    at_row = k * 128 + xy * 32
                    old = wide(held[xy // 2, xy % 2, k, rows, cols])
                    held[xy // 2, xy % 2, k, rows, cols] = low(old + grad[at_row : at_row + 32])

        halves(body)

    def first_sends(c):
        red.x_copy(c, 1).start()
        red.y_copy(c, 1).start()
        red.x_copy(c, 0).start()
        red.y_copy(c, 0).start()

    keep_heads(2, ctx_v.at[:, near_half], da_v)
    first_sends(2)
    go(matrix_loads(0, 1, 0))
    qkv_load.wait()

    key = lax.broadcasted_iota(jnp.int32, (ROWS, 1), 0)
    scale = HD ** (-0.5)

    none = jnp.bfloat16(0)

    pairs, results = act_v, du_v

    def attend_back(k):
        for c in range(3):
            split_heads(qkv_v.at[c], pairs.at[:, :, pl.ds(c * 128, 128)], k)
        split_heads(dctx_v, pairs.at[:, :, pl.ds(384, 128)], k)

        def one_pair(pair, _):
            query = pairs[pair, :, :128] * jnp.bfloat16(scale)
            keys, values = pairs[pair, :, 128:256], pairs[pair, :, 256:384]
            dctx = pairs[pair, :, 384:]
            for h in range(2):
                mask = head_mask(h)
                for r in range(ROWS // 128):
                    cols = slice(r * 128, (r + 1) * 128)
                    scores = dot_on(keys, jnp.where(mask, query[cols], none), 1, 1)
                    scores = jnp.where(key < seq, scores, -1e30)
                    expo = jnp.exp(scores - jnp.max(scores, 0, keepdims=True))
                    probs = expo * (1.0 / jnp.sum(expo, 0, keepdims=True))
                    dprobs = dot_on(values, jnp.where(mask, dctx[cols], none), 1, 1)
                    delta = jnp.sum(probs * dprobs, 0, keepdims=True)
                    p_v[:, cols] = low(probs)
                    ds_v[:, cols] = low(probs * (dprobs - delta))
                dq = dot_on(ds_v[...], keys, 0, 0) * scale
                dk = dot_on(ds_v[...], query, 1, 0)
                dv = dot_on(p_v[...], dctx, 1, 0)
                for c, value in enumerate((dq, dk, dv)):
                    at_c = slice(c * 128, (c + 1) * 128)
                    if h == 0:
                        results[pair, :, at_c] = low(value)
                    else:
                        results[pair, :, at_c] = jnp.where(mask, low(value), results[pair, :, at_c])
            return 0

        lax.fori_loop(0, 2, one_pair, 0)
        for c in range(3):
            join_heads(results.at[:, :, pl.ds(c * 128, 128)], qkv_v.at[c], k)

    def plane_grad(half, k):
        start = pl.multiple_of(half * TILE + k * 128, 128)
        left = jnp.concatenate([qkv_v[c, :, pl.ds(start, 128)] for c in range(3)], 1)
        for j in range(2):
            cols = slice(j * TILE, (j + 1) * TILE)
            grad = dot_on(left, h_v[:, cols], 0, 0)
            for c in range(3):
                for xy in range(4):
                    at_row = c * 128 + xy * 32
                    yield xy // 2, xy % 2, c * 32, cols, grad[at_row : at_row + 32]

    steps = [
        [lambda: red.turn(0), lambda: red.turn(1)],
        [lambda: red.turn(2), lambda: red.rise(0)],
        [lambda: red.plane_turn(0), lambda: red.rise(1), lambda: red.rise(2)],
        [lambda: red.plane_rise(0), lambda: red.plane_turn(2), lambda: red.settle(0)],
    ]
    h1_load.wait()
    stage_free(0)
    stage_free(1)

    def attend_group(i, _):
        k = jnp.where(i == 0, 0, jnp.where(i == 1, 2, jnp.where(i == 2, 1, 3)))
        slot = lax.rem(i, 2)
        attend_back(k)

        @pl.when(i >= 2)
        def _():
            for y in range(2):
                red.give_plane(jnp.where(i == 2, 0, 2), slot, y).wait_send()

        for y, x, row, cols, grad in plane_grad(1, k):
            stage[slot, 2 * y + x, row : row + 32, cols] = low(grad)
        for y in range(2):
            red.give_plane(k, slot, y).start()
        for j in range(4):

            @pl.when(i == j)
            def _():
                for step in steps[j]:
                    step()

        for y in range(2):
            red.give_plane(k, slot, y).wait_recv()
        start = red.starts[3]
        for y, x, row, cols, grad in plane_grad(0, k):
            rows = slice(start + row, start + row + 32)
            held[y, x, k, rows, cols] = low(wide(held[y, x, k, rows, cols]) + grad)
        for j, plane in enumerate((0, 2, 1, 3)):
            pl.when(i == j)(red.plane_first(plane).start)
        return 0

    lax.fori_loop(0, 4, attend_group, 0)
    for i in range(3):
        if i == 2:
            go(matrix_loads(0, 2, 1))
        slot = (i + 1) % 2
        filled(slot)

        def spread_back(cols, c=i, slot=slot):
            value = dot_on(qkv_v[c], w_v[slot, :, cols], 1, 0)
            dh_v[:, cols] = value if c == 0 else value + dh_v[:, cols]

        halves(spread_back)
        if i == 0:
            red.plane_turn(1)
            red.relay(0)
        if i == 1:
            red.plane_turn(3)
            red.plane_rise(2)
    red.plane_rise(1)
    red.settle(1)
    x_load.wait()
    blocks_back.sent()

    def first_norm(block):
        hat, inverse = norm_parts(wide(dy_v[block]))
        dh = dh_v[block]
        collect(0, dh * hat)
        collect(1, dh)
        return low(r_v[block] + norm_reverse(dh, hat, gain1, inverse))

    by_blocks(first_norm)
    grads_back.start()

    for i in range(6):
        value = jnp.sum(sums_v[i], 0, keepdims=True)
        for j in range(RING):
            for side in range(2):
                start = j * quarter + side * 128
                vec[j, 2 * i + side : 2 * i + side + 1] = value[:, start : start + 128]
    for row, c in ((12, 0), (14, 2)):
        value = jnp.sum(wide(qkv_v[c]), 0, keepdims=True)
        for k in range(RING):
            starts = [half * TILE + k * 128 for half in range(2)]
            sides = [jnp.broadcast_to(value[:, i : i + 128], (8, 128)) for i in starts]
            for half, side in enumerate(turn_heads(sides, p)):
                vec[lax.rem(z + RING - k, RING), row + half : row + half + 1] = side[0:1]
    for q in range(8):
        for k in range(RING):
            at_row = pl.ds(16 + turned(p, q), 1)
            vec[lax.rem(z + RING - k, RING), at_row] = dus_v[q : q + 1, k * 128 : (k + 1) * 128]

    def vec_copy(i):
        return remote(vec, vec_far.at[i], vec_send.at[i], vec_recv.at[i], at.near((1, 2, 4)[i]))

    def vec_z(d):
        return remote(
            vec.at[at.shifts[d]],
            vec_far.at[3, d],
            vec_send.at[2 + d],
            vec_recv.at[2 + d],
            (p, at.shifts[d]),
        )

    def vec_step(i):
        vec_copy(i).wait()
        vec[...] = vec[...] + vec_far[i]

    vec_copy(0).start()
    red.plane_rise(3)
    red.settle(2)
    vec_step(0)
    vec_copy(1).start()
    red.last(0)
    red.relay(1)
    vec_step(1)
    vec_copy(2).start()
    red.relay(2)
    red.last(1)
    vec_step(2)
    for d in range(1, RING):
        vec_z(d).start()
    red.settle(3)
    red.last(2)
    red.whole(0)
    red.whole(1)

    for piece in range(8):
        load(s1.at[piece], w_v.at[0, pl.ds(piece * 128, 128)], 8).start()
    load(w_v.at[0], w_v.at[0], 8).wait()
    for piece in range(8):
        rows = slice(piece * 128, (piece + 1) * 128)
        w_v[1, :, rows] = w_v[0, rows].T
    rows_save = load(w_v.at[1], t1, 9)
    rows_save.start()
    for d in range(1, RING):
        vec_z(d).wait()
    vec[0] = vec[z] + (vec_far[3, 1] + (vec_far[3, 2] + vec_far[3, 3]))
    vec_out = pltpu.make_async_copy(vec.at[0], vector_out, local_sem.at[4])
    vec_out.start()
    red.relay(3)
    red.whole(2)
    for y in range(2):
        red.give_plane(1, 0, y).wait_send()
        red.give_plane(3, 1, y).wait_send()
    red.last(3)
    for c in range(3):
        red.finish(c)
    blocks_back.here()
    rows_save.wait()
    red.whole(3)

    def head_loads():
        for piece in range(8):
            for c in range(3):
                yield load(
                    sa.at[piece, pl.ds(c * 32, 32)], w_v.at[0, pl.ds(c * 256 + piece * 32, 32)], 10
                )

    go(head_loads())
    part = w_v.at[0, pl.ds(0, 768)]
    load(part, part, 10).wait()
    saves = []
    for c in range(3):
        rows = slice(c * 256, (c + 1) * 256)
        w_v[1, :, rows] = w_v[0, rows].T
        saves.append(load(w_v.at[1, :, pl.ds(c * 256, 256)], ta.at[c], 11 + c))
        saves[-1].start()
    for copy in saves:
        copy.wait()
    red.finish(3)
    vec_out.wait()
    grads_back.sent()
    grads_back.here()


def backward(mask, *arrays):
    images = mask.shape[0]
    seq, full = arrays[9].shape
    width = full // RING
    bf16 = jnp.bfloat16
    f32 = jnp.float32
    dma = pltpu.SemaphoreType.DMA
    attn_in, out_in, fc1_in, fc2_in = arrays[10:14]
    sizes = (fc2_in.shape[1], fc1_in.shape[1], out_in.shape[1], 3 * attn_in.shape[2])
    every = sum(sizes)
    outs = [jax.ShapeDtypeStruct((images, seq, width), bf16)] * 2
    outs.append(jax.ShapeDtypeStruct((24, 128), f32))
    outs += [jax.ShapeDtypeStruct((8, n, full), bf16) for n in sizes]
    outs.append(jax.ShapeDtypeStruct((full, 8 * sizes[1]), bf16))
    outs.append(jax.ShapeDtypeStruct((3, full, width), bf16))
    any_space = pl.BlockSpec(memory_space=pl.ANY)
    vm = pltpu.VMEM
    return pl.pallas_call(
        functools.partial(backward_kernel, images, seq, sizes),
        out_shape=outs,
        in_specs=[pl.BlockSpec(memory_space=pltpu.SMEM)] + [any_space] * len(arrays),
        out_specs=[any_space] * len(outs),
        scratch_shapes=[
            vm((2, 2, RING, every, full), bf16),
            vm((2, 2, 2, every, full), bf16),
            vm((2, 2, every, full), bf16),
            vm((3, every, full), bf16),
            vm((every, full), bf16),
            vm((2, RING, 128, full), bf16),
            vm((2, 1024, full), bf16),
            vm((ROWS, full), bf16),
            vm((ROWS, full), bf16),
            vm((2, ROWS, TILE), bf16),
            vm((2, ROWS, TILE), bf16),
            vm((ROWS, full), f32),
            vm((ROWS, full), f32),
            vm((ROWS, full), f32),
            vm((ROWS, full), bf16),
            vm((ROWS, full), bf16),
            vm((ROWS, full), bf16),
            vm((3, ROWS, full), bf16),
            vm((ROWS, ROWS), bf16),
            vm((ROWS, ROWS), bf16),
            vm((seq, full), bf16),
            vm((6, 8, full), f32),
            vm((8, TILE), f32),
            vm(arrays[0].shape, bf16),
            vm(arrays[0].shape, f32),
            vm((RING, 24, 128), f32),
            vm((4, RING, 24, 128), f32),
            dma((5, RING)),
            dma((5, RING)),
            dma((4, 20)),
            dma((4, 20)),
            dma((2, RING)),
            dma((2, RING)),
            dma((6,)),
            dma((6,)),
            dma((5,)),
            dma((RING, 2)),
            dma((RING, 2)),
            dma((14,)),
            dma((2, 2)),
            dma((2,)),
        ],
        compiler_params=pltpu.CompilerParams(
            collective_id=1, has_side_effects=True, vmem_limit_bytes=60 * 2**20
        ),
    )(mask, *arrays)


def prepare(vectors, w_attn, qv_bias, w_out, b_fc1, w_fc2):
    full, _, width = w_attn.shape
    attn = jnp.transpose(w_attn, (1, 2, 0)).reshape(3, 8, 32, full).transpose(1, 0, 2, 3)
    qv = qv_bias.reshape(2, 4, 2, 32).transpose(0, 2, 1, 3).reshape(-1)
    start, small = 0, 0
    for v in (*vectors, qv, b_fc1):
        small = small + jnp.pad(v, (start, 4096 - start - v.shape[0]))
        start += v.shape[0]
    return small.reshape(-1, 128), attn, w_out.reshape(8, 32, full), w_fc2.reshape(8, -1, full)


def image_local(
    tokens,
    image_mask,
    ln1_gain,
    first_norm_bias,
    w_attn,
    qv_bias,
    w_out,
    b_out,
    ln2_gain,
    second_norm_bias,
    w_fc1,
    b_fc1,
    w_fc2,
    b_fc2,
    cotangent,
):
    width = tokens.shape[2]
    full = width * RING
    vectors = (ln1_gain, first_norm_bias, b_out, ln2_gain, second_norm_bias, b_fc2)
    small, attn, out, fc2 = prepare(vectors, w_attn, qv_bias, w_out, b_fc1, w_fc2)
    dy, small, *rest = forward(tokens, cotangent, small, attn, out, w_fc1, fc2)
    fulls, kept, fc1 = rest[:4], rest[4:12], rest[12]
    block_out, input_grad, sums, s2, _, so, _, t1, ta = backward(
        image_mask, small, *kept, dy, attn, out, fc1, fc2, *fulls
    )
    pairs = sums.reshape(12, width)
    grad_qv = pairs[6:8].reshape(2, 2, 4, 32).transpose(0, 2, 1, 3).reshape(2, width)
    return (
        block_out,
        input_grad,
        pairs[0],
        pairs[1],
        jnp.transpose(wide(ta), (1, 0, 2)),
        grad_qv,
        wide(so).reshape(width, full),
        pairs[2],
        pairs[3],
        pairs[4],
        wide(t1),
        pairs[8:].reshape(-1),
        wide(s2).reshape(-1, full),
        pairs[5],
    )


def solution(mesh):
    in_specs = (
        P("dp", None, "tensor"),
        P("dp"),
        P("tensor"),
        P("tensor"),
        P(None, None, "tensor"),
        P(None, "tensor"),
        P("tensor", None),
        P("tensor"),
        P("tensor"),
        P("tensor"),
        P(None, "tensor"),
        P("tensor"),
        P("tensor", None),
        P("tensor"),
        P("dp", None, "tensor"),
    )
    out_specs = (
        P("dp", None, "tensor"),
        P("dp", None, "tensor"),
        P("tensor"),
        P("tensor"),
        P(None, None, "tensor"),
        P(None, "tensor"),
        P("tensor", None),
        P("tensor"),
        P("tensor"),
        P("tensor"),
        P(None, "tensor"),
        P("tensor"),
        P("tensor", None),
        P("tensor"),
    )
    owners = mesh.shape["dp"] == 8 and mesh.shape["tensor"] == RING

    def block(*arrays):
        images = arrays[0].shape[0] // mesh.shape["dp"]
        body = image_local if owners and images < RING else local
        return jax.shard_map(
            body, mesh=mesh, in_specs=in_specs, out_specs=out_specs, check_vma=False
        )(*arrays)

    return block
```

```python
import functools

import jax
import jax.numpy as jnp
from jax import lax
from jax.experimental import pallas as pl
from jax.experimental.pallas import tpu as pltpu
from jax.sharding import PartitionSpec as P

MODEL_WIDTH = 1024
HD = 64


EPS = 1e-05


def norm_stats(value):
    total, squares = lax.psum((jnp.sum(value, 1), jnp.sum(value * value, 1)), "tensor")
    middle = total / MODEL_WIDTH
    spread = squares / MODEL_WIDTH - middle * middle
    return (middle[:, None], lax.rsqrt(spread + EPS)[:, None])


def layer_norm_reverse(incoming_gradient, normalized_input, norm_gain, inverse_deviation):
    gain_scaled_gradient = incoming_gradient * norm_gain
    first_norm_result, second_norm_result = lax.psum(
        (jnp.sum(gain_scaled_gradient, 1), jnp.sum(gain_scaled_gradient * normalized_input, 1)),
        "tensor",
    )
    return inverse_deviation * (
        gain_scaled_gradient
        - first_norm_result[:, None] / MODEL_WIDTH
        - normalized_input * second_norm_result[:, None] / MODEL_WIDTH
    )


def spread_features(value):
    return lax.all_gather(value, "tensor", axis=1, tiled=True)


def settle_sums(value):
    return lax.psum_scatter(value, "tensor", scatter_dimension=1, tiled=True)


def pair_dot(left, right):
    return lax.dot_general(
        left, right, (((0,), (0,)), ((), ())), preferred_element_type=jnp.float32
    )


def back_dot(left, right):
    return lax.dot_general(
        left, right, (((1,), (1,)), ((), ())), preferred_element_type=jnp.float32
    )


def attend_image(blocks):
    query, keys, values = blocks
    scale = HD ** (-0.5)
    scores = jnp.einsum("qhd,khd->hqk", query, keys, preferred_element_type=jnp.float32) * scale
    top = jnp.max(scores, -1, keepdims=True)
    expo = jnp.exp(scores - top)
    total = jnp.sum(expo, -1, keepdims=True)
    probs = expo / total
    log_total = top[..., 0] + jnp.log(total[..., 0])
    context = jnp.einsum(
        "hqk,khd->qhd", probs.astype(jnp.bfloat16), values, preferred_element_type=jnp.float32
    )
    return (context.astype(jnp.bfloat16), log_total)


def attend_back(blocks):
    query, keys, values, log_total, dcontext = blocks
    scale = HD ** (-0.5)
    scores = jnp.einsum("qhd,khd->hqk", query, keys, preferred_element_type=jnp.float32) * scale
    probs = jnp.exp(scores - log_total[..., None])
    dvalues = jnp.einsum(
        "hqk,qhd->khd", probs.astype(jnp.bfloat16), dcontext, preferred_element_type=jnp.float32
    )
    dprobs = jnp.einsum("qhd,khd->hqk", dcontext, values, preferred_element_type=jnp.float32)
    delta = jnp.sum(probs * dprobs, -1, keepdims=True)
    dscores = (probs * (dprobs - delta)).astype(jnp.bfloat16)
    dquery = jnp.einsum("hqk,khd->qhd", dscores, keys, preferred_element_type=jnp.float32) * scale
    dkeys = jnp.einsum("hqk,qhd->khd", dscores, query, preferred_element_type=jnp.float32) * scale
    return jnp.stack([dquery, dkeys, dvalues], 1).astype(jnp.bfloat16)


def local(
    tokens,
    image_mask,
    ln1_gain,
    first_norm_bias,
    w_attn,
    qv_bias,
    w_out,
    b_out,
    ln2_gain,
    second_norm_bias,
    w_fc1,
    b_fc1,
    w_fc2,
    b_fc2,
    cotangent,
):
    images, seq, width_dev = tokens.shape
    rows = images * seq
    heads_dev = width_dev // HD
    mask_rows = jnp.repeat(image_mask.astype(jnp.float32), seq)[:, None]
    first_norm_gain = ln1_gain.astype(jnp.float32)
    second_norm_gain = ln2_gain.astype(jnp.float32)
    block_inputs = tokens.astype(jnp.float32).reshape(rows, width_dev)
    first_midpoint_state, first_inverse_deviation = norm_stats(block_inputs)
    first_normalized_input = (block_inputs - first_midpoint_state) * first_inverse_deviation
    h1_full = spread_features(
        (first_normalized_input * first_norm_gain + first_norm_bias.astype(jnp.float32)).astype(
            jnp.bfloat16
        )
    )
    qkv = jnp.einsum("nd,dce->nce", h1_full, w_attn, preferred_element_type=jnp.float32)
    bias_rows = qv_bias.astype(jnp.float32)
    bias_full = jnp.stack([bias_rows[0], jnp.zeros_like(bias_rows[0]), bias_rows[1]], 0)
    qkv = (qkv + bias_full).astype(jnp.bfloat16)
    query = qkv[:, 0].reshape(images, seq, heads_dev, HD)
    keys = qkv[:, 1].reshape(images, seq, heads_dev, HD)
    values = qkv[:, 2].reshape(images, seq, heads_dev, HD)
    context, log_total = lax.map(attend_image, (query, keys, values))
    context_flat = context.reshape(rows, width_dev)
    attn = settle_sums(
        jnp.dot(context_flat, w_out, preferred_element_type=jnp.float32)
    ) + b_out.astype(jnp.float32)
    residual_stream_state = block_inputs + attn
    second_midpoint_state, second_inverse_deviation = norm_stats(residual_stream_state)
    second_normalized_input = (
        residual_stream_state - second_midpoint_state
    ) * second_inverse_deviation
    h2_full = spread_features(
        (second_normalized_input * second_norm_gain + second_norm_bias.astype(jnp.float32)).astype(
            jnp.bfloat16
        )
    )
    hidden = jnp.dot(h2_full, w_fc1, preferred_element_type=jnp.float32) + b_fc1.astype(jnp.float32)
    sigma = jax.nn.sigmoid(1.702 * hidden)
    act = (hidden * sigma).astype(jnp.bfloat16)
    mlp = settle_sums(jnp.dot(act, w_fc2, preferred_element_type=jnp.float32)) + b_fc2.astype(
        jnp.float32
    )
    block_out = (
        ((residual_stream_state + mlp) * mask_rows)
        .astype(jnp.bfloat16)
        .reshape(images, seq, width_dev)
    )
    output_gradient = cotangent.astype(jnp.float32).reshape(rows, width_dev) * mask_rows
    dy_full = spread_features(output_gradient.astype(jnp.bfloat16))
    grad_b_fc2 = jnp.sum(output_gradient, 0)
    grad_w_fc2 = pair_dot(act, dy_full)
    dact = back_dot(dy_full, w_fc2)
    dhidden = (dact * (sigma + 1.702 * hidden * sigma * (1.0 - sigma))).astype(jnp.bfloat16)
    grad_b_fc1 = jnp.sum(dhidden, 0, dtype=jnp.float32)
    grad_w_fc1 = pair_dot(h2_full, dhidden)
    second_hidden_gradient = settle_sums(back_dot(dhidden, w_fc1))
    second_norm_gain_gradient = jnp.sum(second_hidden_gradient * second_normalized_input, 0)
    grad_ln2_bias = jnp.sum(second_hidden_gradient, 0)
    residual_gradient = output_gradient + layer_norm_reverse(
        second_hidden_gradient, second_normalized_input, second_norm_gain, second_inverse_deviation
    )
    dattn = residual_gradient.astype(jnp.bfloat16)
    grad_b_out = jnp.sum(dattn, 0, dtype=jnp.float32)
    dattn_full = spread_features(dattn)
    grad_w_out = pair_dot(context_flat, dattn_full)
    dcontext = back_dot(dattn_full, w_out).astype(jnp.bfloat16).reshape(images, seq, heads_dev, HD)
    dqkv = lax.map(attend_back, (query, keys, values, log_total, dcontext))
    dqkv = dqkv.reshape(rows, 3, width_dev)
    grad_w_attn = jnp.einsum("nd,nce->dce", h1_full, dqkv, preferred_element_type=jnp.float32)
    bias_sums = jnp.sum(dqkv, 0, dtype=jnp.float32)
    grad_qv_bias = jnp.stack([bias_sums[0], bias_sums[2]], 0)
    first_hidden_gradient = settle_sums(
        jnp.einsum("nce,dce->nd", dqkv, w_attn, preferred_element_type=jnp.float32)
    )
    first_norm_gain_gradient = jnp.sum(first_hidden_gradient * first_normalized_input, 0)
    grad_ln1_bias = jnp.sum(first_hidden_gradient, 0)
    input_grad = (
        (
            residual_gradient
            + layer_norm_reverse(
                first_hidden_gradient,
                first_normalized_input,
                first_norm_gain,
                first_inverse_deviation,
            )
        )
        .astype(jnp.bfloat16)
        .reshape(images, seq, width_dev)
    )
    (
        first_norm_gain_gradient,
        grad_ln1_bias,
        grad_w_attn,
        grad_qv_bias,
        grad_w_out,
        grad_b_out,
        second_norm_gain_gradient,
        grad_ln2_bias,
        grad_w_fc1,
        grad_b_fc1,
        grad_w_fc2,
        grad_b_fc2,
    ) = lax.psum(
        (
            first_norm_gain_gradient,
            grad_ln1_bias,
            grad_w_attn,
            grad_qv_bias,
            grad_w_out,
            grad_b_out,
            second_norm_gain_gradient,
            grad_ln2_bias,
            grad_w_fc1,
            grad_b_fc1,
            grad_w_fc2,
            grad_b_fc2,
        ),
        "dp",
    )
    return (
        block_out,
        input_grad,
        first_norm_gain_gradient,
        grad_ln1_bias,
        grad_w_attn,
        grad_qv_bias,
        grad_w_out,
        grad_b_out,
        second_norm_gain_gradient,
        grad_ln2_bias,
        grad_w_fc1,
        grad_b_fc1,
        grad_w_fc2,
        grad_b_fc2,
    )


RING = 4


MESH_ID = pl.DeviceIdType.MESH
ROWS = 640
TILE = 512


def low(value):
    return value.astype(jnp.bfloat16)


def wide(value):
    return value.astype(jnp.float32)


def dot_on(left, right, a, b):
    return lax.dot_general(
        left, right, (((a,), (b,)), ((), ())), preferred_element_type=jnp.float32
    )


def turned(p, q):
    return sum(lax.rem(p // bit + q // bit, 2) * bit for bit in (1, 2, 4))


def remote(src, dst, send, recv, target):
    return pltpu.make_async_remote_copy(
        src_ref=src,
        dst_ref=dst,
        send_sem=send,
        recv_sem=recv,
        device_id=target,
        device_id_type=MESH_ID,
    )


def rows_at(start, size):
    return pl.ds(pl.multiple_of(start, 16), size)


class Place:
    def __init__(self, images):
        self.p = lax.axis_index("dp")
        self.z = lax.axis_index("tensor")
        self.core = lax.rem(self.p, 2)
        self.images = images
        self.shifts = [lax.rem(self.z + d, RING) for d in range(RING)]
        self.slot = self.z - self.core
        self.live = self.holds(self.z)

    def holds(self, plane):
        return (plane - self.core >= 0) & (plane - self.core < self.images)

    def near(self, q):
        return (turned(self.p, q), self.z)

    def greet(self):
        barrier = pltpu.get_barrier_semaphore()
        for d in range(1, RING):
            pl.semaphore_signal(
                barrier, inc=1, device_id=(self.p, self.shifts[d]), device_id_type=MESH_ID
            )
        for q in (1, 2, 4, 6):
            pl.semaphore_signal(barrier, inc=1, device_id=self.near(q), device_id_type=MESH_ID)
        pl.semaphore_wait(barrier, 7)


def weight_copies(place, pieces, full, chunk, target, sem, c=0, q=0):
    if chunk >= 2:
        yield pltpu.make_async_copy(
            pieces.at[turned(place.p, q)], target.at[pl.ds(0, 128)], sem
        )
        yield pltpu.make_async_copy(full.at[q], target.at[pl.ds(128, 384)], sem)
        return
    for half in range(2):
        source = full.at[c, half] if chunk == 0 else full.at[half]
        yield pltpu.make_async_copy(source, target.at[pl.ds(half * TILE + 128, 384)], sem)
        for head in range(4):
            own = pieces.at[turned(place.p, 2 * head + half)]
            if chunk == 0:
                own = own.at[c]
            yield pltpu.make_async_copy(own, target.at[pl.ds(half * TILE + head * 32, 32)], sem)


def pair_heads(one, two):
    lane = lax.broadcasted_iota(jnp.int32, (1, 128), 1)
    return (
        jnp.where(lane < 64, one, low(pltpu.roll(wide(two), 64, 1))),
        jnp.where(lane < 64, low(pltpu.roll(wide(one), 64, 1)), two),
    )


def head_mask(h):
    lane = lax.broadcasted_iota(jnp.int32, (1, 128), 1)
    return lax.rem(lane, 64) // 32 == h


def group_lanes(k):
    return [pl.ds(pl.multiple_of(k * 128 + half * TILE, 128), 128) for half in range(2)]


def split_heads(source, target, k):
    lanes = group_lanes(k)
    target[0], target[1] = pair_heads(source[:, lanes[0]], source[:, lanes[1]])


def join_heads(source, target, k):
    lanes = group_lanes(k)
    target[:, lanes[0]], target[:, lanes[1]] = pair_heads(source[0], source[1])


def turn_heads(sides, p):
    odd = lax.rem(p, 2) == 1
    sides = [jnp.where(odd, sides[1], sides[0]), jnp.where(odd, sides[0], sides[1])]
    lane = lax.broadcasted_iota(jnp.int32, (8, 128), 1)
    out = []
    for v in sides:
        near = jnp.where(lax.rem(lane // 32, 2) == 0, pltpu.roll(v, 96, 1), pltpu.roll(v, 32, 1))
        v = jnp.where(lax.rem(p // 2, 2) == 1, near, v)
        out.append(jnp.where(p // 4 == 1, pltpu.roll(v, 64, 1), v))
    return out


def feature(small_f, z, i):
    parts = [
        small_f[lax.rem(z + RING - j, RING), row : row + 1]
        for j in range(RING)
        for row in (2 * i, 2 * i + 1)
    ]
    return jnp.concatenate(parts, 1)


class Gather:
    def __init__(self, place, pieces, fulls, sems):
        self.at = place
        self.p, self.z = place.p, place.z
        self.pieces = pieces
        self.fulls = fulls
        self.z_send, self.send, self.recv = sems
        z = self.z
        self.order = (
            jnp.where(z == 0, 3, 1),
            jnp.where((z == 0) | (z == 3), 2, 3),
            jnp.where(z == 0, 1, jnp.where(z == 3, 3, 2)),
        )

    def place(self, chunk, q, k, start=0, size=None):
        full = self.fulls[chunk]
        size = self.pieces[chunk].shape[-2] if size is None else size
        start = (k - 1) * 128 + start
        if chunk >= 2:
            return full.at[q, rows_at(start, size)]
        at = rows_at(start + (q // 2) * 32, size)
        return full.at[:, q % 2, at] if chunk == 0 else full.at[q % 2, at]

    def part(self, chunk, q, k, side):
        half = self.pieces[chunk].shape[-2] // 2
        return self.place(chunk, q, k, side * half, half)

    def up(self, chunk, k, source):
        return remote(
            source,
            self.place(chunk, 0, k + 1),
            self.z_send.at[chunk, k, 0],
            self.recv.at[chunk, k + 1, 0],
            (self.p, jnp.minimum(self.z + 1, RING - 1)),
        )

    def down(self, chunk, k, source):
        return remote(
            source,
            self.place(chunk, 0, k - 1),
            self.z_send.at[chunk, lax.rem(k, RING), 1],
            self.recv.at[chunk, k - 1, 0],
            (self.p, jnp.maximum(self.z - 1, 0)),
        )

    def z_start(self, chunk):
        piece = self.pieces[chunk].at[self.p]
        pl.when(self.z < RING - 1)(self.up(chunk, 0, piece).start)
        pl.when(self.z > 0)(self.down(chunk, RING, piece).start)

    def z_sent(self, chunk):
        piece = self.pieces[chunk].at[self.p]
        pl.when(self.z < RING - 1)(self.up(chunk, 0, piece).wait_send)
        pl.when(self.z > 0)(self.down(chunk, RING, piece).wait_send)
        for k in (1, 2, 3):
            here = self.place(chunk, 0, k)
            if k < 3:
                pl.when((self.z >= k) & (self.z < RING - 1))(self.up(chunk, k, here).wait_send)
            if k > 1:
                pl.when((self.z < k) & (self.z > 0))(self.down(chunk, k, here).wait_send)

    def plane(self, chunk, k, source, target):
        return remote(
            self.place(chunk, source, k),
            self.place(chunk, target, k),
            self.send.at[chunk, k, target],
            self.recv.at[chunk, k, target],
            self.at.near(source ^ target),
        )

    def corner(self, chunk, k, side):
        source, flip = ((4, 2), (2, 4))[side]
        return remote(
            self.part(chunk, source, k, side),
            self.part(chunk, 6, k, side),
            self.send.at[chunk, k, (6, 8)[side]],
            self.recv.at[chunk, k, (6, 8)[side]],
            self.at.near(flip),
        )

    def spread(self, chunk, i):
        k = self.order[i]
        here = self.place(chunk, 0, k)
        remote(
            here, here, self.send.at[chunk, k, 0], self.recv.at[chunk, k, 0], self.at.near(1)
        ).wait_recv()
        pl.when((self.z >= k) & (self.z < RING - 1))(self.up(chunk, k, here).start)
        pl.when((self.z < k) & (self.z > 0))(self.down(chunk, k, here).start)
        for target in (2, 4, 1):
            self.plane(chunk, k, 0, target).start()

    def relay(self, chunk, i):
        k = self.order[i]
        self.plane(chunk, k, 0, 4).wait_recv()
        self.corner(chunk, k, 0).start()
        self.plane(chunk, k, 0, 2).wait_recv()
        self.corner(chunk, k, 1).start()
        self.plane(chunk, k, 4, 5).start()
        self.plane(chunk, k, 2, 3).start()

    def share(self, chunk, i):
        k = self.order[i]
        self.corner(chunk, k, 0).wait_recv()
        self.corner(chunk, k, 1).wait_recv()
        self.plane(chunk, k, 6, 7).start()

    def whole(self, chunk):
        for k in range(1, RING):
            for target in (1, 3, 5, 7):
                self.plane(chunk, k, target - 1, target).wait_recv()

    def sent(self, chunk):
        self.z_sent(chunk)
        for k in range(1, RING):
            for source, target in ((0, 2), (0, 4), (0, 1), (4, 5), (2, 3), (6, 7)):
                self.plane(chunk, k, source, target).wait_send()
            self.corner(chunk, k, 0).wait_send()
            self.corner(chunk, k, 1).wait_send()


class Rows:
    def __init__(self, place, source, target, send, recv, local):
        self.at = place
        self.source, self.target = source, target
        self.send, self.recv, self.local = send, recv, local
        self.width = source.shape[2]

    def columns(self):
        return pl.ds(pl.multiple_of(self.at.z * self.width, self.width), self.width)

    def copy(self, d):
        dest = self.at.shifts[d]
        return remote(
            self.source.at[jnp.clip(dest - self.at.core, 0, self.at.images - 1)],
            self.target.at[:, self.columns()],
            self.send.at[d],
            self.recv.at[d],
            (self.at.p, dest),
        )

    def own(self):
        return pltpu.make_async_copy(
            self.source.at[jnp.clip(self.at.slot, 0, self.at.images - 1)],
            self.target.at[:, self.columns()],
            self.local,
        )

    def start(self):
        self.own().start()
        for d in range(1, RING):
            pl.when(self.at.holds(self.at.shifts[d]))(self.copy(d).start)

    def here(self):
        self.own().wait()
        for d in range(1, RING):
            pl.when(self.at.live)(self.copy(d).wait_recv)

    def sent(self):
        for d in range(1, RING):
            pl.when(self.at.holds(self.at.shifts[d]))(self.copy(d).wait_send)


def norm_rows(value, gain, shift):
    middle = jnp.mean(value, 1, keepdims=True)
    spread = jnp.mean(value * value, 1, keepdims=True) - middle * middle
    return (value - middle) * lax.rsqrt(spread + EPS) * gain + shift


def forward_kernel(images, seq, *refs):
    (
        tokens,
        cotangent,
        small,
        attn_in,
        out_in,
        fc1_raw,
        fc2_in,
        dy_full,
        small_full,
        attn_full,
        out_full,
        fc1_full,
        fc2_full,
        x_rows_out,
        h1_out,
        qkv_out,
        ctx_out,
        r_out,
        h2_out,
        act_out,
        slope_out,
        fc1_in,
        x_full,
        x_in,
        x_v,
        h1_v,
        h2_v,
        qkv_v,
        ctx_v,
        r_v,
        w_v,
        act_v,
        slope_v,
        small_v,
        small_f,
        bias_v,
        pair_v,
        row_send,
        row_recv,
        small_send,
        small_recv,
        z_send,
        unit_send,
        unit_recv,
        local_sem,
        w_sem,
        tile_sem,
        out_sem,
    ) = refs
    at = Place(images)
    p, z = at.p, at.z
    g = Gather(
        at,
        (attn_in, out_in, fc1_in, fc2_in),
        (attn_full, out_full, fc1_full, fc2_full),
        (z_send, unit_send, unit_recv),
    )
    x_rows = Rows(at, tokens, x_full, row_send.at[0], row_recv.at[0], local_sem.at[0])
    dy_rows = Rows(at, cotangent, dy_full, row_send.at[1], row_recv.at[1], local_sem.at[1])
    full = x_full.shape[1]

    def small_copy(d):
        return remote(
            small, small_full.at[d], small_send.at[d], small_recv.at[d], (p, at.shifts[d])
        )

    small_own = pltpu.make_async_copy(small, small_full.at[0], local_sem.at[2])

    fc1_load = pltpu.make_async_copy(fc1_raw, w_v.at[0], local_sem.at[6])
    fc1_load.start()
    at.greet()
    g.z_start(0)
    for d in range(1, RING):
        small_copy(d).start()
    small_own.start()

    g.z_start(1)
    fc1_load.wait()
    for i in range(8):
        rows = slice(i * 128, (i + 1) * 128)
        w_v[1, rows] = w_v[0, :, rows].T
        pltpu.make_async_copy(w_v.at[1, pl.ds(i * 128, 128)], fc1_in.at[i], local_sem.at[5]).start()
    g.spread(0, 0)
    x_rows.start()
    g.spread(0, 1)
    g.spread(0, 2)
    pltpu.make_async_copy(w_v.at[1], w_v.at[1], local_sem.at[5]).wait()
    for d in range(1, RING):
        small_copy(d).wait()
    small_own.wait()
    small_load = pltpu.make_async_copy(small_full, small_v, local_sem.at[3])
    small_load.start()
    x_rows.here()
    x_load = pltpu.make_async_copy(x_full, x_in, local_sem.at[4])
    x_load.start()
    small_load.wait()

    small_f[...] = wide(small_v[...])
    gain, shift = feature(small_f, z, 0), feature(small_f, z, 1)
    for c, row in ((0, 12), (2, 14)):
        for k in range(RING):
            sides = [
                jnp.broadcast_to(small_f[k, row + half : row + half + 1], (8, 128))
                for half in range(2)
            ]
            for half, side in enumerate(turn_heads(sides, p)):
                start = half * TILE + k * 128
                bias_v[c : c + 1, start : start + 128] = side[0:1]
    bias_v[1:2] = jnp.zeros((1, full), jnp.float32)
    x_load.wait()

    def first_norm_of(block, value):
        value = jnp.where(at.live, wide(value), 0.0)
        x_v[block] = low(value)
        h1_v[block] = low(norm_rows(value, gain, shift))

    def first_norm(i, _):
        block = rows_at(i * 64, 64)
        first_norm_of(block, x_in[block])
        return 0

    whole_blocks = seq // 64 * 64
    lax.fori_loop(0, seq // 64, first_norm, 0)
    rest = wide(x_in[whole_blocks:seq])
    rest = jnp.concatenate([rest, jnp.zeros((ROWS - seq, full), jnp.float32)], 0)
    first_norm_of(slice(whole_blocks, ROWS), rest)
    saves = [
        pltpu.make_async_copy(x_v, x_rows_out, out_sem.at[0]),
        pltpu.make_async_copy(h1_v, h1_out, out_sem.at[1]),
    ]
    for s in saves:
        s.start()

    for i in range(3):
        g.relay(0, i)
        g.spread(1, i)
        if i == 1:
            g.z_start(2)
        if i:
            g.share(0, i - 1)
    g.share(0, 2)
    g.whole(0)

    def tile_load(chunk, c, slot):
        return list(
            weight_copies(
                at,
                (attn_in, out_in)[chunk],
                (attn_full, out_full)[chunk],
                chunk,
                w_v.at[slot],
                w_sem.at[slot],
                c,
            )
        )

    def go(copies):
        for copy in copies:
            copy.start()

    def arrive(copies):
        for copy in copies:
            copy.wait()

    def filled(slot):
        pltpu.make_async_copy(w_v.at[slot], w_v.at[slot], w_sem.at[slot]).wait()

    loads = [tile_load(0, c, c % 2) for c in range(3)] + [tile_load(1, 0, 1)]
    go(loads[0])
    go(loads[1])
    steps = [
        lambda: g.spread(2, 0),
        lambda: g.relay(1, 0),
        lambda: g.relay(1, 1),
    ]
    for c in range(3):
        filled(c % 2)

        def project(i, _, c=c):
            block = rows_at(i * TILE, TILE)
            out = dot_on(h1_v[...], w_v[c % 2, block], 1, 1)
            lanes = pl.ds(pl.multiple_of(i * TILE, TILE), TILE)
            qkv_v[c, :, lanes] = low(out + bias_v[c : c + 1, lanes])
            return 0

        lax.fori_loop(0, 2, project, 0)
        if c == 0:
            go(loads[2])
        steps[c]()
    save = pltpu.make_async_copy(qkv_v, qkv_out, out_sem.at[2])
    save.start()
    saves.append(save)

    key = lax.broadcasted_iota(jnp.int32, (ROWS, 1), 0)

    def attend(k, _):
        for c in range(3):
            split_heads(qkv_v.at[c], pair_v.at[c], k)
        for pair in range(2):
            keys, values = pair_v[1, pair], pair_v[2, pair]
            for r in range(ROWS // 128):
                block = slice(r * 128, (r + 1) * 128)
                query = pair_v[0, pair, block] * jnp.bfloat16(HD ** (-0.5))
                out = None
                for h in range(2):
                    mask = head_mask(h)
                    scores = dot_on(keys, jnp.where(mask, query, jnp.bfloat16(0)), 1, 1)
                    scores = jnp.where(key < seq, scores, -1e30)
                    expo = jnp.exp(scores - jnp.max(scores, 0, keepdims=True))
                    probs = low(expo * (1.0 / jnp.sum(expo, 0, keepdims=True)))
                    part = dot_on(probs, values, 0, 0)
                    out = part if out is None else jnp.where(mask, part, out)
                pair_v[0, pair, block] = low(out)
        join_heads(pair_v.at[0], ctx_v, k)
        for i in range(4):

            @pl.when(k == i)
            def _():
                for step in attention_steps[i]:
                    step()

        return 0

    attention_steps = [
        [lambda: g.spread(2, 1), lambda: g.z_start(3), lambda: g.relay(1, 2)],
        [lambda: g.spread(2, 2), lambda: g.share(1, 0), lambda: g.share(1, 1)],
        [lambda: g.share(1, 2), lambda: g.relay(2, 0), lambda: g.spread(3, 0)],
        [lambda: g.relay(2, 1), lambda: g.spread(3, 1), dy_rows.start],
    ]
    lax.fori_loop(0, 4, attend, 0)
    g.whole(1)
    go(loads[3])
    save = pltpu.make_async_copy(ctx_v, ctx_out, out_sem.at[3])
    save.start()
    saves.append(save)
    out_bias = feature(small_f, z, 2)
    gain2, shift2 = feature(small_f, z, 3), feature(small_f, z, 4)
    filled(1)
    for i in range(2):
        lanes = slice(i * TILE, (i + 1) * TILE)
        attn = dot_on(ctx_v[...], w_v[1, :, lanes], 1, 0)
        r_v[:, lanes] = wide(x_v[:, lanes]) + (attn + out_bias[:, lanes])
    save = pltpu.make_async_copy(r_v, r_out, out_sem.at[4])
    save.start()
    saves.append(save)
    g.relay(2, 2)
    g.spread(3, 2)
    g.share(2, 0)

    def second_norm(i, _):
        block = rows_at(i * 64, 64)
        h2_v[block] = low(norm_rows(r_v[block], gain2, shift2))
        return 0

    lax.fori_loop(0, ROWS // 64, second_norm, 0)
    save = pltpu.make_async_copy(h2_v, h2_out, out_sem.at[5])
    save.start()
    saves.append(save)
    g.share(2, 1)
    g.relay(3, 0)
    g.share(2, 2)
    g.whole(2)

    def pair_load(i):
        slot = i % 2
        for side in range(2):
            yield from weight_copies(
                at,
                fc1_in,
                fc1_full,
                2,
                w_v.at[slot, pl.ds(side * TILE, TILE)],
                w_sem.at[slot],
                q=2 * i + side,
            )

    def tile_saves(q):
        slot = q % 2
        return [
            pltpu.make_async_copy(act_v.at[slot], act_out.at[q], tile_sem.at[0, slot]),
            pltpu.make_async_copy(slope_v.at[slot], slope_out.at[q], tile_sem.at[1, slot]),
        ]

    pairs = [list(pair_load(i)) for i in range(4)]
    go(pairs[0])
    go(pairs[1])
    steps = [
        [lambda: g.relay(3, 1)],
        [lambda: g.relay(3, 2)],
        [lambda: g.share(3, 0), lambda: g.share(3, 1)],
        [lambda: g.share(3, 2)],
    ]
    for i in range(4):
        filled(i % 2)
        for side in range(2):
            q = 2 * i + side
            if q >= 2:
                arrive(tile_saves(q - 2))
            row = pl.ds(16 + turned(p, q), 1)
            bias = jnp.concatenate([small_f[k, row] for k in range(RING)], 1)
            for j in range(2):
                cols = slice(j * 256, (j + 1) * 256)
                start = side * TILE + j * 256
                u = dot_on(h2_v[...], w_v[i % 2, start : start + 256], 1, 1) + bias[:, cols]
                sg = 1.0 / (1.0 + jnp.exp(-1.702 * u))
                act_v[side, :, cols] = low(u * sg)
                slope_v[side, :, cols] = low(sg + 1.702 * u * sg * (1.0 - sg))
            go(tile_saves(q))
        if i < 2:
            go(pairs[i + 2])
        for step in steps[i]:
            step()
    for q in (6, 7):
        arrive(tile_saves(q))
    arrive(saves)
    g.whole(3)
    dy_rows.here()
    for chunk in range(4):
        g.sent(chunk)
    x_rows.sent()
    dy_rows.sent()


def forward(tokens, cotangent, small, attn_in, out_in, fc1_raw, fc2_in):
    images, rows, width = tokens.shape
    full = RING * width
    bf16 = jnp.bfloat16
    f32 = jnp.float32
    dma = pltpu.SemaphoreType.DMA
    shapes = (
        ((rows, full), bf16),
        ((RING,) + small.shape, bf16),
        ((3, 2, 384, full), bf16),
        ((2, 384, full), bf16),
        ((8, 384, full), bf16),
        ((8, 384, full), bf16),
        ((ROWS, full), bf16),
        ((ROWS, full), bf16),
        ((3, ROWS, full), bf16),
        ((ROWS, full), bf16),
        ((ROWS, full), f32),
        ((ROWS, full), bf16),
        ((8, ROWS, TILE), bf16),
        ((8, ROWS, TILE), bf16),
        (fc2_in.shape, bf16),
        ((rows, full), bf16),
    )
    return pl.pallas_call(
        functools.partial(forward_kernel, images, rows),
        out_shape=[jax.ShapeDtypeStruct(s, d) for s, d in shapes],
        in_specs=[pl.BlockSpec(memory_space=pl.ANY)] * 7,
        out_specs=[pl.BlockSpec(memory_space=pl.ANY)] * len(shapes),
        scratch_shapes=[
            pltpu.VMEM((rows, full), bf16),
            pltpu.VMEM((ROWS, full), bf16),
            pltpu.VMEM((ROWS, full), bf16),
            pltpu.VMEM((ROWS, full), bf16),
            pltpu.VMEM((3, ROWS, full), bf16),
            pltpu.VMEM((ROWS, full), bf16),
            pltpu.VMEM((ROWS, full), f32),
            pltpu.VMEM((2, 1024, full), bf16),
            pltpu.VMEM((2, ROWS, TILE), bf16),
            pltpu.VMEM((2, ROWS, TILE), bf16),
            pltpu.VMEM((RING,) + small.shape, bf16),
            pltpu.VMEM((RING,) + small.shape, f32),
            pltpu.VMEM((8, full), f32),
            pltpu.VMEM((3, 2, ROWS, 128), bf16),
            dma((2, RING)),
            dma((2, RING)),
            dma((RING,)),
            dma((RING,)),
            dma((4, RING, 2)),
            dma((4, RING, 9)),
            dma((4, RING, 9)),
            dma((7,)),
            dma((2,)),
            dma((2, 2)),
            dma((6,)),
        ],
        compiler_params=pltpu.CompilerParams(
            collective_id=0, has_side_effects=True, vmem_limit_bytes=56 * 2**20
        ),
    )(tokens, cotangent, small, attn_in, out_in, fc1_raw, fc2_in)


class Reduce:
    def __init__(self, place, sizes, outs, bufs, sems):
        self.at = place
        self.sizes = sizes
        self.starts = [sum(sizes[:i]) for i in range(4)]
        self.outs = outs
        self.held, self.first, self.second, self.far, self.total, self.stage = bufs
        self.core_send, self.core_recv, self.send, self.recv, self.local = sems[:5]
        self.plane_send, self.plane_recv = sems[5:]

    def rows(self, c):
        return pl.ds(self.starts[c], self.sizes[c])

    def give(self, group, xy, slot):
        y, x = xy // 2, lax.rem(xy, 2)
        at = self.rows(group)
        source = self.stage.at[slot]
        if group == 2:
            source = source.at[:, pl.ds(xy * 32, 32)]
        return remote(
            source,
            self.held.at[y, x, :, at],
            self.core_send.at[group, xy],
            self.core_recv.at[group, xy],
            self.at.near(1),
        )

    def hop(self, source, target, c, i, q):
        return remote(source, target, self.send.at[c, i], self.recv.at[c, i], self.at.near(q))

    def x_copy(self, c, y):
        at = self.rows(c)
        return self.hop(self.held.at[y, 1, 0:2, at], self.first.at[0, y, :, at], c, y, 2)

    def y_copy(self, c, x):
        at = self.rows(c)
        return self.hop(self.held.at[1, x, 2:4, at], self.first.at[1, x, :, at], c, 2 + x, 4)

    def xy_copy(self, c):
        at = self.rows(c)
        return self.hop(self.first.at[0, 1, :, at], self.second.at[0, :, at], c, 4, 4)

    def yx_copy(self, c):
        at = self.rows(c)
        return self.hop(self.first.at[1, 1, :, at], self.second.at[1, :, at], c, 5, 2)

    def z_copy(self, c, k):
        return remote(
            self.second.at[k // 2, k % 2, self.rows(c)],
            self.far.at[k - 1, self.rows(c)],
            self.send.at[c, 5 + k],
            self.recv.at[c, 5 + k],
            (self.at.p, self.at.shifts[RING - k]),
        )

    def out_copy(self, c, q):
        return self.hop(self.total.at[self.rows(c)], self.outs[c].at[self.at.p], c, {1: 9, 2: 10, 4: 11}[q], q)

    def out_here(self, c, q):
        block = self.outs[c].at[turned(self.at.p, q)]
        self.hop(self.total.at[self.rows(c)], block, c, {1: 9, 2: 10, 4: 11}[q], q).wait_recv()

    def corner(self, c, side):
        source, flip = ((4, 2), (2, 4))[side]
        half = self.sizes[c] // 2
        at = pl.ds(side * half, half)
        block = self.outs[c].at[turned(self.at.p, source), at]
        return self.hop(block, block, c, 14 + side, flip)

    def corner_here(self, c):
        half = self.sizes[c] // 2
        for side in range(2):
            block = self.outs[c].at[turned(self.at.p, 6), pl.ds(side * half, half)]
            self.hop(block, block, c, 14 + side, 2).wait_recv()

    def out_own(self, c):
        return pltpu.make_async_copy(
            self.total.at[self.rows(c)], self.outs[c].at[self.at.p], self.local.at[c]
        )

    def share(self, c, q):
        block = self.outs[c].at[turned(self.at.p, q)]
        return self.hop(block, block, c, 16 + q // 2, 1)

    def share_here(self, c, q):
        block = self.outs[c].at[turned(self.at.p, q)]
        theirs = self.outs[c].at[turned(self.at.p, q + 1)]
        self.hop(block, theirs, c, 16 + q // 2, 1).wait_recv()

    def add(self, dest, *sources):
        def body(i, _):
            at = rows_at(i * 16, 16)
            value = wide(sources[0][at])
            for s in sources[1:]:
                value = value + wide(s[at])
            dest[at] = low(value)
            return 0

        lax.fori_loop(0, dest.shape[0] // 16, body, 0)

    def turn(self, c):
        at = self.rows(c)
        self.x_copy(c, 1).wait_recv()
        for k in range(2):
            block = self.first.at[0, 1, k, at]
            self.add(block, block, self.held.at[1, 0, k, at])
        self.xy_copy(c).start()
        self.y_copy(c, 1).wait_recv()
        for k in range(2):
            block = self.first.at[1, 1, k, at]
            self.add(block, block, self.held.at[0, 1, 2 + k, at])
        self.yx_copy(c).start()

    def rise(self, c):
        at = self.rows(c)
        self.x_copy(c, 0).wait_recv()
        self.xy_copy(c).wait_recv()
        for k in range(2):
            block = self.second.at[0, k, at]
            self.add(block, block, self.first.at[0, 0, k, at], self.held.at[0, 0, k, at])
        self.z_copy(c, 1).start()
        self.y_copy(c, 0).wait_recv()
        self.yx_copy(c).wait_recv()
        for k in range(2):
            block = self.second.at[1, k, at]
            self.add(block, block, self.first.at[1, 0, k, at], self.held.at[0, 0, 2 + k, at])
            self.z_copy(c, 2 + k).start()

    def settle(self, c):
        at = self.rows(c)
        for k in range(1, RING):
            self.z_copy(c, k).wait_recv()
        self.add(
            self.total.at[at], self.second.at[0, 0, at], *(self.far.at[k, at] for k in range(3))
        )
        self.out_own(c).start()
        for q in (2, 4, 1):
            self.out_copy(c, q).start()

    def relay(self, c):
        self.out_here(c, 4)
        self.corner(c, 0).start()
        self.out_here(c, 2)
        self.corner(c, 1).start()
        for q in (2, 4):
            self.share(c, q).start()

    def last(self, c):
        self.corner_here(c)
        self.share(c, 6).start()

    def whole(self, c):
        self.out_own(c).wait()
        self.out_here(c, 1)
        for q in (2, 4, 6):
            self.share_here(c, q)

    def give_plane(self, k, slot, y):
        return remote(
            self.stage.at[slot, pl.ds(2 * y, 2), pl.ds(0, self.sizes[3])],
            self.held.at[y, :, k, self.rows(3)],
            self.core_send.at[3 + y, k],
            self.core_recv.at[3 + y, k],
            self.at.near(1),
        )

    def plane_hop(self, source, target, k, i, q):
        return remote(
            source, target, self.plane_send.at[k, i], self.plane_recv.at[k, i], self.at.near(q)
        )

    def plane_first(self, k):
        at, side = self.rows(3), k // 2
        source = self.held.at[:, 1, k, at] if side == 0 else self.held.at[1, :, k, at]
        return self.plane_hop(source, self.first.at[side, :, k % 2, at], k, 0, (2, 4)[side])

    def plane_second(self, k):
        at, side = self.rows(3), k // 2
        return self.plane_hop(
            self.first.at[side, 1, k % 2, at],
            self.second.at[side, k % 2, at],
            k,
            1,
            (4, 2)[side],
        )

    def plane_turn(self, k):
        at, side = self.rows(3), k // 2
        self.plane_first(k).wait_recv()
        block = self.first.at[side, 1, k % 2, at]
        own = self.held.at[1, 0, k, at] if side == 0 else self.held.at[0, 1, k, at]
        self.add(block, block, own)
        self.plane_second(k).start()

    def plane_rise(self, k):
        at, side = self.rows(3), k // 2
        self.plane_second(k).wait_recv()
        block = self.second.at[side, k % 2, at]
        self.add(block, block, self.first.at[side, 0, k % 2, at], self.held.at[0, 0, k, at])
        if k:
            self.z_copy(3, k).start()

    def finish(self, c):
        for q in (2, 4, 6):
            self.share(c, q).wait_send()
        if c < 3:
            for i in range(2):
                self.x_copy(c, i).wait_send()
                self.y_copy(c, i).wait_send()
            self.xy_copy(c).wait_send()
            self.yx_copy(c).wait_send()
        else:
            for k in range(RING):
                self.plane_first(k).wait_send()
                self.plane_second(k).wait_send()
        for k in range(1, RING):
            self.z_copy(c, k).wait_send()
        for q in (2, 4, 1):
            self.out_copy(c, q).wait_send()
        for side in range(2):
            self.corner(c, side).wait_send()


class Return:
    def __init__(self, place, source, target, send, recv):
        self.at = place
        self.source, self.target = source, target
        self.send, self.recv = send, recv
        self.width = target.shape[2]

    def pair(self, plane):
        columns = pl.ds(pl.multiple_of(plane * self.width, self.width), self.width)
        slot = jnp.clip(self.at.slot, 0, self.at.images - 1)
        return self.source.at[:, columns], self.target.at[slot]

    def copy(self, d):
        source, target = self.pair(self.at.shifts[d])
        return remote(
            source, target, self.send.at[d], self.recv.at[d], (self.at.p, self.at.shifts[d])
        )

    def own(self):
        return pltpu.make_async_copy(*self.pair(self.at.z), self.send.at[0])

    def start(self):
        pl.when(self.at.live)(self.own().start)
        for d in range(1, RING):
            pl.when(self.at.live)(self.copy(d).start)

    def sent(self):
        pl.when(self.at.live)(self.own().wait)
        for d in range(1, RING):
            pl.when(self.at.live)(self.copy(d).wait_send)

    def here(self):
        for d in range(1, RING):
            other = lax.rem(self.at.z + RING - d, RING)
            pl.when(self.at.holds(other))(self.copy(d).wait_recv)


def norm_parts(value):
    middle = jnp.mean(value, 1, keepdims=True)
    spread = jnp.mean(value * value, 1, keepdims=True) - middle * middle
    inverse = lax.rsqrt(spread + EPS)
    return (value - middle) * inverse, inverse


def norm_reverse(gradient, normalized, gain, inverse):
    scaled = gradient * gain
    first = jnp.mean(scaled, 1, keepdims=True)
    second = jnp.mean(scaled * normalized, 1, keepdims=True)
    return inverse * (scaled - first - normalized * second)


def backward_kernel(images, seq, sizes, *refs):
    (
        mask_in,
        small_full,
        x_in,
        h1_in,
        qkv_in,
        ctx_in,
        r_in,
        h2_in,
        act_in,
        slope_in,
        dy_in,
        attn_in,
        out_in,
        fc1_in,
        fc2_in,
        attn_full,
        out_full,
        fc1_full,
        fc2_full,
        block_out,
        grad_out,
        vector_out,
        s2,
        s1,
        so,
        sa,
        t1,
        ta,
        held,
        first,
        second,
        far,
        total,
        stage,
        w_v,
        dy_v,
        h_v,
        act_v,
        du_v,
        mlp_v,
        dh_v,
        r_v,
        da_v,
        ctx_v,
        dctx_v,
        qkv_v,
        p_v,
        ds_v,
        blk_v,
        sums_v,
        dus_v,
        small_v,
        small_f,
        vec,
        vec_far,
        core_send,
        core_recv,
        send,
        recv,
        row_send,
        row_recv,
        vec_send,
        vec_recv,
        local_sem,
        plane_send,
        plane_recv,
        load_sem,
        tile_sem,
        w_sem,
    ) = refs
    at = Place(images)
    p, z = at.p, at.z
    full = x_in.shape[1]
    quarter = full // RING
    done = seq // 32 * 32
    red = Reduce(
        at,
        sizes,
        (s2, s1, so, sa),
        (held, first, second, far, total, stage),
        (core_send, core_recv, send, recv, local_sem, plane_send, plane_recv),
    )
    blocks_back = Return(at, blk_v, block_out, row_send.at[0], row_recv.at[0])
    grads_back = Return(at, blk_v, grad_out, row_send.at[1], row_recv.at[1])

    def load(source, target, i):
        return pltpu.make_async_copy(source, target, load_sem.at[i])

    dy_load = load(dy_in, blk_v, 0)
    h2_load = load(h2_in, h_v, 1)
    r_load = load(r_in, r_v, 2)
    ctx_load = load(ctx_in, ctx_v, 3)
    qkv_load = load(qkv_in, qkv_v, 4)
    small_load = load(small_full, small_v, 5)
    h1_load = load(h1_in, h_v, 6)
    x_load = load(x_in, dy_v, 7)

    def tile_loads(q, slot):
        yield pltpu.make_async_copy(act_in.at[q], act_v.at[slot], tile_sem.at[0, slot])
        yield pltpu.make_async_copy(slope_in.at[q], du_v.at[slot], tile_sem.at[1, slot])
        for side, (pieces, whole) in enumerate(((fc1_in, fc1_full), (fc2_in, fc2_full))):
            yield from weight_copies(
                at, pieces, whole, 2, w_v.at[slot, pl.ds(side * TILE, TILE)], w_sem.at[slot], q=q
            )

    def matrix_loads(chunk, c, slot):
        pieces, whole = ((attn_in, attn_full), (out_in, out_full))[chunk]
        return weight_copies(at, pieces, whole, chunk, w_v.at[slot], w_sem.at[slot], c)

    def go(copies):
        for copy in copies:
            copy.start()

    def filled(slot):
        pltpu.make_async_copy(w_v.at[slot], w_v.at[slot], w_sem.at[slot]).wait()

    def turn_of(i):
        return jnp.where(i == 0, 3, jnp.where(i == 1, 1, jnp.where(i == 2, 2, 0)))

    dy_load.start()
    go(tile_loads(7, 0))
    h2_load.start()
    at.greet()
    go(tile_loads(6, 1))
    small_load.start()
    r_load.start()
    ctx_load.start()
    qkv_load.start()

    sums_v[...] = jnp.zeros_like(sums_v)
    mask = mask_in[jnp.clip(at.slot, 0, images - 1)].astype(jnp.float32)
    dy_load.wait()

    def masked(value):
        return jnp.where(at.live, wide(value), 0.0) * mask

    def mask_rows(i, _):
        block = rows_at(i * 32, 32)
        dy_v[block] = low(masked(blk_v[block]))
        return 0

    lax.fori_loop(0, done // 32, mask_rows, 0)
    rest = jnp.zeros((ROWS - seq, full), jnp.float32)
    dy_v[done:] = low(jnp.concatenate([masked(blk_v[done:seq]), rest], 0))
    h2_load.wait()

    def halves(body):
        lax.fori_loop(0, 2, lambda j, _: (body(pl.ds(pl.multiple_of(j * TILE, TILE), TILE)), 0)[1], 0)

    def keep(group, xy, left, right):
        y, x = xy // 2, lax.rem(xy, 2)
        red.give(group, xy, 0).wait_recv()
        at_rows = red.rows(group)

        def body(cols):
            grad = dot_on(left[...], right[:, cols], 0, 0)
            for k in range(RING):
                old = wide(held[y, x, k, at_rows, cols])
                held[y, x, k, at_rows, cols] = low(old + grad[k * 128 : (k + 1) * 128])

        halves(body)
        pl.when(x == 1)(red.x_copy(group, y).start)
        pl.when(y == 1)(red.y_copy(group, x).start)

    def stage_fill(slot, left, right):
        def body(cols):
            grad = low(dot_on(left[...], right[:, cols], 0, 0))
            for k in range(RING):
                stage[slot, k, :, cols] = grad[k * 128 : (k + 1) * 128]

        halves(body)

    mlp_v[...] = jnp.zeros_like(mlp_v)
    dh_v[...] = jnp.zeros_like(dh_v)

    def hidden_tile(i, core):
        slot = 1 - core
        xy = turn_of(i)
        q = 2 * xy + core
        pltpu.make_async_copy(act_in.at[q], act_v.at[slot], tile_sem.at[0, slot]).wait()
        if core:
            pl.when(i > 0)(red.give(0, turn_of(i - 1), 0).wait_send)
            stage_fill(0, act_v.at[slot], dy_v)
            red.give(0, xy, 0).start()
        else:
            keep(0, xy, act_v.at[slot], dy_v)
        pltpu.make_async_copy(slope_in.at[q], du_v.at[slot], tile_sem.at[1, slot]).wait()
        filled(slot)

        def slopes(j, _):
            cols = pl.ds(pl.multiple_of(j * 256, 256), 256)
            start = pl.ds(pl.multiple_of(TILE + j * 256, 256), 256)
            dact = dot_on(dy_v[...], w_v[slot, start], 1, 1)
            du = low(dact * wide(du_v[slot, :, cols]))
            du_v[slot, :, cols] = du
            dus_v[pl.ds(q, 1), cols] = jnp.sum(wide(du), 0, keepdims=True)
            return 0

        lax.fori_loop(0, 2, slopes, 0)
        if core:
            pl.when(i > 0)(red.give(1, turn_of(i - 1), 1).wait_send)
            stage_fill(1, du_v.at[slot], h_v)
            red.give(1, xy, 1).start()
        else:
            keep(1, xy, du_v.at[slot], h_v)

        def back(cols):
            mlp_v[:, cols] += dot_on(act_v[slot], w_v[slot, TILE:, cols], 1, 0)
            dh_v[:, cols] += dot_on(du_v[slot], w_v[slot, :TILE, cols], 1, 0)

        halves(back)

        @pl.when(i < 3)
        def _():
            go(tile_loads(2 * turn_of(i + 1) + core, slot))

    def hidden_tiles(i, _):
        hidden_tile(i, 1)
        hidden_tile(i, 0)
        return 0

    lax.fori_loop(0, 4, hidden_tiles, 0)
    go(matrix_loads(1, 0, 0))
    go(matrix_loads(0, 0, 1))
    h1_load.start()

    small_load.wait()

    small_f[...] = wide(small_v[...])
    gain1, gain2 = feature(small_f, z, 0), feature(small_f, z, 3)
    fc2_bias = feature(small_f, z, 5)
    r_load.wait()

    def collect(i, value):
        sums_v[i] = sums_v[i] + sum(value[r : r + 8] for r in range(0, value.shape[0], 8))

    def second_norm(block):
        r1 = r_v[block]
        dy = wide(dy_v[block])
        out = low((r1 + (mlp_v[block] + fc2_bias)) * mask)
        hat, inverse = norm_parts(r1)
        dh = dh_v[block]
        dr1 = dy + norm_reverse(dh, hat, gain2, inverse)
        da = low(dr1)
        r_v[block] = dr1
        da_v[block] = da
        collect(2, wide(da))
        collect(3, dh * hat)
        collect(4, dh)
        collect(5, dy)
        return out

    def by_blocks(norm):
        def body(i, _):
            block = rows_at(i * 32, 32)
            blk_v[block] = norm(block)
            return 0

        lax.fori_loop(0, done // 32, body, 0)
        out = norm(slice(done, done + 32))
        blk_v[done:seq] = out[: seq - done]

    by_blocks(second_norm)
    for ref in (r_v, da_v):
        ref[done + 32 :] = jnp.zeros((ROWS - done - 32, full), ref.dtype)
    blocks_back.start()
    x_load.start()
    ctx_load.wait()

    pending = [[red.give(0, 0, 0)], [red.give(1, 0, 1)]]

    def stage_free(slot):
        for copy in pending[slot]:
            copy.wait_send()
        pending[slot] = []

    def stage_go(slot, copies):
        go(copies)
        pending[slot] = copies

    far_half = pl.ds(TILE, TILE)
    near_half = pl.ds(0, TILE)
    stage_free(0)
    stage_fill(0, ctx_v.at[:, far_half], da_v)
    stage_go(0, [red.give(2, xy, 0) for xy in range(4)])
    filled(0)

    def dctx_half(rows):
        dctx_v[:, rows] = low(dot_on(da_v[...], w_v[0, rows], 1, 1))

    halves(dctx_half)

    def keep_heads(group, left, right):
        start = red.starts[group]
        for xy in range(4):
            red.give(group, xy, 0).wait_recv()
        def body(cols):
            grad = dot_on(left[...], right[:, cols], 0, 0)
            for xy in range(4):
                for k in range(RING):
                    rows = slice(start, start + 32)
                    at_row = k * 128 + xy * 32
                    old = wide(held[xy // 2, xy % 2, k, rows, cols])
                    held[xy // 2, xy % 2, k, rows, cols] = low(old + grad[at_row : at_row + 32])

        halves(body)

    def first_sends(c):
        red.x_copy(c, 1).start()
        red.y_copy(c, 1).start()
        red.x_copy(c, 0).start()
        red.y_copy(c, 0).start()

    keep_heads(2, ctx_v.at[:, near_half], da_v)
    first_sends(2)
    go(matrix_loads(0, 1, 0))
    qkv_load.wait()
    red.turn(0)

    key = lax.broadcasted_iota(jnp.int32, (ROWS, 1), 0)
    scale = HD ** (-0.5)

    none = jnp.bfloat16(0)

    pairs, results = act_v, du_v

    def attend_back(k):
        for c in range(3):
            split_heads(qkv_v.at[c], pairs.at[:, :, pl.ds(c * 128, 128)], k)
        split_heads(dctx_v, pairs.at[:, :, pl.ds(384, 128)], k)

        def one_pair(pair, _):
            query = pairs[pair, :, :128] * jnp.bfloat16(scale)
            keys, values = pairs[pair, :, 128:256], pairs[pair, :, 256:384]
            dctx = pairs[pair, :, 384:]
            for h in range(2):
                mask = head_mask(h)
                for r in range(ROWS // 128):
                    cols = slice(r * 128, (r + 1) * 128)
                    scores = dot_on(keys, jnp.where(mask, query[cols], none), 1, 1)
                    scores = jnp.where(key < seq, scores, -1e30)
                    expo = jnp.exp(scores - jnp.max(scores, 0, keepdims=True))
                    probs = expo * (1.0 / jnp.sum(expo, 0, keepdims=True))
                    dprobs = dot_on(values, jnp.where(mask, dctx[cols], none), 1, 1)
                    delta = jnp.sum(probs * dprobs, 0, keepdims=True)
                    p_v[:, cols] = low(probs)
                    ds_v[:, cols] = low(probs * (dprobs - delta))
                dq = dot_on(ds_v[...], keys, 0, 0) * scale
                dk = dot_on(ds_v[...], query, 1, 0)
                dv = dot_on(p_v[...], dctx, 1, 0)
                for c, value in enumerate((dq, dk, dv)):
                    at_c = slice(c * 128, (c + 1) * 128)
                    if h == 0:
                        results[pair, :, at_c] = low(value)
                    else:
                        results[pair, :, at_c] = jnp.where(mask, low(value), results[pair, :, at_c])
            return 0

        lax.fori_loop(0, 2, one_pair, 0)
        for c in range(3):
            join_heads(results.at[:, :, pl.ds(c * 128, 128)], qkv_v.at[c], k)

    def plane_grad(half, k):
        start = pl.multiple_of(half * TILE + k * 128, 128)
        left = jnp.concatenate([qkv_v[c, :, pl.ds(start, 128)] for c in range(3)], 1)
        for j in range(2):
            cols = slice(j * TILE, (j + 1) * TILE)
            grad = dot_on(left, h_v[:, cols], 0, 0)
            for c in range(3):
                for xy in range(4):
                    at_row = c * 128 + xy * 32
                    yield xy // 2, xy % 2, c * 32, cols, grad[at_row : at_row + 32]

    steps = [
        [lambda: red.turn(1)],
        [lambda: red.turn(2), lambda: red.rise(0)],
        [lambda: red.plane_turn(2), lambda: red.rise(1), lambda: red.rise(2)],
        [lambda: red.plane_rise(2), lambda: red.plane_turn(1), lambda: red.settle(0)],
    ]
    h1_load.wait()
    stage_free(0)
    stage_free(1)

    def attend_group(i, _):
        k = jnp.where(i == 0, 2, jnp.where(i == 1, 1, jnp.where(i == 2, 3, 0)))
        slot = lax.rem(i, 2)
        attend_back(k)

        @pl.when(i >= 2)
        def _():
            for y in range(2):
                red.give_plane(jnp.where(i == 2, 2, 1), slot, y).wait_send()

        for y, x, row, cols, grad in plane_grad(1, k):
            stage[slot, 2 * y + x, row : row + 32, cols] = low(grad)
        for y in range(2):
            red.give_plane(k, slot, y).start()
        for j in range(4):

            @pl.when(i == j)
            def _():
                for step in steps[j]:
                    step()

        for y in range(2):
            red.give_plane(k, slot, y).wait_recv()
        start = red.starts[3]
        for y, x, row, cols, grad in plane_grad(0, k):
            rows = slice(start + row, start + row + 32)
            held[y, x, k, rows, cols] = low(wide(held[y, x, k, rows, cols]) + grad)
        for j, plane in enumerate((2, 1, 3, 0)):
            pl.when(i == j)(red.plane_first(plane).start)
        return 0

    lax.fori_loop(0, 4, attend_group, 0)
    for i in range(3):
        if i == 2:
            go(matrix_loads(0, 2, 1))
        slot = (i + 1) % 2
        filled(slot)

        def spread_back(cols, c=i, slot=slot):
            value = dot_on(qkv_v[c], w_v[slot, :, cols], 1, 0)
            dh_v[:, cols] = value if c == 0 else value + dh_v[:, cols]

        halves(spread_back)
        if i == 0:
            red.plane_turn(3)
            red.relay(0)
        if i == 1:
            red.plane_rise(1)
    red.plane_rise(3)
    x_load.wait()
    blocks_back.sent()

    def first_norm(block):
        hat, inverse = norm_parts(wide(dy_v[block]))
        dh = dh_v[block]
        collect(0, dh * hat)
        collect(1, dh)
        return low(r_v[block] + norm_reverse(dh, hat, gain1, inverse))

    red.plane_turn(0)
    by_blocks(first_norm)
    red.plane_rise(0)
    grads_back.start()
    red.settle(1)

    for i in range(6):
        value = jnp.sum(sums_v[i], 0, keepdims=True)
        for j in range(RING):
            for side in range(2):
                start = j * quarter + side * 128
                vec[j, 2 * i + side : 2 * i + side + 1] = value[:, start : start + 128]
    for row, c in ((12, 0), (14, 2)):
        value = jnp.sum(wide(qkv_v[c]), 0, keepdims=True)
        for k in range(RING):
            starts = [half * TILE + k * 128 for half in range(2)]
            sides = [jnp.broadcast_to(value[:, i : i + 128], (8, 128)) for i in starts]
            for half, side in enumerate(turn_heads(sides, p)):
                vec[lax.rem(z + RING - k, RING), row + half : row + half + 1] = side[0:1]
    for q in range(8):
        for k in range(RING):
            at_row = pl.ds(16 + turned(p, q), 1)
            vec[lax.rem(z + RING - k, RING), at_row] = dus_v[q : q + 1, k * 128 : (k + 1) * 128]

    def vec_copy(i):
        return remote(vec, vec_far.at[i], vec_send.at[i], vec_recv.at[i], at.near((1, 2, 4)[i]))

    def vec_z(d):
        return remote(
            vec.at[at.shifts[d]],
            vec_far.at[3, d],
            vec_send.at[2 + d],
            vec_recv.at[2 + d],
            (p, at.shifts[d]),
        )

    def vec_step(i):
        vec_copy(i).wait()
        vec[...] = vec[...] + vec_far[i]

    vec_copy(0).start()
    red.settle(2)
    red.settle(3)
    vec_step(0)
    vec_copy(1).start()
    red.relay(1)
    red.last(0)
    vec_step(1)
    vec_copy(2).start()
    red.relay(2)
    red.last(1)
    red.relay(3)
    vec_step(2)
    for d in range(1, RING):
        vec_z(d).start()
    red.last(2)
    red.last(3)
    red.whole(0)
    red.whole(1)

    for piece in range(8):
        load(s1.at[piece], w_v.at[0, pl.ds(piece * 128, 128)], 8).start()
    load(w_v.at[0], w_v.at[0], 8).wait()
    for piece in range(8):
        rows = slice(piece * 128, (piece + 1) * 128)
        w_v[1, :, rows] = w_v[0, rows].T
    rows_save = load(w_v.at[1], t1, 9)
    rows_save.start()
    for d in range(1, RING):
        vec_z(d).wait()
    vec[0] = vec[z] + (vec_far[3, 1] + (vec_far[3, 2] + vec_far[3, 3]))
    vec_out = pltpu.make_async_copy(vec.at[0], vector_out, local_sem.at[4])
    vec_out.start()
    red.whole(2)
    for y in range(2):
        red.give_plane(3, 0, y).wait_send()
        red.give_plane(0, 1, y).wait_send()
    for c in range(3):
        red.finish(c)
    blocks_back.here()
    rows_save.wait()
    red.whole(3)

    def head_loads():
        for piece in range(8):
            for c in range(3):
                yield load(
                    sa.at[piece, pl.ds(c * 32, 32)], w_v.at[0, pl.ds(c * 256 + piece * 32, 32)], 10
                )

    go(head_loads())
    part = w_v.at[0, pl.ds(0, 768)]
    load(part, part, 10).wait()
    saves = []
    for c in range(3):
        rows = slice(c * 256, (c + 1) * 256)
        w_v[1, :, rows] = w_v[0, rows].T
        saves.append(load(w_v.at[1, :, pl.ds(c * 256, 256)], ta.at[c], 11 + c))
        saves[-1].start()
    for copy in saves:
        copy.wait()
    red.finish(3)
    vec_out.wait()
    grads_back.sent()
    grads_back.here()


def backward(mask, *arrays):
    images = mask.shape[0]
    seq, full = arrays[9].shape
    width = full // RING
    bf16 = jnp.bfloat16
    f32 = jnp.float32
    dma = pltpu.SemaphoreType.DMA
    attn_in, out_in, fc1_in, fc2_in = arrays[10:14]
    sizes = (fc2_in.shape[1], fc1_in.shape[1], out_in.shape[1], 3 * attn_in.shape[2])
    every = sum(sizes)
    outs = [jax.ShapeDtypeStruct((images, seq, width), bf16)] * 2
    outs.append(jax.ShapeDtypeStruct((24, 128), f32))
    outs += [jax.ShapeDtypeStruct((8, n, full), bf16) for n in sizes]
    outs.append(jax.ShapeDtypeStruct((full, 8 * sizes[1]), bf16))
    outs.append(jax.ShapeDtypeStruct((3, full, width), bf16))
    any_space = pl.BlockSpec(memory_space=pl.ANY)
    vm = pltpu.VMEM
    return pl.pallas_call(
        functools.partial(backward_kernel, images, seq, sizes),
        out_shape=outs,
        in_specs=[pl.BlockSpec(memory_space=pltpu.SMEM)] + [any_space] * len(arrays),
        out_specs=[any_space] * len(outs),
        scratch_shapes=[
            vm((2, 2, RING, every, full), bf16),
            vm((2, 2, 2, every, full), bf16),
            vm((2, 2, every, full), bf16),
            vm((3, every, full), bf16),
            vm((every, full), bf16),
            vm((2, RING, 128, full), bf16),
            vm((2, 1024, full), bf16),
            vm((ROWS, full), bf16),
            vm((ROWS, full), bf16),
            vm((2, ROWS, TILE), bf16),
            vm((2, ROWS, TILE), bf16),
            vm((ROWS, full), f32),
            vm((ROWS, full), f32),
            vm((ROWS, full), f32),
            vm((ROWS, full), bf16),
            vm((ROWS, full), bf16),
            vm((ROWS, full), bf16),
            vm((3, ROWS, full), bf16),
            vm((ROWS, ROWS), bf16),
            vm((ROWS, ROWS), bf16),
            vm((seq, full), bf16),
            vm((6, 8, full), f32),
            vm((8, TILE), f32),
            vm(arrays[0].shape, bf16),
            vm(arrays[0].shape, f32),
            vm((RING, 24, 128), f32),
            vm((4, RING, 24, 128), f32),
            dma((5, RING)),
            dma((5, RING)),
            dma((4, 20)),
            dma((4, 20)),
            dma((2, RING)),
            dma((2, RING)),
            dma((6,)),
            dma((6,)),
            dma((5,)),
            dma((RING, 2)),
            dma((RING, 2)),
            dma((14,)),
            dma((2, 2)),
            dma((2,)),
        ],
        compiler_params=pltpu.CompilerParams(
            collective_id=1, has_side_effects=True, vmem_limit_bytes=60 * 2**20
        ),
    )(mask, *arrays)


def prepare(vectors, w_attn, qv_bias, w_out, b_fc1, w_fc2):
    full, _, width = w_attn.shape
    attn = jnp.transpose(w_attn, (1, 2, 0)).reshape(3, 8, 32, full).transpose(1, 0, 2, 3)
    qv = qv_bias.reshape(2, 4, 2, 32).transpose(0, 2, 1, 3).reshape(-1)
    start, small = 0, 0
    for v in (*vectors, qv, b_fc1):
        small = small + jnp.pad(v, (start, 4096 - start - v.shape[0]))
        start += v.shape[0]
    return small.reshape(-1, 128), attn, w_out.reshape(8, 32, full), w_fc2.reshape(8, -1, full)


def image_local(
    tokens,
    image_mask,
    ln1_gain,
    first_norm_bias,
    w_attn,
    qv_bias,
    w_out,
    b_out,
    ln2_gain,
    second_norm_bias,
    w_fc1,
    b_fc1,
    w_fc2,
    b_fc2,
    cotangent,
):
    width = tokens.shape[2]
    full = width * RING
    vectors = (ln1_gain, first_norm_bias, b_out, ln2_gain, second_norm_bias, b_fc2)
    small, attn, out, fc2 = prepare(vectors, w_attn, qv_bias, w_out, b_fc1, w_fc2)
    dy, small, *rest = forward(tokens, cotangent, small, attn, out, w_fc1, fc2)
    fulls, kept, fc1 = rest[:4], rest[4:12], rest[12]
    block_out, input_grad, sums, s2, _, so, _, t1, ta = backward(
        image_mask, small, *kept, dy, attn, out, fc1, fc2, *fulls
    )
    pairs = sums.reshape(12, width)
    grad_qv = pairs[6:8].reshape(2, 2, 4, 32).transpose(0, 2, 1, 3).reshape(2, width)
    return (
        block_out,
        input_grad,
        pairs[0],
        pairs[1],
        jnp.transpose(wide(ta), (1, 0, 2)),
        grad_qv,
        wide(so).reshape(width, full),
        pairs[2],
        pairs[3],
        pairs[4],
        wide(t1),
        pairs[8:].reshape(-1),
        wide(s2).reshape(-1, full),
        pairs[5],
    )


def solution(mesh):
    in_specs = (
        P("dp", None, "tensor"),
        P("dp"),
        P("tensor"),
        P("tensor"),
        P(None, None, "tensor"),
        P(None, "tensor"),
        P("tensor", None),
        P("tensor"),
        P("tensor"),
        P("tensor"),
        P(None, "tensor"),
        P("tensor"),
        P("tensor", None),
        P("tensor"),
        P("dp", None, "tensor"),
    )
    out_specs = (
        P("dp", None, "tensor"),
        P("dp", None, "tensor"),
        P("tensor"),
        P("tensor"),
        P(None, None, "tensor"),
        P(None, "tensor"),
        P("tensor", None),
        P("tensor"),
        P("tensor"),
        P("tensor"),
        P(None, "tensor"),
        P("tensor"),
        P("tensor", None),
        P("tensor"),
    )
    owners = mesh.shape["dp"] == 8 and mesh.shape["tensor"] == RING

    def block(*arrays):
        images = arrays[0].shape[0] // mesh.shape["dp"]
        body = image_local if owners and images < RING else local
        return jax.shard_map(
            body, mesh=mesh, in_specs=in_specs, out_specs=out_specs, check_vma=False
        )(*arrays)

    return block
```

```python
import functools

import jax
import jax.numpy as jnp
from jax import lax
from jax.experimental import pallas as pl
from jax.experimental.pallas import tpu as pltpu
from jax.sharding import PartitionSpec as P

MODEL_WIDTH = 1024
HD = 64


EPS = 1e-05


def norm_stats(value):
    total, squares = lax.psum((jnp.sum(value, 1), jnp.sum(value * value, 1)), "tensor")
    middle = total / MODEL_WIDTH
    spread = squares / MODEL_WIDTH - middle * middle
    return (middle[:, None], lax.rsqrt(spread + EPS)[:, None])


def layer_norm_reverse(incoming_gradient, normalized_input, norm_gain, inverse_deviation):
    gain_scaled_gradient = incoming_gradient * norm_gain
    first_norm_result, second_norm_result = lax.psum(
        (jnp.sum(gain_scaled_gradient, 1), jnp.sum(gain_scaled_gradient * normalized_input, 1)),
        "tensor",
    )
    return inverse_deviation * (
        gain_scaled_gradient
        - first_norm_result[:, None] / MODEL_WIDTH
        - normalized_input * second_norm_result[:, None] / MODEL_WIDTH
    )


def spread_features(value):
    return lax.all_gather(value, "tensor", axis=1, tiled=True)


def settle_sums(value):
    return lax.psum_scatter(value, "tensor", scatter_dimension=1, tiled=True)


def pair_dot(left, right):
    return lax.dot_general(
        left, right, (((0,), (0,)), ((), ())), preferred_element_type=jnp.float32
    )


def back_dot(left, right):
    return lax.dot_general(
        left, right, (((1,), (1,)), ((), ())), preferred_element_type=jnp.float32
    )


def attend_image(blocks):
    query, keys, values = blocks
    scale = HD ** (-0.5)
    scores = jnp.einsum("qhd,khd->hqk", query, keys, preferred_element_type=jnp.float32) * scale
    top = jnp.max(scores, -1, keepdims=True)
    expo = jnp.exp(scores - top)
    total = jnp.sum(expo, -1, keepdims=True)
    probs = expo / total
    log_total = top[..., 0] + jnp.log(total[..., 0])
    context = jnp.einsum(
        "hqk,khd->qhd", probs.astype(jnp.bfloat16), values, preferred_element_type=jnp.float32
    )
    return (context.astype(jnp.bfloat16), log_total)


def attend_back(blocks):
    query, keys, values, log_total, dcontext = blocks
    scale = HD ** (-0.5)
    scores = jnp.einsum("qhd,khd->hqk", query, keys, preferred_element_type=jnp.float32) * scale
    probs = jnp.exp(scores - log_total[..., None])
    dvalues = jnp.einsum(
        "hqk,qhd->khd", probs.astype(jnp.bfloat16), dcontext, preferred_element_type=jnp.float32
    )
    dprobs = jnp.einsum("qhd,khd->hqk", dcontext, values, preferred_element_type=jnp.float32)
    delta = jnp.sum(probs * dprobs, -1, keepdims=True)
    dscores = (probs * (dprobs - delta)).astype(jnp.bfloat16)
    dquery = jnp.einsum("hqk,khd->qhd", dscores, keys, preferred_element_type=jnp.float32) * scale
    dkeys = jnp.einsum("hqk,qhd->khd", dscores, query, preferred_element_type=jnp.float32) * scale
    return jnp.stack([dquery, dkeys, dvalues], 1).astype(jnp.bfloat16)


def local(
    tokens,
    image_mask,
    ln1_gain,
    first_norm_bias,
    w_attn,
    qv_bias,
    w_out,
    b_out,
    ln2_gain,
    second_norm_bias,
    w_fc1,
    b_fc1,
    w_fc2,
    b_fc2,
    cotangent,
):
    images, seq, width_dev = tokens.shape
    rows = images * seq
    heads_dev = width_dev // HD
    mask_rows = jnp.repeat(image_mask.astype(jnp.float32), seq)[:, None]
    first_norm_gain = ln1_gain.astype(jnp.float32)
    second_norm_gain = ln2_gain.astype(jnp.float32)
    block_inputs = tokens.astype(jnp.float32).reshape(rows, width_dev)
    first_midpoint_state, first_inverse_deviation = norm_stats(block_inputs)
    first_normalized_input = (block_inputs - first_midpoint_state) * first_inverse_deviation
    h1_full = spread_features(
        (first_normalized_input * first_norm_gain + first_norm_bias.astype(jnp.float32)).astype(
            jnp.bfloat16
        )
    )
    qkv = jnp.einsum("nd,dce->nce", h1_full, w_attn, preferred_element_type=jnp.float32)
    bias_rows = qv_bias.astype(jnp.float32)
    bias_full = jnp.stack([bias_rows[0], jnp.zeros_like(bias_rows[0]), bias_rows[1]], 0)
    qkv = (qkv + bias_full).astype(jnp.bfloat16)
    query = qkv[:, 0].reshape(images, seq, heads_dev, HD)
    keys = qkv[:, 1].reshape(images, seq, heads_dev, HD)
    values = qkv[:, 2].reshape(images, seq, heads_dev, HD)
    context, log_total = lax.map(attend_image, (query, keys, values))
    context_flat = context.reshape(rows, width_dev)
    attn = settle_sums(
        jnp.dot(context_flat, w_out, preferred_element_type=jnp.float32)
    ) + b_out.astype(jnp.float32)
    residual_stream_state = block_inputs + attn
    second_midpoint_state, second_inverse_deviation = norm_stats(residual_stream_state)
    second_normalized_input = (
        residual_stream_state - second_midpoint_state
    ) * second_inverse_deviation
    h2_full = spread_features(
        (second_normalized_input * second_norm_gain + second_norm_bias.astype(jnp.float32)).astype(
            jnp.bfloat16
        )
    )
    hidden = jnp.dot(h2_full, w_fc1, preferred_element_type=jnp.float32) + b_fc1.astype(jnp.float32)
    sigma = jax.nn.sigmoid(1.702 * hidden)
    act = (hidden * sigma).astype(jnp.bfloat16)
    mlp = settle_sums(jnp.dot(act, w_fc2, preferred_element_type=jnp.float32)) + b_fc2.astype(
        jnp.float32
    )
    block_out = (
        ((residual_stream_state + mlp) * mask_rows)
        .astype(jnp.bfloat16)
        .reshape(images, seq, width_dev)
    )
    output_gradient = cotangent.astype(jnp.float32).reshape(rows, width_dev) * mask_rows
    dy_full = spread_features(output_gradient.astype(jnp.bfloat16))
    grad_b_fc2 = jnp.sum(output_gradient, 0)
    grad_w_fc2 = pair_dot(act, dy_full)
    dact = back_dot(dy_full, w_fc2)
    dhidden = (dact * (sigma + 1.702 * hidden * sigma * (1.0 - sigma))).astype(jnp.bfloat16)
    grad_b_fc1 = jnp.sum(dhidden, 0, dtype=jnp.float32)
    grad_w_fc1 = pair_dot(h2_full, dhidden)
    second_hidden_gradient = settle_sums(back_dot(dhidden, w_fc1))
    second_norm_gain_gradient = jnp.sum(second_hidden_gradient * second_normalized_input, 0)
    grad_ln2_bias = jnp.sum(second_hidden_gradient, 0)
    residual_gradient = output_gradient + layer_norm_reverse(
        second_hidden_gradient, second_normalized_input, second_norm_gain, second_inverse_deviation
    )
    dattn = residual_gradient.astype(jnp.bfloat16)
    grad_b_out = jnp.sum(dattn, 0, dtype=jnp.float32)
    dattn_full = spread_features(dattn)
    grad_w_out = pair_dot(context_flat, dattn_full)
    dcontext = back_dot(dattn_full, w_out).astype(jnp.bfloat16).reshape(images, seq, heads_dev, HD)
    dqkv = lax.map(attend_back, (query, keys, values, log_total, dcontext))
    dqkv = dqkv.reshape(rows, 3, width_dev)
    grad_w_attn = jnp.einsum("nd,nce->dce", h1_full, dqkv, preferred_element_type=jnp.float32)
    bias_sums = jnp.sum(dqkv, 0, dtype=jnp.float32)
    grad_qv_bias = jnp.stack([bias_sums[0], bias_sums[2]], 0)
    first_hidden_gradient = settle_sums(
        jnp.einsum("nce,dce->nd", dqkv, w_attn, preferred_element_type=jnp.float32)
    )
    first_norm_gain_gradient = jnp.sum(first_hidden_gradient * first_normalized_input, 0)
    grad_ln1_bias = jnp.sum(first_hidden_gradient, 0)
    input_grad = (
        (
            residual_gradient
            + layer_norm_reverse(
                first_hidden_gradient,
                first_normalized_input,
                first_norm_gain,
                first_inverse_deviation,
            )
        )
        .astype(jnp.bfloat16)
        .reshape(images, seq, width_dev)
    )
    (
        first_norm_gain_gradient,
        grad_ln1_bias,
        grad_w_attn,
        grad_qv_bias,
        grad_w_out,
        grad_b_out,
        second_norm_gain_gradient,
        grad_ln2_bias,
        grad_w_fc1,
        grad_b_fc1,
        grad_w_fc2,
        grad_b_fc2,
    ) = lax.psum(
        (
            first_norm_gain_gradient,
            grad_ln1_bias,
            grad_w_attn,
            grad_qv_bias,
            grad_w_out,
            grad_b_out,
            second_norm_gain_gradient,
            grad_ln2_bias,
            grad_w_fc1,
            grad_b_fc1,
            grad_w_fc2,
            grad_b_fc2,
        ),
        "dp",
    )
    return (
        block_out,
        input_grad,
        first_norm_gain_gradient,
        grad_ln1_bias,
        grad_w_attn,
        grad_qv_bias,
        grad_w_out,
        grad_b_out,
        second_norm_gain_gradient,
        grad_ln2_bias,
        grad_w_fc1,
        grad_b_fc1,
        grad_w_fc2,
        grad_b_fc2,
    )


RING = 4


MESH_ID = pl.DeviceIdType.MESH
ROWS = 640
TILE = 512


def low(value):
    return value.astype(jnp.bfloat16)


def wide(value):
    return value.astype(jnp.float32)


def dot_on(left, right, a, b):
    return lax.dot_general(
        left, right, (((a,), (b,)), ((), ())), preferred_element_type=jnp.float32
    )


def turned(p, q):
    return sum(lax.rem(p // bit + q // bit, 2) * bit for bit in (1, 2, 4))


def remote(src, dst, send, recv, target):
    return pltpu.make_async_remote_copy(
        src_ref=src,
        dst_ref=dst,
        send_sem=send,
        recv_sem=recv,
        device_id=target,
        device_id_type=MESH_ID,
    )


def rows_at(start, size):
    return pl.ds(pl.multiple_of(start, 16), size)


class Place:
    def __init__(self, images):
        self.p = lax.axis_index("dp")
        self.z = lax.axis_index("tensor")
        self.core = lax.rem(self.p, 2)
        self.images = images
        self.shifts = [lax.rem(self.z + d, RING) for d in range(RING)]
        self.slot = self.z - self.core
        self.live = self.holds(self.z)

    def holds(self, plane):
        return (plane - self.core >= 0) & (plane - self.core < self.images)

    def near(self, q):
        return (turned(self.p, q), self.z)

    def greet(self):
        barrier = pltpu.get_barrier_semaphore()
        for d in range(1, RING):
            pl.semaphore_signal(
                barrier, inc=1, device_id=(self.p, self.shifts[d]), device_id_type=MESH_ID
            )
        for q in (1, 2, 4, 6):
            pl.semaphore_signal(barrier, inc=1, device_id=self.near(q), device_id_type=MESH_ID)
        pl.semaphore_wait(barrier, 7)


def weight_copies(place, pieces, full, chunk, target, sem, c=0, q=0):
    if chunk >= 2:
        yield pltpu.make_async_copy(
            pieces.at[turned(place.p, q)], target.at[pl.ds(0, 128)], sem
        )
        yield pltpu.make_async_copy(full.at[q], target.at[pl.ds(128, 384)], sem)
        return
    for half in range(2):
        source = full.at[c, half] if chunk == 0 else full.at[half]
        yield pltpu.make_async_copy(source, target.at[pl.ds(half * TILE + 128, 384)], sem)
        for head in range(4):
            piece = turned(place.p, 2 * head + half)
            own = pieces.at[c, piece] if chunk == 0 else pieces.at[piece]
            yield pltpu.make_async_copy(own, target.at[pl.ds(half * TILE + head * 32, 32)], sem)


def pair_heads(one, two):
    lane = lax.broadcasted_iota(jnp.int32, (1, 128), 1)
    return (
        jnp.where(lane < 64, one, low(pltpu.roll(wide(two), 64, 1))),
        jnp.where(lane < 64, low(pltpu.roll(wide(one), 64, 1)), two),
    )


def head_mask(h):
    lane = lax.broadcasted_iota(jnp.int32, (1, 128), 1)
    return lax.rem(lane, 64) // 32 == h


def group_lanes(k):
    return [pl.ds(pl.multiple_of(k * 128 + half * TILE, 128), 128) for half in range(2)]


def split_heads(source, target, k):
    lanes = group_lanes(k)
    target[0], target[1] = pair_heads(source[:, lanes[0]], source[:, lanes[1]])


def join_heads(source, target, k):
    lanes = group_lanes(k)
    target[:, lanes[0]], target[:, lanes[1]] = pair_heads(source[0], source[1])


def turn_heads(sides, p):
    odd = lax.rem(p, 2) == 1
    sides = [jnp.where(odd, sides[1], sides[0]), jnp.where(odd, sides[0], sides[1])]
    lane = lax.broadcasted_iota(jnp.int32, (8, 128), 1)
    out = []
    for v in sides:
        near = jnp.where(lax.rem(lane // 32, 2) == 0, pltpu.roll(v, 96, 1), pltpu.roll(v, 32, 1))
        v = jnp.where(lax.rem(p // 2, 2) == 1, near, v)
        out.append(jnp.where(p // 4 == 1, pltpu.roll(v, 64, 1), v))
    return out


def feature(small_f, z, i):
    parts = [
        small_f[lax.rem(z + RING - j, RING), row : row + 1]
        for j in range(RING)
        for row in (2 * i, 2 * i + 1)
    ]
    return jnp.concatenate(parts, 1)


class Gather:
    def __init__(self, place, pieces, fulls, sems):
        self.at = place
        self.p, self.z = place.p, place.z
        self.pieces = pieces
        self.fulls = fulls
        self.z_send, self.send, self.recv = sems
        z = self.z
        self.order = (
            jnp.where(z == 0, 3, 1),
            jnp.where((z == 0) | (z == 3), 2, 3),
            jnp.where(z == 0, 1, jnp.where(z == 3, 3, 2)),
        )

    def place(self, chunk, q, k, start=0, size=None):
        full = self.fulls[chunk]
        size = self.pieces[chunk].shape[-2] if size is None else size
        start = (k - 1) * 128 + start
        if chunk >= 2:
            return full.at[q, rows_at(start, size)]
        at = rows_at(start + (q // 2) * 32, size)
        return full.at[:, q % 2, at] if chunk == 0 else full.at[q % 2, at]

    def part(self, chunk, q, k, side):
        half = self.pieces[chunk].shape[-2] // 2
        return self.place(chunk, q, k, side * half, half)

    def up(self, chunk, k, source):
        return remote(
            source,
            self.place(chunk, 0, k + 1),
            self.z_send.at[chunk, k, 0],
            self.recv.at[chunk, k + 1, 0],
            (self.p, jnp.minimum(self.z + 1, RING - 1)),
        )

    def down(self, chunk, k, source):
        return remote(
            source,
            self.place(chunk, 0, k - 1),
            self.z_send.at[chunk, lax.rem(k, RING), 1],
            self.recv.at[chunk, k - 1, 0],
            (self.p, jnp.maximum(self.z - 1, 0)),
        )

    def own(self, chunk):
        pieces = self.pieces[chunk]
        return pieces.at[:, self.p] if chunk == 0 else pieces.at[self.p]

    def z_start(self, chunk):
        piece = self.own(chunk)
        pl.when(self.z < RING - 1)(self.up(chunk, 0, piece).start)
        pl.when(self.z > 0)(self.down(chunk, RING, piece).start)

    def z_sent(self, chunk):
        piece = self.own(chunk)
        pl.when(self.z < RING - 1)(self.up(chunk, 0, piece).wait_send)
        pl.when(self.z > 0)(self.down(chunk, RING, piece).wait_send)
        for k in (1, 2, 3):
            here = self.place(chunk, 0, k)
            if k < 3:
                pl.when((self.z >= k) & (self.z < RING - 1))(self.up(chunk, k, here).wait_send)
            if k > 1:
                pl.when((self.z < k) & (self.z > 0))(self.down(chunk, k, here).wait_send)

    def plane(self, chunk, k, source, target):
        return remote(
            self.place(chunk, source, k),
            self.place(chunk, target, k),
            self.send.at[chunk, k, target],
            self.recv.at[chunk, k, target],
            self.at.near(source ^ target),
        )

    def corner(self, chunk, k, side):
        source, flip = ((4, 2), (2, 4))[side]
        return remote(
            self.part(chunk, source, k, side),
            self.part(chunk, 6, k, side),
            self.send.at[chunk, k, (6, 8)[side]],
            self.recv.at[chunk, k, (6, 8)[side]],
            self.at.near(flip),
        )

    def spread(self, chunk, i):
        k = self.order[i]
        here = self.place(chunk, 0, k)
        remote(
            here, here, self.send.at[chunk, k, 0], self.recv.at[chunk, k, 0], self.at.near(1)
        ).wait_recv()
        pl.when((self.z >= k) & (self.z < RING - 1))(self.up(chunk, k, here).start)
        pl.when((self.z < k) & (self.z > 0))(self.down(chunk, k, here).start)
        for target in (2, 4, 1):
            self.plane(chunk, k, 0, target).start()

    def relay(self, chunk, i):
        k = self.order[i]
        self.plane(chunk, k, 0, 4).wait_recv()
        self.corner(chunk, k, 0).start()
        self.plane(chunk, k, 0, 2).wait_recv()
        self.corner(chunk, k, 1).start()
        self.plane(chunk, k, 4, 5).start()
        self.plane(chunk, k, 2, 3).start()

    def share(self, chunk, i):
        k = self.order[i]
        self.corner(chunk, k, 0).wait_recv()
        self.corner(chunk, k, 1).wait_recv()
        self.plane(chunk, k, 6, 7).start()

    def whole(self, chunk):
        for k in range(1, RING):
            for target in (1, 3, 5, 7):
                self.plane(chunk, k, target - 1, target).wait_recv()

    def sent(self, chunk):
        self.z_sent(chunk)
        for k in range(1, RING):
            for source, target in ((0, 2), (0, 4), (0, 1), (4, 5), (2, 3), (6, 7)):
                self.plane(chunk, k, source, target).wait_send()
            self.corner(chunk, k, 0).wait_send()
            self.corner(chunk, k, 1).wait_send()


class Rows:
    def __init__(self, place, source, target, send, recv, local):
        self.at = place
        self.source, self.target = source, target
        self.send, self.recv, self.local = send, recv, local
        self.width = source.shape[2]

    def columns(self):
        return pl.ds(pl.multiple_of(self.at.z * self.width, self.width), self.width)

    def copy(self, d):
        dest = self.at.shifts[d]
        return remote(
            self.source.at[jnp.clip(dest - self.at.core, 0, self.at.images - 1)],
            self.target.at[:, self.columns()],
            self.send.at[d],
            self.recv.at[d],
            (self.at.p, dest),
        )

    def own(self):
        return pltpu.make_async_copy(
            self.source.at[jnp.clip(self.at.slot, 0, self.at.images - 1)],
            self.target.at[:, self.columns()],
            self.local,
        )

    def start(self):
        self.own().start()
        for d in range(1, RING):
            pl.when(self.at.holds(self.at.shifts[d]))(self.copy(d).start)

    def here(self):
        self.own().wait()
        for d in range(1, RING):
            pl.when(self.at.live)(self.copy(d).wait_recv)

    def sent(self):
        for d in range(1, RING):
            pl.when(self.at.holds(self.at.shifts[d]))(self.copy(d).wait_send)


def norm_rows(value, gain, shift):
    middle = jnp.mean(value, 1, keepdims=True)
    spread = jnp.mean(value * value, 1, keepdims=True) - middle * middle
    return (value - middle) * lax.rsqrt(spread + EPS) * gain + shift


def forward_kernel(images, seq, *refs):
    (
        tokens,
        cotangent,
        small,
        attn_in,
        out_in,
        fc1_raw,
        fc2_in,
        dy_full,
        small_full,
        attn_full,
        out_full,
        fc1_full,
        fc2_full,
        x_rows_out,
        h1_out,
        qkv_out,
        ctx_out,
        r_out,
        h2_out,
        act_out,
        slope_out,
        fc1_in,
        x_full,
        x_in,
        x_v,
        h1_v,
        h2_v,
        qkv_v,
        ctx_v,
        r_v,
        w_v,
        act_v,
        slope_v,
        small_v,
        small_f,
        bias_v,
        pair_v,
        row_send,
        row_recv,
        small_send,
        small_recv,
        z_send,
        unit_send,
        unit_recv,
        local_sem,
        w_sem,
        tile_sem,
        out_sem,
    ) = refs
    at = Place(images)
    p, z = at.p, at.z
    g = Gather(
        at,
        (attn_in, out_in, fc1_in, fc2_in),
        (attn_full, out_full, fc1_full, fc2_full),
        (z_send, unit_send, unit_recv),
    )
    x_rows = Rows(at, tokens, x_full, row_send.at[0], row_recv.at[0], local_sem.at[0])
    dy_rows = Rows(at, cotangent, dy_full, row_send.at[1], row_recv.at[1], local_sem.at[1])
    full = x_full.shape[1]

    def small_copy(d):
        return remote(
            small, small_full.at[d], small_send.at[d], small_recv.at[d], (p, at.shifts[d])
        )

    small_own = pltpu.make_async_copy(small, small_full.at[0], local_sem.at[2])

    fc1_load = pltpu.make_async_copy(fc1_raw, w_v.at[0], local_sem.at[6])
    fc1_load.start()
    at.greet()
    g.z_start(0)
    for d in range(1, RING):
        small_copy(d).start()
    small_own.start()

    g.z_start(1)
    fc1_load.wait()
    for i in range(8):
        rows = slice(i * 128, (i + 1) * 128)
        w_v[1, rows] = w_v[0, :, rows].T
        pltpu.make_async_copy(w_v.at[1, pl.ds(i * 128, 128)], fc1_in.at[i], local_sem.at[5]).start()
    g.spread(0, 0)
    x_rows.start()
    g.spread(0, 1)
    g.spread(0, 2)
    pltpu.make_async_copy(w_v.at[1], w_v.at[1], local_sem.at[5]).wait()
    for d in range(1, RING):
        small_copy(d).wait()
    small_own.wait()
    small_load = pltpu.make_async_copy(small_full, small_v, local_sem.at[3])
    small_load.start()
    x_rows.here()
    x_load = pltpu.make_async_copy(x_full, x_in, local_sem.at[4])
    x_load.start()
    small_load.wait()

    small_f[...] = wide(small_v[...])
    gain, shift = feature(small_f, z, 0), feature(small_f, z, 1)
    for c, row in ((0, 12), (2, 14)):
        for k in range(RING):
            sides = [
                jnp.broadcast_to(small_f[k, row + half : row + half + 1], (8, 128))
                for half in range(2)
            ]
            for half, side in enumerate(turn_heads(sides, p)):
                start = half * TILE + k * 128
                bias_v[c : c + 1, start : start + 128] = side[0:1]
    bias_v[1:2] = jnp.zeros((1, full), jnp.float32)
    x_load.wait()

    def first_norm_of(block, value):
        value = jnp.where(at.live, wide(value), 0.0)
        x_v[block] = low(value)
        h1_v[block] = low(norm_rows(value, gain, shift))

    def first_norm(i, _):
        block = rows_at(i * 64, 64)
        first_norm_of(block, x_in[block])
        return 0

    whole_blocks = seq // 64 * 64
    lax.fori_loop(0, seq // 64, first_norm, 0)
    rest = wide(x_in[whole_blocks:seq])
    rest = jnp.concatenate([rest, jnp.zeros((ROWS - seq, full), jnp.float32)], 0)
    first_norm_of(slice(whole_blocks, ROWS), rest)
    saves = [
        pltpu.make_async_copy(x_v, x_rows_out, out_sem.at[0]),
        pltpu.make_async_copy(h1_v, h1_out, out_sem.at[1]),
    ]
    for s in saves:
        s.start()

    for i in range(3):
        g.relay(0, i)
        g.spread(1, i)
        if i == 1:
            g.z_start(2)
        if i:
            g.share(0, i - 1)
    g.share(0, 2)
    g.whole(0)

    def tile_load(chunk, c, slot):
        return list(
            weight_copies(
                at,
                (attn_in, out_in)[chunk],
                (attn_full, out_full)[chunk],
                chunk,
                w_v.at[slot],
                w_sem.at[slot],
                c,
            )
        )

    def go(copies):
        for copy in copies:
            copy.start()

    def arrive(copies):
        for copy in copies:
            copy.wait()

    def filled(slot):
        pltpu.make_async_copy(w_v.at[slot], w_v.at[slot], w_sem.at[slot]).wait()

    loads = [tile_load(0, c, c % 2) for c in range(3)] + [tile_load(1, 0, 1)]
    go(loads[0])
    go(loads[1])
    steps = [
        lambda: g.spread(2, 0),
        lambda: g.relay(1, 0),
        lambda: g.relay(1, 1),
    ]
    for c in range(3):
        filled(c % 2)

        def project(i, _, c=c):
            block = rows_at(i * TILE, TILE)
            out = dot_on(h1_v[...], w_v[c % 2, block], 1, 1)
            lanes = pl.ds(pl.multiple_of(i * TILE, TILE), TILE)
            qkv_v[c, :, lanes] = low(out + bias_v[c : c + 1, lanes])
            return 0

        lax.fori_loop(0, 2, project, 0)
        if c == 0:
            go(loads[2])
        steps[c]()
    save = pltpu.make_async_copy(qkv_v, qkv_out, out_sem.at[2])
    save.start()
    saves.append(save)

    key = lax.broadcasted_iota(jnp.int32, (ROWS, 1), 0)

    def attend(k, _):
        for c in range(3):
            split_heads(qkv_v.at[c], pair_v.at[c], k)
        for pair in range(2):
            keys, values = pair_v[1, pair], pair_v[2, pair]
            for r in range(ROWS // 128):
                block = slice(r * 128, (r + 1) * 128)
                query = pair_v[0, pair, block] * jnp.bfloat16(HD ** (-0.5))
                out = None
                for h in range(2):
                    mask = head_mask(h)
                    scores = dot_on(keys, jnp.where(mask, query, jnp.bfloat16(0)), 1, 1)
                    scores = jnp.where(key < seq, scores, -1e30)
                    expo = jnp.exp(scores - jnp.max(scores, 0, keepdims=True))
                    probs = low(expo * (1.0 / jnp.sum(expo, 0, keepdims=True)))
                    part = dot_on(probs, values, 0, 0)
                    out = part if out is None else jnp.where(mask, part, out)
                pair_v[0, pair, block] = low(out)
        join_heads(pair_v.at[0], ctx_v, k)
        for i in range(4):

            @pl.when(k == i)
            def _():
                for step in attention_steps[i]:
                    step()

        return 0

    attention_steps = [
        [lambda: g.spread(2, 1), lambda: g.z_start(3), lambda: g.relay(1, 2)],
        [lambda: g.spread(2, 2), lambda: g.share(1, 0), lambda: g.share(1, 1)],
        [lambda: g.share(1, 2), lambda: g.relay(2, 0), lambda: g.spread(3, 0)],
        [lambda: g.relay(2, 1), lambda: g.spread(3, 1), dy_rows.start],
    ]
    lax.fori_loop(0, 4, attend, 0)
    g.whole(1)
    go(loads[3])
    save = pltpu.make_async_copy(ctx_v, ctx_out, out_sem.at[3])
    save.start()
    saves.append(save)
    out_bias = feature(small_f, z, 2)
    gain2, shift2 = feature(small_f, z, 3), feature(small_f, z, 4)
    filled(1)
    for i in range(2):
        lanes = slice(i * TILE, (i + 1) * TILE)
        attn = dot_on(ctx_v[...], w_v[1, :, lanes], 1, 0)
        r_v[:, lanes] = wide(x_v[:, lanes]) + (attn + out_bias[:, lanes])
    save = pltpu.make_async_copy(r_v, r_out, out_sem.at[4])
    save.start()
    saves.append(save)
    g.relay(2, 2)
    g.spread(3, 2)
    g.share(2, 0)

    def second_norm(i, _):
        block = rows_at(i * 64, 64)
        h2_v[block] = low(norm_rows(r_v[block], gain2, shift2))
        return 0

    lax.fori_loop(0, ROWS // 64, second_norm, 0)
    save = pltpu.make_async_copy(h2_v, h2_out, out_sem.at[5])
    save.start()
    saves.append(save)
    g.share(2, 1)
    g.relay(3, 0)
    g.share(2, 2)
    g.whole(2)

    def pair_load(i):
        slot = i % 2
        for side in range(2):
            yield from weight_copies(
                at,
                fc1_in,
                fc1_full,
                2,
                w_v.at[slot, pl.ds(side * TILE, TILE)],
                w_sem.at[slot],
                q=2 * i + side,
            )

    def tile_saves(q):
        slot = q % 2
        return [
            pltpu.make_async_copy(act_v.at[slot], act_out.at[q], tile_sem.at[0, slot]),
            pltpu.make_async_copy(slope_v.at[slot], slope_out.at[q], tile_sem.at[1, slot]),
        ]

    pairs = [list(pair_load(i)) for i in range(4)]
    go(pairs[0])
    go(pairs[1])
    steps = [
        [lambda: g.relay(3, 1)],
        [lambda: g.relay(3, 2)],
        [lambda: g.share(3, 0), lambda: g.share(3, 1)],
        [lambda: g.share(3, 2)],
    ]
    for i in range(4):
        filled(i % 2)
        for side in range(2):
            q = 2 * i + side
            if q >= 2:
                arrive(tile_saves(q - 2))
            row = pl.ds(16 + turned(p, q), 1)
            bias = jnp.concatenate([small_f[k, row] for k in range(RING)], 1)
            for j in range(2):
                cols = slice(j * 256, (j + 1) * 256)
                start = side * TILE + j * 256
                u = dot_on(h2_v[...], w_v[i % 2, start : start + 256], 1, 1) + bias[:, cols]
                sg = 1.0 / (1.0 + jnp.exp(-1.702 * u))
                act_v[side, :, cols] = low(u * sg)
                slope_v[side, :, cols] = low(sg + 1.702 * u * sg * (1.0 - sg))
            go(tile_saves(q))
        if i < 2:
            go(pairs[i + 2])
        for step in steps[i]:
            step()
    for q in (6, 7):
        arrive(tile_saves(q))
    arrive(saves)
    g.whole(3)
    dy_rows.here()
    for chunk in range(4):
        g.sent(chunk)
    x_rows.sent()
    dy_rows.sent()


def forward(tokens, cotangent, small, attn_in, out_in, fc1_raw, fc2_in):
    images, rows, width = tokens.shape
    full = RING * width
    bf16 = jnp.bfloat16
    f32 = jnp.float32
    dma = pltpu.SemaphoreType.DMA
    shapes = (
        ((rows, full), bf16),
        ((RING,) + small.shape, bf16),
        ((3, 2, 384, full), bf16),
        ((2, 384, full), bf16),
        ((8, 384, full), bf16),
        ((8, 384, full), bf16),
        ((ROWS, full), bf16),
        ((ROWS, full), bf16),
        ((3, ROWS, full), bf16),
        ((ROWS, full), bf16),
        ((ROWS, full), f32),
        ((ROWS, full), bf16),
        ((8, ROWS, TILE), bf16),
        ((8, ROWS, TILE), bf16),
        (fc2_in.shape, bf16),
        ((rows, full), bf16),
    )
    return pl.pallas_call(
        functools.partial(forward_kernel, images, rows),
        out_shape=[jax.ShapeDtypeStruct(s, d) for s, d in shapes],
        in_specs=[pl.BlockSpec(memory_space=pl.ANY)] * 7,
        out_specs=[pl.BlockSpec(memory_space=pl.ANY)] * len(shapes),
        scratch_shapes=[
            pltpu.VMEM((rows, full), bf16),
            pltpu.VMEM((ROWS, full), bf16),
            pltpu.VMEM((ROWS, full), bf16),
            pltpu.VMEM((ROWS, full), bf16),
            pltpu.VMEM((3, ROWS, full), bf16),
            pltpu.VMEM((ROWS, full), bf16),
            pltpu.VMEM((ROWS, full), f32),
            pltpu.VMEM((2, 1024, full), bf16),
            pltpu.VMEM((2, ROWS, TILE), bf16),
            pltpu.VMEM((2, ROWS, TILE), bf16),
            pltpu.VMEM((RING,) + small.shape, bf16),
            pltpu.VMEM((RING,) + small.shape, f32),
            pltpu.VMEM((8, full), f32),
            pltpu.VMEM((3, 2, ROWS, 128), bf16),
            dma((2, RING)),
            dma((2, RING)),
            dma((RING,)),
            dma((RING,)),
            dma((4, RING, 2)),
            dma((4, RING, 9)),
            dma((4, RING, 9)),
            dma((7,)),
            dma((2,)),
            dma((2, 2)),
            dma((6,)),
        ],
        compiler_params=pltpu.CompilerParams(
            collective_id=0, has_side_effects=True, vmem_limit_bytes=56 * 2**20
        ),
    )(tokens, cotangent, small, attn_in, out_in, fc1_raw, fc2_in)


class Reduce:
    def __init__(self, place, sizes, outs, bufs, sems):
        self.at = place
        self.sizes = sizes
        self.starts = [sum(sizes[:i]) for i in range(4)]
        self.outs = outs
        self.held, self.first, self.second, self.far, self.total, self.stage = bufs
        self.core_send, self.core_recv, self.send, self.recv, self.local = sems[:5]
        self.plane_send, self.plane_recv = sems[5:]

    def rows(self, c):
        return pl.ds(self.starts[c], self.sizes[c])

    def give(self, group, xy, slot):
        y, x = xy // 2, lax.rem(xy, 2)
        at = self.rows(group)
        source = self.stage.at[slot]
        if group == 2:
            source = source.at[:, pl.ds(xy * 32, 32)]
        return remote(
            source,
            self.held.at[y, x, :, at],
            self.core_send.at[group, xy],
            self.core_recv.at[group, xy],
            self.at.near(1),
        )

    def hop(self, source, target, c, i, q):
        return remote(source, target, self.send.at[c, i], self.recv.at[c, i], self.at.near(q))

    def x_copy(self, c, y):
        at = self.rows(c)
        return self.hop(self.held.at[y, 1, 0:2, at], self.first.at[0, y, :, at], c, y, 2)

    def y_copy(self, c, x):
        at = self.rows(c)
        return self.hop(self.held.at[1, x, 2:4, at], self.first.at[1, x, :, at], c, 2 + x, 4)

    def xy_copy(self, c):
        at = self.rows(c)
        return self.hop(self.first.at[0, 1, :, at], self.second.at[0, :, at], c, 4, 4)

    def yx_copy(self, c):
        at = self.rows(c)
        return self.hop(self.first.at[1, 1, :, at], self.second.at[1, :, at], c, 5, 2)

    def z_copy(self, c, k):
        return remote(
            self.second.at[k // 2, k % 2, self.rows(c)],
            self.far.at[k - 1, self.rows(c)],
            self.send.at[c, 5 + k],
            self.recv.at[c, 5 + k],
            (self.at.p, self.at.shifts[RING - k]),
        )

    def out_copy(self, c, q):
        return self.hop(self.total.at[self.rows(c)], self.outs[c].at[self.at.p], c, {1: 9, 2: 10, 4: 11}[q], q)

    def out_here(self, c, q):
        block = self.outs[c].at[turned(self.at.p, q)]
        self.hop(self.total.at[self.rows(c)], block, c, {1: 9, 2: 10, 4: 11}[q], q).wait_recv()

    def corner(self, c, side):
        source, flip = ((4, 2), (2, 4))[side]
        half = self.sizes[c] // 2
        at = pl.ds(side * half, half)
        block = self.outs[c].at[turned(self.at.p, source), at]
        return self.hop(block, block, c, 14 + side, flip)

    def corner_here(self, c):
        half = self.sizes[c] // 2
        for side in range(2):
            block = self.outs[c].at[turned(self.at.p, 6), pl.ds(side * half, half)]
            self.hop(block, block, c, 14 + side, 2).wait_recv()

    def out_own(self, c):
        return pltpu.make_async_copy(
            self.total.at[self.rows(c)], self.outs[c].at[self.at.p], self.local.at[c]
        )

    def share(self, c, q):
        block = self.outs[c].at[turned(self.at.p, q)]
        return self.hop(block, block, c, 16 + q // 2, 1)

    def share_here(self, c, q):
        block = self.outs[c].at[turned(self.at.p, q)]
        theirs = self.outs[c].at[turned(self.at.p, q + 1)]
        self.hop(block, theirs, c, 16 + q // 2, 1).wait_recv()

    def add(self, dest, *sources):
        def body(i, _):
            at = rows_at(i * 16, 16)
            value = wide(sources[0][at])
            for s in sources[1:]:
                value = value + wide(s[at])
            dest[at] = low(value)
            return 0

        lax.fori_loop(0, dest.shape[0] // 16, body, 0)

    def turn(self, c):
        at = self.rows(c)
        self.x_copy(c, 1).wait_recv()
        for k in range(2):
            block = self.first.at[0, 1, k, at]
            self.add(block, block, self.held.at[1, 0, k, at])
        self.xy_copy(c).start()
        self.y_copy(c, 1).wait_recv()
        for k in range(2):
            block = self.first.at[1, 1, k, at]
            self.add(block, block, self.held.at[0, 1, 2 + k, at])
        self.yx_copy(c).start()

    def rise(self, c):
        at = self.rows(c)
        self.x_copy(c, 0).wait_recv()
        self.xy_copy(c).wait_recv()
        for k in range(2):
            block = self.second.at[0, k, at]
            self.add(block, block, self.first.at[0, 0, k, at], self.held.at[0, 0, k, at])
        self.z_copy(c, 1).start()
        self.y_copy(c, 0).wait_recv()
        self.yx_copy(c).wait_recv()
        for k in range(2):
            block = self.second.at[1, k, at]
            self.add(block, block, self.first.at[1, 0, k, at], self.held.at[0, 0, 2 + k, at])
            self.z_copy(c, 2 + k).start()

    def settle(self, c):
        at = self.rows(c)
        for k in range(1, RING):
            self.z_copy(c, k).wait_recv()
        self.add(
            self.total.at[at], self.second.at[0, 0, at], *(self.far.at[k, at] for k in range(3))
        )
        self.out_own(c).start()
        for q in (2, 4, 1):
            self.out_copy(c, q).start()

    def relay(self, c):
        self.out_here(c, 4)
        self.corner(c, 0).start()
        self.out_here(c, 2)
        self.corner(c, 1).start()
        for q in (2, 4):
            self.share(c, q).start()

    def last(self, c):
        self.corner_here(c)
        self.share(c, 6).start()

    def whole(self, c):
        self.out_own(c).wait()
        self.out_here(c, 1)
        for q in (2, 4, 6):
            self.share_here(c, q)

    def give_plane(self, k, slot, y):
        return remote(
            self.stage.at[slot, pl.ds(2 * y, 2), pl.ds(0, self.sizes[3])],
            self.held.at[y, :, k, self.rows(3)],
            self.core_send.at[3 + y, k],
            self.core_recv.at[3 + y, k],
            self.at.near(1),
        )

    def plane_hop(self, source, target, k, i, q):
        return remote(
            source, target, self.plane_send.at[k, i], self.plane_recv.at[k, i], self.at.near(q)
        )

    def plane_first(self, k):
        at, side = self.rows(3), k // 2
        source = self.held.at[:, 1, k, at] if side == 0 else self.held.at[1, :, k, at]
        return self.plane_hop(source, self.first.at[side, :, k % 2, at], k, 0, (2, 4)[side])

    def plane_second(self, k):
        at, side = self.rows(3), k // 2
        return self.plane_hop(
            self.first.at[side, 1, k % 2, at],
            self.second.at[side, k % 2, at],
            k,
            1,
            (4, 2)[side],
        )

    def plane_turn(self, k):
        at, side = self.rows(3), k // 2
        self.plane_first(k).wait_recv()
        block = self.first.at[side, 1, k % 2, at]
        own = self.held.at[1, 0, k, at] if side == 0 else self.held.at[0, 1, k, at]
        self.add(block, block, own)
        self.plane_second(k).start()

    def plane_rise(self, k):
        at, side = self.rows(3), k // 2
        self.plane_second(k).wait_recv()
        block = self.second.at[side, k % 2, at]
        self.add(block, block, self.first.at[side, 0, k % 2, at], self.held.at[0, 0, k, at])
        if k:
            self.z_copy(3, k).start()

    def finish(self, c):
        for q in (2, 4, 6):
            self.share(c, q).wait_send()
        if c < 3:
            for i in range(2):
                self.x_copy(c, i).wait_send()
                self.y_copy(c, i).wait_send()
            self.xy_copy(c).wait_send()
            self.yx_copy(c).wait_send()
        else:
            for k in range(RING):
                self.plane_first(k).wait_send()
                self.plane_second(k).wait_send()
        for k in range(1, RING):
            self.z_copy(c, k).wait_send()
        for q in (2, 4, 1):
            self.out_copy(c, q).wait_send()
        for side in range(2):
            self.corner(c, side).wait_send()


class Return:
    def __init__(self, place, source, target, send, recv):
        self.at = place
        self.source, self.target = source, target
        self.send, self.recv = send, recv
        self.width = target.shape[2]

    def pair(self, plane):
        columns = pl.ds(pl.multiple_of(plane * self.width, self.width), self.width)
        slot = jnp.clip(self.at.slot, 0, self.at.images - 1)
        return self.source.at[:, columns], self.target.at[slot]

    def copy(self, d):
        source, target = self.pair(self.at.shifts[d])
        return remote(
            source, target, self.send.at[d], self.recv.at[d], (self.at.p, self.at.shifts[d])
        )

    def own(self):
        return pltpu.make_async_copy(*self.pair(self.at.z), self.send.at[0])

    def start(self):
        pl.when(self.at.live)(self.own().start)
        for d in range(1, RING):
            pl.when(self.at.live)(self.copy(d).start)

    def sent(self):
        pl.when(self.at.live)(self.own().wait)
        for d in range(1, RING):
            pl.when(self.at.live)(self.copy(d).wait_send)

    def here(self):
        for d in range(1, RING):
            other = lax.rem(self.at.z + RING - d, RING)
            pl.when(self.at.holds(other))(self.copy(d).wait_recv)


def norm_parts(value):
    middle = jnp.mean(value, 1, keepdims=True)
    spread = jnp.mean(value * value, 1, keepdims=True) - middle * middle
    inverse = lax.rsqrt(spread + EPS)
    return (value - middle) * inverse, inverse


def norm_reverse(gradient, normalized, gain, inverse):
    scaled = gradient * gain
    first = jnp.mean(scaled, 1, keepdims=True)
    second = jnp.mean(scaled * normalized, 1, keepdims=True)
    return inverse * (scaled - first - normalized * second)


def backward_kernel(images, seq, sizes, *refs):
    (
        mask_in,
        small_full,
        x_in,
        h1_in,
        qkv_in,
        ctx_in,
        r_in,
        h2_in,
        act_in,
        slope_in,
        dy_in,
        attn_in,
        out_in,
        fc1_in,
        fc2_in,
        attn_full,
        out_full,
        fc1_full,
        fc2_full,
        block_out,
        grad_out,
        vector_out,
        s2,
        s1,
        so,
        sa,
        t1,
        ta,
        held,
        first,
        second,
        far,
        total,
        stage,
        w_v,
        dy_v,
        h_v,
        act_v,
        du_v,
        mlp_v,
        dh_v,
        r_v,
        da_v,
        ctx_v,
        dctx_v,
        qkv_v,
        p_v,
        ds_v,
        blk_v,
        sums_v,
        dus_v,
        small_v,
        small_f,
        vec,
        vec_far,
        core_send,
        core_recv,
        send,
        recv,
        row_send,
        row_recv,
        vec_send,
        vec_recv,
        local_sem,
        plane_send,
        plane_recv,
        load_sem,
        tile_sem,
        w_sem,
    ) = refs
    at = Place(images)
    p, z = at.p, at.z
    full = x_in.shape[1]
    quarter = full // RING
    done = seq // 32 * 32
    red = Reduce(
        at,
        sizes,
        (s2, s1, so, sa),
        (held, first, second, far, total, stage),
        (core_send, core_recv, send, recv, local_sem, plane_send, plane_recv),
    )
    blocks_back = Return(at, blk_v, block_out, row_send.at[0], row_recv.at[0])
    grads_back = Return(at, blk_v, grad_out, row_send.at[1], row_recv.at[1])

    def load(source, target, i):
        return pltpu.make_async_copy(source, target, load_sem.at[i])

    dy_load = load(dy_in, blk_v, 0)
    h2_load = load(h2_in, h_v, 1)
    r_load = load(r_in, r_v, 2)
    ctx_load = load(ctx_in, ctx_v, 3)
    qkv_load = load(qkv_in, qkv_v, 4)
    small_load = load(small_full, small_v, 5)
    h1_load = load(h1_in, h_v, 6)
    x_load = load(x_in, dy_v, 7)

    def tile_loads(q, slot):
        yield pltpu.make_async_copy(act_in.at[q], act_v.at[slot], tile_sem.at[0, slot])
        yield pltpu.make_async_copy(slope_in.at[q], du_v.at[slot], tile_sem.at[1, slot])
        for side, (pieces, whole) in enumerate(((fc1_in, fc1_full), (fc2_in, fc2_full))):
            yield from weight_copies(
                at, pieces, whole, 2, w_v.at[slot, pl.ds(side * TILE, TILE)], w_sem.at[slot], q=q
            )

    def matrix_loads(chunk, c, slot):
        pieces, whole = ((attn_in, attn_full), (out_in, out_full))[chunk]
        return weight_copies(at, pieces, whole, chunk, w_v.at[slot], w_sem.at[slot], c)

    def go(copies):
        for copy in copies:
            copy.start()

    def filled(slot):
        pltpu.make_async_copy(w_v.at[slot], w_v.at[slot], w_sem.at[slot]).wait()

    def turn_of(i):
        return jnp.where(i == 0, 3, jnp.where(i == 1, 1, jnp.where(i == 2, 2, 0)))

    dy_load.start()
    go(tile_loads(7, 0))
    h2_load.start()
    at.greet()
    go(tile_loads(6, 1))
    small_load.start()
    r_load.start()
    ctx_load.start()
    qkv_load.start()

    sums_v[...] = jnp.zeros_like(sums_v)
    mask = mask_in[jnp.clip(at.slot, 0, images - 1)].astype(jnp.float32)
    dy_load.wait()

    def masked(value):
        return jnp.where(at.live, wide(value), 0.0) * mask

    def mask_rows(i, _):
        block = rows_at(i * 32, 32)
        dy_v[block] = low(masked(blk_v[block]))
        return 0

    lax.fori_loop(0, done // 32, mask_rows, 0)
    rest = jnp.zeros((ROWS - seq, full), jnp.float32)
    dy_v[done:] = low(jnp.concatenate([masked(blk_v[done:seq]), rest], 0))
    h2_load.wait()

    def halves(body):
        lax.fori_loop(0, 2, lambda j, _: (body(pl.ds(pl.multiple_of(j * TILE, TILE), TILE)), 0)[1], 0)

    def keep(group, xy, left, right):
        y, x = xy // 2, lax.rem(xy, 2)
        red.give(group, xy, 0).wait_recv()
        at_rows = red.rows(group)

        def body(cols):
            grad = dot_on(left[...], right[:, cols], 0, 0)
            for k in range(RING):
                old = wide(held[y, x, k, at_rows, cols])
                held[y, x, k, at_rows, cols] = low(old + grad[k * 128 : (k + 1) * 128])

        halves(body)
        pl.when(x == 1)(red.x_copy(group, y).start)
        pl.when(y == 1)(red.y_copy(group, x).start)

    def stage_fill(slot, left, right):
        def body(cols):
            grad = low(dot_on(left[...], right[:, cols], 0, 0))
            for k in range(RING):
                stage[slot, k, :, cols] = grad[k * 128 : (k + 1) * 128]

        halves(body)

    mlp_v[...] = jnp.zeros_like(mlp_v)
    dh_v[...] = jnp.zeros_like(dh_v)

    def hidden_tile(i, core):
        slot = 1 - core
        xy = turn_of(i)
        q = 2 * xy + core
        pltpu.make_async_copy(act_in.at[q], act_v.at[slot], tile_sem.at[0, slot]).wait()
        if core:
            pl.when(i > 0)(red.give(0, turn_of(i - 1), 0).wait_send)
            stage_fill(0, act_v.at[slot], dy_v)
            red.give(0, xy, 0).start()
        else:
            keep(0, xy, act_v.at[slot], dy_v)
        pltpu.make_async_copy(slope_in.at[q], du_v.at[slot], tile_sem.at[1, slot]).wait()
        filled(slot)

        def slopes(j, _):
            cols = pl.ds(pl.multiple_of(j * 256, 256), 256)
            start = pl.ds(pl.multiple_of(TILE + j * 256, 256), 256)
            dact = dot_on(dy_v[...], w_v[slot, start], 1, 1)
            du = low(dact * wide(du_v[slot, :, cols]))
            du_v[slot, :, cols] = du
            dus_v[pl.ds(q, 1), cols] = jnp.sum(wide(du), 0, keepdims=True)
            return 0

        lax.fori_loop(0, 2, slopes, 0)
        if core:
            pl.when(i > 0)(red.give(1, turn_of(i - 1), 1).wait_send)
            stage_fill(1, du_v.at[slot], h_v)
            red.give(1, xy, 1).start()
        else:
            keep(1, xy, du_v.at[slot], h_v)

        def back(cols):
            mlp_v[:, cols] += dot_on(act_v[slot], w_v[slot, TILE:, cols], 1, 0)
            dh_v[:, cols] += dot_on(du_v[slot], w_v[slot, :TILE, cols], 1, 0)

        halves(back)

        @pl.when(i < 3)
        def _():
            go(tile_loads(2 * turn_of(i + 1) + core, slot))

    def hidden_tiles(i, _):
        hidden_tile(i, 1)
        hidden_tile(i, 0)
        return 0

    lax.fori_loop(0, 4, hidden_tiles, 0)
    go(matrix_loads(1, 0, 0))
    go(matrix_loads(0, 0, 1))
    h1_load.start()

    small_load.wait()

    small_f[...] = wide(small_v[...])
    gain1, gain2 = feature(small_f, z, 0), feature(small_f, z, 3)
    fc2_bias = feature(small_f, z, 5)
    r_load.wait()

    def collect(i, value):
        sums_v[i] = sums_v[i] + sum(value[r : r + 8] for r in range(0, value.shape[0], 8))

    def second_norm(block):
        r1 = r_v[block]
        dy = wide(dy_v[block])
        out = low((r1 + (mlp_v[block] + fc2_bias)) * mask)
        hat, inverse = norm_parts(r1)
        dh = dh_v[block]
        dr1 = dy + norm_reverse(dh, hat, gain2, inverse)
        da = low(dr1)
        r_v[block] = dr1
        da_v[block] = da
        collect(2, wide(da))
        collect(3, dh * hat)
        collect(4, dh)
        collect(5, dy)
        return out

    def by_blocks(norm):
        def body(i, _):
            block = rows_at(i * 32, 32)
            blk_v[block] = norm(block)
            return 0

        lax.fori_loop(0, done // 32, body, 0)
        out = norm(slice(done, done + 32))
        blk_v[done:seq] = out[: seq - done]

    by_blocks(second_norm)
    for ref in (r_v, da_v):
        ref[done + 32 :] = jnp.zeros((ROWS - done - 32, full), ref.dtype)
    blocks_back.start()
    x_load.start()
    ctx_load.wait()

    pending = [[red.give(0, 0, 0)], [red.give(1, 0, 1)]]

    def stage_free(slot):
        for copy in pending[slot]:
            copy.wait_send()
        pending[slot] = []

    def stage_go(slot, copies):
        go(copies)
        pending[slot] = copies

    far_half = pl.ds(TILE, TILE)
    near_half = pl.ds(0, TILE)
    stage_free(0)
    stage_fill(0, ctx_v.at[:, far_half], da_v)
    stage_go(0, [red.give(2, xy, 0) for xy in range(4)])
    filled(0)

    def dctx_half(rows):
        dctx_v[:, rows] = low(dot_on(da_v[...], w_v[0, rows], 1, 1))

    halves(dctx_half)

    def keep_heads(group, left, right):
        start = red.starts[group]
        for xy in range(4):
            red.give(group, xy, 0).wait_recv()
        def body(cols):
            grad = dot_on(left[...], right[:, cols], 0, 0)
            for xy in range(4):
                for k in range(RING):
                    rows = slice(start, start + 32)
                    at_row = k * 128 + xy * 32
                    old = wide(held[xy // 2, xy % 2, k, rows, cols])
                    held[xy // 2, xy % 2, k, rows, cols] = low(old + grad[at_row : at_row + 32])

        halves(body)

    def first_sends(c):
        red.x_copy(c, 1).start()
        red.y_copy(c, 1).start()
        red.x_copy(c, 0).start()
        red.y_copy(c, 0).start()

    keep_heads(2, ctx_v.at[:, near_half], da_v)
    first_sends(2)
    go(matrix_loads(0, 1, 0))
    qkv_load.wait()
    red.turn(0)

    key = lax.broadcasted_iota(jnp.int32, (ROWS, 1), 0)
    scale = HD ** (-0.5)

    none = jnp.bfloat16(0)

    pairs, results = act_v, du_v

    def attend_back(k):
        for c in range(3):
            split_heads(qkv_v.at[c], pairs.at[:, :, pl.ds(c * 128, 128)], k)
        split_heads(dctx_v, pairs.at[:, :, pl.ds(384, 128)], k)

        def one_pair(pair, _):
            query = pairs[pair, :, :128] * jnp.bfloat16(scale)
            keys, values = pairs[pair, :, 128:256], pairs[pair, :, 256:384]
            dctx = pairs[pair, :, 384:]
            for h in range(2):
                mask = head_mask(h)
                for r in range(ROWS // 128):
                    cols = slice(r * 128, (r + 1) * 128)
                    scores = dot_on(keys, jnp.where(mask, query[cols], none), 1, 1)
                    scores = jnp.where(key < seq, scores, -1e30)
                    expo = jnp.exp(scores - jnp.max(scores, 0, keepdims=True))
                    probs = expo * (1.0 / jnp.sum(expo, 0, keepdims=True))
                    dprobs = dot_on(values, jnp.where(mask, dctx[cols], none), 1, 1)
                    delta = jnp.sum(probs * dprobs, 0, keepdims=True)
                    p_v[:, cols] = low(probs)
                    ds_v[:, cols] = low(probs * (dprobs - delta))
                dq = dot_on(ds_v[...], keys, 0, 0) * scale
                dk = dot_on(ds_v[...], query, 1, 0)
                dv = dot_on(p_v[...], dctx, 1, 0)
                for c, value in enumerate((dq, dk, dv)):
                    at_c = slice(c * 128, (c + 1) * 128)
                    if h == 0:
                        results[pair, :, at_c] = low(value)
                    else:
                        results[pair, :, at_c] = jnp.where(mask, low(value), results[pair, :, at_c])
            return 0

        lax.fori_loop(0, 2, one_pair, 0)
        for c in range(3):
            join_heads(results.at[:, :, pl.ds(c * 128, 128)], qkv_v.at[c], k)

    def plane_grad(half, k):
        start = pl.multiple_of(half * TILE + k * 128, 128)
        left = jnp.concatenate([qkv_v[c, :, pl.ds(start, 128)] for c in range(3)], 1)
        for j in range(2):
            cols = slice(j * TILE, (j + 1) * TILE)
            grad = dot_on(left, h_v[:, cols], 0, 0)
            for c in range(3):
                for xy in range(4):
                    at_row = c * 128 + xy * 32
                    yield xy // 2, xy % 2, c * 32, cols, grad[at_row : at_row + 32]

    steps = [
        [lambda: red.turn(1)],
        [lambda: red.turn(2), lambda: red.rise(0)],
        [lambda: red.plane_turn(2), lambda: red.rise(1), lambda: red.rise(2)],
        [lambda: red.plane_rise(2), lambda: red.plane_turn(1), lambda: red.settle(0)],
    ]
    h1_load.wait()
    stage_free(0)
    stage_free(1)

    def attend_group(i, _):
        k = jnp.where(i == 0, 2, jnp.where(i == 1, 1, jnp.where(i == 2, 3, 0)))
        slot = lax.rem(i, 2)
        attend_back(k)

        @pl.when(i >= 2)
        def _():
            for y in range(2):
                red.give_plane(jnp.where(i == 2, 2, 1), slot, y).wait_send()

        for y, x, row, cols, grad in plane_grad(1, k):
            stage[slot, 2 * y + x, row : row + 32, cols] = low(grad)
        for y in range(2):
            red.give_plane(k, slot, y).start()
        for j in range(4):

            @pl.when(i == j)
            def _():
                for step in steps[j]:
                    step()

        for y in range(2):
            red.give_plane(k, slot, y).wait_recv()
        start = red.starts[3]
        for y, x, row, cols, grad in plane_grad(0, k):
            rows = slice(start + row, start + row + 32)
            held[y, x, k, rows, cols] = low(wide(held[y, x, k, rows, cols]) + grad)
        for j, plane in enumerate((2, 1, 3, 0)):
            pl.when(i == j)(red.plane_first(plane).start)
        return 0

    lax.fori_loop(0, 4, attend_group, 0)
    for i in range(3):
        if i == 2:
            go(matrix_loads(0, 2, 1))
        slot = (i + 1) % 2
        filled(slot)

        def spread_back(cols, c=i, slot=slot):
            value = dot_on(qkv_v[c], w_v[slot, :, cols], 1, 0)
            dh_v[:, cols] = value if c == 0 else value + dh_v[:, cols]

        halves(spread_back)
        if i == 0:
            red.plane_turn(3)
            red.relay(0)
        if i == 1:
            red.plane_rise(1)
    red.plane_rise(3)
    x_load.wait()
    blocks_back.sent()

    def first_norm(block):
        hat, inverse = norm_parts(wide(dy_v[block]))
        dh = dh_v[block]
        collect(0, dh * hat)
        collect(1, dh)
        return low(r_v[block] + norm_reverse(dh, hat, gain1, inverse))

    red.plane_turn(0)
    by_blocks(first_norm)
    red.plane_rise(0)
    grads_back.start()
    red.settle(1)

    for i in range(6):
        value = jnp.sum(sums_v[i], 0, keepdims=True)
        for j in range(RING):
            for side in range(2):
                start = j * quarter + side * 128
                vec[j, 2 * i + side : 2 * i + side + 1] = value[:, start : start + 128]
    for row, c in ((12, 0), (14, 2)):
        value = jnp.sum(wide(qkv_v[c]), 0, keepdims=True)
        for k in range(RING):
            starts = [half * TILE + k * 128 for half in range(2)]
            sides = [jnp.broadcast_to(value[:, i : i + 128], (8, 128)) for i in starts]
            for half, side in enumerate(turn_heads(sides, p)):
                vec[lax.rem(z + RING - k, RING), row + half : row + half + 1] = side[0:1]
    for q in range(8):
        for k in range(RING):
            at_row = pl.ds(16 + turned(p, q), 1)
            vec[lax.rem(z + RING - k, RING), at_row] = dus_v[q : q + 1, k * 128 : (k + 1) * 128]

    def vec_copy(i):
        return remote(vec, vec_far.at[i], vec_send.at[i], vec_recv.at[i], at.near((1, 2, 4)[i]))

    def vec_z(d):
        return remote(
            vec.at[at.shifts[d]],
            vec_far.at[3, d],
            vec_send.at[2 + d],
            vec_recv.at[2 + d],
            (p, at.shifts[d]),
        )

    def vec_step(i):
        vec_copy(i).wait()
        vec[...] = vec[...] + vec_far[i]

    vec_copy(0).start()
    red.settle(2)
    red.settle(3)
    vec_step(0)
    vec_copy(1).start()
    red.relay(1)
    red.last(0)
    vec_step(1)
    vec_copy(2).start()
    red.relay(2)
    red.last(1)
    red.relay(3)
    vec_step(2)
    for d in range(1, RING):
        vec_z(d).start()
    red.last(2)
    red.last(3)
    red.whole(0)
    red.whole(1)

    for piece in range(8):
        load(s1.at[piece], w_v.at[0, pl.ds(piece * 128, 128)], 8).start()
    load(w_v.at[0], w_v.at[0], 8).wait()
    for piece in range(8):
        rows = slice(piece * 128, (piece + 1) * 128)
        w_v[1, :, rows] = w_v[0, rows].T
    rows_save = load(w_v.at[1], t1, 9)
    rows_save.start()
    for d in range(1, RING):
        vec_z(d).wait()
    vec[0] = vec[z] + (vec_far[3, 1] + (vec_far[3, 2] + vec_far[3, 3]))
    vec_out = pltpu.make_async_copy(vec.at[0], vector_out, local_sem.at[4])
    vec_out.start()
    red.whole(2)
    for y in range(2):
        red.give_plane(3, 0, y).wait_send()
        red.give_plane(0, 1, y).wait_send()
    for c in range(3):
        red.finish(c)
    blocks_back.here()
    rows_save.wait()
    red.whole(3)

    def head_loads():
        for piece in range(8):
            for c in range(3):
                yield load(
                    sa.at[piece, pl.ds(c * 32, 32)], w_v.at[0, pl.ds(c * 256 + piece * 32, 32)], 10
                )

    go(head_loads())
    part = w_v.at[0, pl.ds(0, 768)]
    load(part, part, 10).wait()
    saves = []
    for c in range(3):
        rows = slice(c * 256, (c + 1) * 256)
        w_v[1, :, rows] = w_v[0, rows].T
        saves.append(load(w_v.at[1, :, pl.ds(c * 256, 256)], ta.at[c], 11 + c))
        saves[-1].start()
    for copy in saves:
        copy.wait()
    red.finish(3)
    vec_out.wait()
    grads_back.sent()
    grads_back.here()


def backward(mask, *arrays):
    images = mask.shape[0]
    seq, full = arrays[9].shape
    width = full // RING
    bf16 = jnp.bfloat16
    f32 = jnp.float32
    dma = pltpu.SemaphoreType.DMA
    attn_in, out_in, fc1_in, fc2_in = arrays[10:14]
    sizes = (fc2_in.shape[1], fc1_in.shape[1], out_in.shape[1], 3 * attn_in.shape[2])
    every = sum(sizes)
    outs = [jax.ShapeDtypeStruct((images, seq, width), bf16)] * 2
    outs.append(jax.ShapeDtypeStruct((24, 128), f32))
    outs += [jax.ShapeDtypeStruct((8, n, full), bf16) for n in sizes]
    outs.append(jax.ShapeDtypeStruct((full, 8 * sizes[1]), bf16))
    outs.append(jax.ShapeDtypeStruct((3, full, width), bf16))
    any_space = pl.BlockSpec(memory_space=pl.ANY)
    vm = pltpu.VMEM
    return pl.pallas_call(
        functools.partial(backward_kernel, images, seq, sizes),
        out_shape=outs,
        in_specs=[pl.BlockSpec(memory_space=pltpu.SMEM)] + [any_space] * len(arrays),
        out_specs=[any_space] * len(outs),
        scratch_shapes=[
            vm((2, 2, RING, every, full), bf16),
            vm((2, 2, 2, every, full), bf16),
            vm((2, 2, every, full), bf16),
            vm((3, every, full), bf16),
            vm((every, full), bf16),
            vm((2, RING, 128, full), bf16),
            vm((2, 1024, full), bf16),
            vm((ROWS, full), bf16),
            vm((ROWS, full), bf16),
            vm((2, ROWS, TILE), bf16),
            vm((2, ROWS, TILE), bf16),
            vm((ROWS, full), f32),
            vm((ROWS, full), f32),
            vm((ROWS, full), f32),
            vm((ROWS, full), bf16),
            vm((ROWS, full), bf16),
            vm((ROWS, full), bf16),
            vm((3, ROWS, full), bf16),
            vm((ROWS, ROWS), bf16),
            vm((ROWS, ROWS), bf16),
            vm((seq, full), bf16),
            vm((6, 8, full), f32),
            vm((8, TILE), f32),
            vm(arrays[0].shape, bf16),
            vm(arrays[0].shape, f32),
            vm((RING, 24, 128), f32),
            vm((4, RING, 24, 128), f32),
            dma((5, RING)),
            dma((5, RING)),
            dma((4, 20)),
            dma((4, 20)),
            dma((2, RING)),
            dma((2, RING)),
            dma((6,)),
            dma((6,)),
            dma((5,)),
            dma((RING, 2)),
            dma((RING, 2)),
            dma((14,)),
            dma((2, 2)),
            dma((2,)),
        ],
        compiler_params=pltpu.CompilerParams(
            collective_id=1, has_side_effects=True, vmem_limit_bytes=60 * 2**20
        ),
    )(mask, *arrays)


def prepare(vectors, w_attn, qv_bias, w_out, b_fc1, w_fc2):
    full, _, width = w_attn.shape
    attn = jnp.transpose(w_attn, (1, 2, 0)).reshape(3, 8, 32, full)
    qv = qv_bias.reshape(2, 4, 2, 32).transpose(0, 2, 1, 3).reshape(-1)
    start, small = 0, 0
    for v in (*vectors, qv, b_fc1):
        small = small + jnp.pad(v, (start, 4096 - start - v.shape[0]))
        start += v.shape[0]
    return small.reshape(-1, 128), attn, w_out.reshape(8, 32, full), w_fc2.reshape(8, -1, full)


def image_local(
    tokens,
    image_mask,
    ln1_gain,
    first_norm_bias,
    w_attn,
    qv_bias,
    w_out,
    b_out,
    ln2_gain,
    second_norm_bias,
    w_fc1,
    b_fc1,
    w_fc2,
    b_fc2,
    cotangent,
):
    width = tokens.shape[2]
    full = width * RING
    vectors = (ln1_gain, first_norm_bias, b_out, ln2_gain, second_norm_bias, b_fc2)
    small, attn, out, fc2 = prepare(vectors, w_attn, qv_bias, w_out, b_fc1, w_fc2)
    dy, small, *rest = forward(tokens, cotangent, small, attn, out, w_fc1, fc2)
    fulls, kept, fc1 = rest[:4], rest[4:12], rest[12]
    block_out, input_grad, sums, s2, _, so, _, t1, ta = backward(
        image_mask, small, *kept, dy, attn, out, fc1, fc2, *fulls
    )
    pairs = sums.reshape(12, width)
    grad_qv = pairs[6:8].reshape(2, 2, 4, 32).transpose(0, 2, 1, 3).reshape(2, width)
    return (
        block_out,
        input_grad,
        pairs[0],
        pairs[1],
        jnp.transpose(wide(ta), (1, 0, 2)),
        grad_qv,
        wide(so).reshape(width, full),
        pairs[2],
        pairs[3],
        pairs[4],
        wide(t1),
        pairs[8:].reshape(-1),
        wide(s2).reshape(-1, full),
        pairs[5],
    )


def solution(mesh):
    in_specs = (
        P("dp", None, "tensor"),
        P("dp"),
        P("tensor"),
        P("tensor"),
        P(None, None, "tensor"),
        P(None, "tensor"),
        P("tensor", None),
        P("tensor"),
        P("tensor"),
        P("tensor"),
        P(None, "tensor"),
        P("tensor"),
        P("tensor", None),
        P("tensor"),
        P("dp", None, "tensor"),
    )
    out_specs = (
        P("dp", None, "tensor"),
        P("dp", None, "tensor"),
        P("tensor"),
        P("tensor"),
        P(None, None, "tensor"),
        P(None, "tensor"),
        P("tensor", None),
        P("tensor"),
        P("tensor"),
        P("tensor"),
        P(None, "tensor"),
        P("tensor"),
        P("tensor", None),
        P("tensor"),
    )
    owners = mesh.shape["dp"] == 8 and mesh.shape["tensor"] == RING

    def block(*arrays):
        images = arrays[0].shape[0] // mesh.shape["dp"]
        body = image_local if owners and images < RING else local
        return jax.shard_map(
            body, mesh=mesh, in_specs=in_specs, out_specs=out_specs, check_vma=False
        )(*arrays)

    return block
```
